128 devices in a mesh: dp: 32 (over y, x, core), mp: 4 (over z).
Axes of the slice: x: 4, y: 4, z: 4, core: 2. Of those that a mesh axis runs over, the one named last changes fastest.
Arguments:
- feats: bfloat16 [16384, 768], P(('dp', 'mp')), may hold values from -6 to 6
- edge_owner: int32 [262144, 1], P(('dp', 'mp')), may hold values from 0 to 127; in each aligned block of 2048 rows (0 to 2047, 2048 to 4095, ...) at most 32 rows name the same one
- edge_row: int32 [262144], P(('dp', 'mp')), may hold values from 0 to 2047
- counts: int32 [16384], P(('dp', 'mp')), may hold values from 12 to 16
- table: float32 [262144, 128], P(('dp', 'mp')), may hold values from -6 to 6
- moment1: float32 [262144, 128], P(('dp', 'mp')), may hold values from -3 to 3
- moment2: float32 [262144, 128], P(('dp', 'mp')), may hold values from 0.001 to 0.1
- w_self: bfloat16 [768, 1024], replicated, may hold values from -0.21875 to 0.21875
- w_rel: bfloat16 [128, 1024], replicated, may hold values from -0.5 to 0.5
- cotangent: float32 [16384, 1024], P(('dp', 'mp')), may hold values from -6 to 6
- next_owner: int32 [16384, 1], P(('dp', 'mp')), may hold values from 0 to 127; in each aligned block of 128 rows (0 to 127, 128 to 255, ...) at most 2 rows name the same one
- next_row: int32 [16384], P(('dp', 'mp')), may hold values from 0 to 1023
- paper_table: bfloat16 [131072, 768], P(('dp', 'mp')), may hold values from -6 to 6
Outputs:
- new_table: float32 [262144, 128], P(('dp', 'mp'))
- new_moment1: float32 [262144, 128], P(('dp', 'mp'))
- new_moment2: float32 [262144, 128], P(('dp', 'mp'))
- grad_self: float32 [768, 1024], replicated
- grad_rel: float32 [128, 1024], replicated
- next_feats: bfloat16 [16384, 768], P(('dp', 'mp'))
The draws below stay inside these ranges and needn't reach their ends.
Inputs may be any that keep to these rules, and one draw needn't show every extreme that they name: `edge_owner`: in the author slots of one device at most 32 name one owner, a bound that some block reaches. `next_owner`: in the next seeds of one device at most 2 name one owner, a bound that some block reaches.
All inputs are finite; a program needn't handle non-finite values.
Results may differ from the reference program's by a relative error of at most 0.0049.
Values may be sent and summed in bfloat16 or wider, within the bound.
No kernel may reach another device: no remote copies, remote signals or barrier semaphores. Data moves between devices by JAX's collectives and lax.ppermute only.
A program may use at most 64 MiB of HBM per device.

```python
import math
import jax
import jax.numpy as jnp
import numpy as np
from jax import lax

F = 768
E = 128
H = 1024
K = 16
S_DEV = 128
AROWS_DEV = 2048
PROWS_DEV = 1024
SEEDS = 16384
EDGES = 262144
AROWS = 262144
PROWS = 131072
CAP = 32
FCAP = 2
DEVICES = 128


def with_ends(array, stream_key, smallest, high):
    place = [jax.random.randint(jax.random.fold_in(stream_key, axis), (), 0, length) for axis, length in enumerate(array.shape)]
    main_axis = array.shape.index(max(array.shape))
    next_to = place[:main_axis] + [(place[main_axis] + 1) % array.shape[main_axis]] + place[main_axis + 1:]
    return array.at[tuple(place)].set(smallest).at[tuple(next_to)].set(high)


def levels(rng, shape, cuts, smallest, top_value):
    gain, own = 1.0, jax.random.fold_in(rng, 6)
    for axis_at, parts in cuts:
        heights = jnp.exp(jax.random.uniform(jax.random.fold_in(own, axis_at), (parts,), jnp.float32, smallest / len(cuts), top_value / len(cuts)))
        gain = gain * jnp.repeat(heights, shape[axis_at] // parts).reshape([-1 if axis == axis_at else 1 for axis in range(len(shape))])
    return gain


def assign_block(key, own, number, rows, amount, top, reach, lean):
    sequence = jax.random.permutation(key, amount)
    crowded, ordinary = shares(amount, rows * top, reach, lean, True), shares(amount, rows * top, reach, lean, False)
    places = jnp.arange(amount)

    def named(tallies, offset_by):
        used = int((tallies > 0).sum())
        fixed = max(1, used // 4)
        moved = fixed + (places - fixed + offset_by * (used - fixed)) % max(1, amount - fixed)
        return jnp.zeros((amount,), jnp.int32).at[sequence[jnp.where(places < fixed, places, moved)]].set(jnp.asarray(tallies, jnp.int32))

    tallies = jnp.where(number % 4 == 0, named(crowded, number // 4), named(ordinary, number - number // 4 - 1))
    mixed = jax.random.permutation(jax.random.fold_in(own, 3), amount)
    source_of, sink = mixed[0:amount // 2 * 2:2], mixed[1:amount // 2 * 2:2]
    room = jnp.minimum(tallies[source_of] - 1, reach - tallies[sink]) // 2
    room = jnp.where((source_of == sequence[0]) | (sink == sequence[0]) | (tallies[sink] == 0), 0, jnp.maximum(room, 0))
    moved = jax.random.randint(jax.random.fold_in(own, 4), (amount // 2,), 0, 1 << 20) % (room + 1)
    tallies = tallies.at[source_of].add(-moved).at[sink].add(moved)
    labels = jnp.searchsorted(jnp.cumsum(tallies), jnp.arange(rows * top), side="right").astype(jnp.int32)
    table = labels.reshape(top, rows).T
    table = table[jax.random.permutation(jax.random.fold_in(own, 1), rows)]
    offset_by = jax.random.randint(jax.random.fold_in(own, 2), (rows, 1), 0, top)
    return jnp.take_along_axis(table, (jnp.arange(top)[None, :] + offset_by) % top, axis=1)


def shares(amount, total, limit, lean, full):
    portions = [(1 << 20) // math.isqrt(rank ** lean) + 1 for rank in range(1, amount + 1)]
    largest = limit if full else min(limit, max(-(-total // amount), total * portions[0] // sum(portions)))
    least = 1 if total - largest >= amount - 1 else 0
    given, surplus = [largest] + [least] * (amount - 1), total - largest - least * (amount - 1)
    while surplus > 0:
        movable = [i for i in range(1, amount) if given[i] < largest] or [i for i in range(1, amount) if given[i] < limit]
        pool, left = sum([portions[i] for i in movable]), surplus
        for i in movable:
            more = min(limit - given[i], max(1, left * portions[i] // pool), surplus)
            given[i] = given[i] + more
            surplus = surplus - more
    return np.array(given)


def normal_values(rng, extent, spread, reach, pieces=(), held_as=jnp.bfloat16):
    values = jax.random.normal(rng, extent, jnp.float32) * spread
    if len(pieces) > 0:
        values = levels(rng, extent, pieces, -0.22, 0.18) * values
    return jnp.clip(values, min=-reach, max=reach).astype(held_as)


def setup_inputs(seed: int = 0) -> dict:
    key_list = jax.random.split(jax.random.key(seed), 14)
    feats = normal_values(key_list[0], (SEEDS, F), 1.0, 6.0, ((0, 128),))
    edge_owner_keys = jax.random.split(jax.random.fold_in(key_list[1], 1), EDGES // (S_DEV * K))
    edge_owner_turns = jax.random.permutation(jax.random.fold_in(key_list[1], 3), EDGES // (S_DEV * K))
    edge_owner = jax.vmap(lambda own, number: assign_block(jax.random.fold_in(key_list[1], 2), own, number, S_DEV * K, DEVICES, 1, CAP, 2))(edge_owner_keys, edge_owner_turns).reshape((EDGES, 1))
    edge_row = with_ends(jax.random.randint(key_list[2], (EDGES,), 0, AROWS_DEV), jax.random.fold_in(key_list[2], 1), 0, AROWS_DEV - 1).astype(jnp.int32)
    counts = with_ends(jax.random.randint(key_list[3], (SEEDS,), K - K // 4, K + 1), jax.random.fold_in(key_list[3], 1), K - K // 4, K).astype(jnp.int32)
    table = normal_values(key_list[4], (AROWS, E), 1.0, 6.0, ((0, 128),), jnp.float32)
    moment1 = normal_values(key_list[5], (AROWS, E), 0.2, 3.0, ((0, 128),), jnp.float32)
    moment2 = jnp.clip(jnp.exp(math.log(0.1) - 4.6051702 * jax.random.uniform(key_list[6], (AROWS, E), jnp.float32) ** levels(key_list[6], (AROWS, E), ((0, 128),), -0.2, 0.2)), 0.001, 0.1)
    w_self = normal_values(key_list[7], (F, H), F ** -0.5, 0.21875)
    w_rel = normal_values(key_list[8], (E, H), E ** -0.5, 0.5)
    cotangent = normal_values(key_list[9], (SEEDS, H), 1.0, 6.0, ((0, 128),), jnp.float32)
    next_owner_keys = jax.random.split(jax.random.fold_in(key_list[10], 1), SEEDS // S_DEV)
    next_owner_turns = jax.random.permutation(jax.random.fold_in(key_list[10], 3), SEEDS // S_DEV)
    next_owner = jax.vmap(lambda own, number: assign_block(jax.random.fold_in(key_list[10], 2), own, number, S_DEV, DEVICES, 1, FCAP, 2))(next_owner_keys, next_owner_turns).reshape((SEEDS, 1))
    next_row = with_ends(jax.random.randint(key_list[11], (SEEDS,), 0, PROWS_DEV), jax.random.fold_in(key_list[11], 1), 0, PROWS_DEV - 1).astype(jnp.int32)
    paper_table = normal_values(key_list[12], (PROWS, F), 1.0, 6.0, ((0, 128),))
    return {"feats": feats, "edge_owner": edge_owner, "edge_row": edge_row, "counts": counts, "table": table, "moment1": moment1, "moment2": moment2, "w_self": w_self, "w_rel": w_rel, "cotangent": cotangent, "next_owner": next_owner, "next_row": next_row, "paper_table": paper_table}


def reference(feats, edge_owner, edge_row, counts, table, moment1, moment2, w_self, w_rel, cotangent, next_owner, next_row, paper_table):
    author_id = edge_owner[:, 0].astype(jnp.int32) * AROWS_DEV + edge_row
    live = jnp.arange(K, dtype=jnp.int32)[None, :] < counts[:, None]
    count_f = counts.astype(jnp.float32)
    edge_vals = jnp.take(table, author_id, axis=0).reshape(SEEDS, K, E)
    agg = lax.optimization_barrier(jnp.sum(jnp.where(live[:, :, None], edge_vals, jnp.float32(0.0)), axis=1)) / count_f[:, None]
    agg_b = agg.astype(jnp.bfloat16)
    pre = jnp.dot(feats, w_self, preferred_element_type=jnp.float32) + jnp.dot(agg_b, w_rel, preferred_element_type=jnp.float32)
    sig = jax.nn.sigmoid(pre)
    dpre = (cotangent * sig * (1.0 + pre * (1.0 - sig))).astype(jnp.bfloat16)
    grad_self = jnp.dot(feats.T, dpre, preferred_element_type=jnp.float32)
    grad_rel = jnp.dot(agg_b.T, dpre, preferred_element_type=jnp.float32)
    dagg = jnp.dot(dpre, w_rel.T, preferred_element_type=jnp.float32)
    slot_grad = jnp.where(live[:, :, None], (dagg / count_f[:, None])[:, None, :], jnp.float32(0.0)).reshape(SEEDS * K, E)
    row_grad = jax.ops.segment_sum(slot_grad, author_id, num_segments=AROWS)
    hits = jax.ops.segment_sum(live.reshape(-1).astype(jnp.int32), author_id, num_segments=AROWS)
    touched = (hits > 0)[:, None]
    m_new = 0.9 * moment1 + 0.1 * row_grad
    v_new = 0.999 * moment2 + 0.001 * row_grad * row_grad
    step = 0.05 * (m_new / (1.0 - 0.9 ** 10)) / (jnp.sqrt(v_new / (1.0 - 0.999 ** 10)) + 1e-08)
    new_table = jnp.where(touched, table - step, table)
    new_moment1 = jnp.where(touched, m_new, moment1)
    new_moment2 = jnp.where(touched, v_new, moment2)
    paper_id = next_owner[:, 0].astype(jnp.int32) * PROWS_DEV + next_row
    next_feats = jnp.take(paper_table, paper_id, axis=0)
    return (new_table, new_moment1, new_moment2, grad_self, grad_rel, next_feats)
```

```python
import functools

import jax
import jax.numpy as jnp
from jax import lax
from jax.experimental import pallas as pl
from jax.experimental.pallas import tpu as pltpu
from jax.sharding import Mesh, PartitionSpec as P

F32 = jnp.float32
BF16 = jnp.bfloat16
I32 = jnp.int32
LANES = 128
CAP = 32
FCAP = 2
GROUP = LANES // CAP
EMPTY = 4095
VMEM = pl.BlockSpec(memory_space=pltpu.VMEM)
SMEM = pl.BlockSpec(memory_space=pltpu.SMEM)


def iota(shape, dim):
    return lax.broadcasted_iota(I32, shape, dim)


def dot(a, b, contract=((1,), (0,))):
    return lax.dot_general(a, b, (contract, ((), ())), preferred_element_type=F32)


def params():
    return pltpu.CompilerParams(vmem_limit_bytes=48 * 1024 * 1024)


def onehot(mask):
    return jnp.where(mask, F32(1.0), F32(0.0)).astype(BF16)


def place_kernel(
    lane_group, owner, row, counts, next_owner, next_row, asked, seed_of, cnt, paper_pick, seed_scr
):
    devs = LANES
    blocks = owner.shape[0]
    group = lane_group[0]
    sub = iota((devs, LANES), 0)
    lane = iota((devs, LANES), 1)
    seeds_row = LANES // (LANES * blocks // devs)
    count_row = counts[...].astype(F32)
    spread = jnp.where(
        iota((blocks, LANES), 1) // seeds_row == iota((blocks, LANES), 0), count_row, F32(0.0)
    ).astype(BF16)
    slots_per = LANES // seeds_row
    pick = onehot(sub % seeds_row == lane // slots_per)
    cnt_edge = dot(spread, pick)
    k_edge = (iota((blocks, LANES), 1) % slots_per).astype(F32)
    live_owner = jnp.where(k_edge < cnt_edge, owner[...], -1)
    upper = onehot(sub < lane)
    ones = jnp.ones((devs, LANES), BF16)
    scan = jnp.concatenate([upper, ones], axis=1)
    base = jnp.zeros((devs, LANES), F32)
    acc = jnp.zeros((devs, 3 * CAP), F32)
    ksub = iota((CAP, LANES), 0).astype(F32)
    for b in range(blocks):
        hot = sub == live_owner[b : b + 1, :]
        hot_f = jnp.where(hot, F32(1.0), F32(0.0))
        hot_b = hot_f.astype(BF16)
        scanned = dot(hot_b, scan)
        slot = jnp.sum(hot_f * (scanned[:, :LANES] + base), axis=0, keepdims=True)
        base = base + scanned[:, LANES:]
        at = ksub == slot
        r = row[b : b + 1, :]
        seed1 = b * seeds_row + iota((1, LANES), 1) // slots_per + 1
        vals = jnp.concatenate(
            [
                jnp.where(at, (r // LANES).astype(F32), F32(0.0)),
                jnp.where(at, (r % LANES).astype(F32), F32(0.0)),
                jnp.where(at, seed1.astype(F32), F32(0.0)),
            ],
            axis=0,
        ).astype(BF16)
        acc = acc + dot(hot_b, vals, ((1,), (1,)))
    acc_i = acc.astype(I32)
    seeds = acc_i[:, 2 * CAP :]
    wanted = jnp.where(seeds > 0, acc_i[:, :CAP] * LANES + acc_i[:, CAP : 2 * CAP], EMPTY)

    hot = sub == next_owner[...]
    hot_f = jnp.where(hot, F32(1.0), F32(0.0))
    hot_b = hot_f.astype(BF16)
    before = dot(hot_b, upper)
    slot = jnp.sum(hot_f * before, axis=0, keepdims=True)
    nrow = next_row[...]
    vals = []
    for t in range(FCAP):
        paper_pick[t] = jnp.where(slot == t, hot_f, F32(0.0)).astype(BF16)
        at = (slot == t) & (iota((CAP, LANES), 0) == t)
        vals.append(
            (
                jnp.where(at, (nrow // LANES).astype(F32), F32(0.0)),
                jnp.where(at, (nrow % LANES).astype(F32), F32(0.0)),
            )
        )
    hi = functools.reduce(lambda a, b: a + b, [v[0] for v in vals])
    lo = functools.reduce(lambda a, b: a + b, [v[1] for v in vals])
    pacc = dot(hot_b, jnp.concatenate([hi, lo], axis=0).astype(BF16), ((1,), (1,))).astype(I32)
    paper = pacc[:, :CAP] * LANES + pacc[:, CAP:]

    quarter = lane // CAP
    wide_wanted = jnp.concatenate([wanted] * GROUP, axis=1)
    wide_paper = jnp.concatenate([paper] * GROUP, axis=1)
    asked[...] = jnp.where(
        quarter == group,
        wide_wanted,
        jnp.where(quarter == (group + 1) % GROUP, wide_paper, 0),
    )
    seed_scr[...] = jnp.where(quarter == sub % GROUP, jnp.concatenate([seeds] * GROUP, axis=1), 0)
    total = seed_scr[pl.ds(0, devs // GROUP, stride=GROUP), :]
    for i in range(1, GROUP):
        total = total + seed_scr[pl.ds(i, devs // GROUP, stride=GROUP), :]
    seed_of[...] = total
    cnt[...] = jnp.broadcast_to(count_row, (devs, LANES)).T


def place(group, owner, row, counts, next_owner, next_row):
    devs = LANES
    return pl.pallas_call(
        place_kernel,
        out_shape=(
            jax.ShapeDtypeStruct((devs, LANES), I32),
            jax.ShapeDtypeStruct((devs // GROUP, LANES), I32),
            jax.ShapeDtypeStruct((devs, LANES), F32),
            jax.ShapeDtypeStruct((FCAP, devs, LANES), BF16),
        ),
        in_specs=[SMEM, VMEM, VMEM, VMEM, VMEM, VMEM],
        out_specs=(VMEM, VMEM, VMEM, VMEM),
        scratch_shapes=[pltpu.VMEM((devs, LANES), I32)],
        compiler_params=params(),
        name="place",
    )(group, owner, row, counts, next_owner, next_row)


def gather_kernel(got, table, rows, wanted_out, hot_scr, hi_scr):
    devs = LANES
    lines = devs // GROUP
    quarter = iota((lines, LANES), 1) // CAP
    wanted = jnp.zeros((lines, LANES), I32)
    for i in range(GROUP):
        wanted = wanted + jnp.where(
            quarter == i, got[pl.ds(i, lines, stride=GROUP), :], 0
        )
    wanted_out[...] = wanted
    lo = (wanted % 256).T
    hi = (wanted // 256).T
    lane2 = iota((LANES, 256), 1)
    for b in range(lines):
        hot_scr[b * LANES : (b + 1) * LANES, :] = onehot(lo[:, b : b + 1] == lane2)
        hi_scr[b * LANES : (b + 1) * LANES, :] = jnp.broadcast_to(
            hi[:, b : b + 1], (LANES, LANES)
        )
    chunk = 512
    tiles = table.shape[0] // 512
    wide = [
        jnp.concatenate(
            [
                table[q * 512 : q * 512 + 256, :].astype(BF16),
                table[q * 512 + 256 : (q + 1) * 512, :].astype(BF16),
            ],
            axis=1,
        )
        for q in range(tiles)
    ]

    def body(c, carry):
        at = pl.ds(pl.multiple_of(c * chunk, chunk), chunk)
        hot = hot_scr[at, :]
        high = hi_scr[at, :]
        out = jnp.zeros((chunk, LANES), F32)
        for q in range(tiles):
            both = dot(hot, wide[q])
            out = jnp.where(high == 2 * q, both[:, :LANES], out)
            out = jnp.where(high == 2 * q + 1, both[:, LANES:], out)
        rows[at, :] = out.astype(BF16)
        return carry

    lax.fori_loop(0, rows.shape[0] // chunk, body, 0)


def gather(got, table):
    slots = LANES * CAP
    return pl.pallas_call(
        gather_kernel,
        out_shape=(
            jax.ShapeDtypeStruct((slots, LANES), BF16),
            jax.ShapeDtypeStruct((LANES // GROUP, LANES), I32),
        ),
        in_specs=[VMEM, VMEM],
        out_specs=(VMEM, VMEM),
        scratch_shapes=[pltpu.VMEM((slots, 256), BF16), pltpu.VMEM((slots, LANES), I32)],
        compiler_params=params(),
        name="gather_rows",
    )(got, table)


def paper_kernel(got, paper, rows):
    devs = LANES
    sub = iota((devs, LANES), 0)
    lane = iota((devs, LANES), 1)
    first = ((sub % GROUP + 1) % GROUP) * CAP
    for t in range(FCAP):
        asked = jnp.sum(jnp.where(lane == first + t, got[...], 0), axis=1, keepdims=True)
        hot = onehot(asked == iota((devs, paper.shape[0]), 1))
        rows[t] = dot(hot, paper[...]).astype(BF16)


def paper_rows(got, paper):
    return pl.pallas_call(
        paper_kernel,
        out_shape=jax.ShapeDtypeStruct((FCAP, LANES, paper.shape[1]), BF16),
        in_specs=[VMEM, VMEM],
        out_specs=VMEM,
        compiler_params=params(),
        name="gather_papers",
    )(got, paper)


def forward_kernel(
    fetched, seed_of, cnt, pre_self, w_rel, cotangent, agg_out, dpre_out, outgoing, match_scr
):
    devs = LANES
    lines = seed_of.shape[0]
    seed1 = iota((devs, LANES), 0) + 1
    agg = jnp.zeros((devs, LANES), F32)
    for b in range(lines):
        at = slice(b * LANES, (b + 1) * LANES)
        match = onehot(seed1 == seed_of[b : b + 1, :])
        agg = agg + dot(match, fetched[at, :])
    count = cnt[...]
    agg_b = (agg / count).astype(BF16)
    agg_out[...] = agg_b
    pre = pre_self[...] + dot(agg_b, w_rel[...])
    sig = jax.nn.sigmoid(pre)
    dpre = (cotangent[...] * sig * (1.0 + pre * (1.0 - sig))).astype(BF16)
    dpre_out[...] = dpre
    dagg = dot(dpre, w_rel[...], ((1,), (1,)))
    grad = (dagg / count).astype(BF16)
    seeds_t = seed_of[...].T
    lane1 = iota((devs, LANES), 1) + 1
    for b in range(lines):
        at = slice(b * LANES, (b + 1) * LANES)
        match = onehot(seeds_t[:, b : b + 1] == lane1)
        outgoing[at, :] = dot(match, grad).astype(BF16)


def forward(fetched, seed_of, cnt, pre_self, w_rel, cotangent):
    seeds, hidden = cotangent.shape
    return pl.pallas_call(
        forward_kernel,
        out_shape=(
            jax.ShapeDtypeStruct((seeds, LANES), BF16),
            jax.ShapeDtypeStruct((seeds, hidden), BF16),
            jax.ShapeDtypeStruct(fetched.shape, BF16),
        ),
        in_specs=[VMEM] * 6,
        out_specs=(VMEM, VMEM, VMEM),
        scratch_shapes=[pltpu.VMEM((8, LANES), F32)],
        compiler_params=params(),
        name="layer",
    )(fetched, seed_of, cnt, pre_self, w_rel, cotangent)


def weight_kernel(feats0, feats1, agg0, agg1, dpre0, dpre1, out):
    left = jnp.concatenate(
        [
            jnp.concatenate([feats0[...], agg0[...]], axis=1),
            jnp.concatenate([feats1[...], agg1[...]], axis=1),
        ],
        axis=0,
    )
    right = jnp.concatenate([dpre0[...], dpre1[...]], axis=0)
    rows = left.shape[1]
    part = dot(left, right, ((0,), (0,)))
    for cb in range(right.shape[1] // LANES):
        out[cb * rows : (cb + 1) * rows, :] = part[:, cb * LANES : (cb + 1) * LANES].astype(BF16)


def weight_part(feats0, feats1, agg0, agg1, dpre0, dpre1):
    rows = feats0.shape[1] + agg0.shape[1]
    cols = dpre0.shape[1]
    return pl.pallas_call(
        weight_kernel,
        out_shape=jax.ShapeDtypeStruct((rows * cols // LANES, LANES), BF16),
        in_specs=[VMEM] * 6,
        out_specs=VMEM,
        compiler_params=params(),
        name="weight_part",
    )(feats0, feats1, agg0, agg1, dpre0, dpre1)


def spread_kernel(core, mine, other, grad_self, grad_rel):
    first = core[0] == 0
    feats = grad_self.shape[0]
    rows = feats + grad_rel.shape[0]
    blocks = mine.shape[0] // rows
    for cb in range(blocks):
        own = mine[cb * rows : (cb + 1) * rows, :].astype(F32)
        far = other[cb * rows : (cb + 1) * rows, :].astype(F32)
        low = jnp.where(first, own, far)
        high = jnp.where(first, far, own)
        for block, at in ((low, cb), (high, blocks + cb)):
            cols = slice(at * LANES, (at + 1) * LANES)
            grad_self[:, cols] = block[:feats]
            grad_rel[:, cols] = block[feats:]


def spread(core, mine, other, feats, emb, hidden):
    return pl.pallas_call(
        spread_kernel,
        out_shape=(
            jax.ShapeDtypeStruct((feats, hidden), F32),
            jax.ShapeDtypeStruct((emb, hidden), F32),
        ),
        in_specs=[SMEM, VMEM, VMEM],
        out_specs=(VMEM, VMEM),
        compiler_params=params(),
        name="weight_out",
    )(core, mine, other)


def adam_kernel(wanted, arrived, table, m1, m2, new_table, new_m1, new_m2, hot_scr, side_scr):
    step = pl.program_id(0)
    lines = wanted.shape[0]

    @pl.when(step == 0)
    def _():
        lo = wanted[...] % 256
        hi = (wanted[...] // 256).astype(F32).T
        sub = iota((256, LANES), 0)
        for b in range(lines):
            at = slice(b * LANES, (b + 1) * LANES)
            hot_scr[:, at] = onehot(sub == lo[b : b + 1, :])
            side_scr[at, :] = jnp.broadcast_to(hi[:, b : b + 1], (LANES, LANES)).astype(BF16)

    here = side_scr[...] == step.astype(F32).astype(BF16)
    mark = jnp.where(here, BF16(1.0), BF16(0.0))
    right = jnp.concatenate([arrived[...] * mark, mark], axis=1)
    both = dot(hot_scr[...], right)
    grad = both[:, :LANES]
    touched = both[:, LANES:] > 0.0
    m = 0.9 * m1[...] + 0.1 * grad
    v = 0.999 * m2[...] + 0.001 * grad * grad
    update = 0.05 * (m / (1.0 - 0.9**10)) / (jnp.sqrt(v / (1.0 - 0.999**10)) + 1e-08)
    new_table[...] = jnp.where(touched, table[...] - update, table[...])
    new_m1[...] = jnp.where(touched, m, m1[...])
    new_m2[...] = jnp.where(touched, v, m2[...])


def adam(wanted, arrived, table, m1, m2):
    rows = 256
    block = pl.BlockSpec((rows, LANES), lambda i: (i, 0))
    whole = lambda a: pl.BlockSpec(a.shape, lambda i: (0, 0))
    slots = arrived.shape[0]
    return pl.pallas_call(
        adam_kernel,
        grid=(table.shape[0] // rows,),
        out_shape=(jax.ShapeDtypeStruct(table.shape, F32),) * 3,
        in_specs=[whole(wanted), whole(arrived), block, block, block],
        out_specs=(block, block, block),
        scratch_shapes=[pltpu.VMEM((rows, slots), BF16), pltpu.VMEM((slots, LANES), BF16)],
        compiler_params=params(),
        name="adam",
    )(wanted, arrived, table, m1, m2)


def shards(
    feats,
    edge_owner,
    edge_row,
    counts,
    table,
    moment1,
    moment2,
    w_self,
    w_rel,
    cotangent,
    next_owner,
    next_row,
    paper_table,
):
    every = ("chip", "core", "mp")
    peers = ("chip", "mp")
    devs = lax.axis_size(every)
    seeds, width = feats.shape
    hidden = cotangent.shape[1]
    emb = table.shape[1]
    core = lax.axis_index("core")
    group = lax.axis_index("mp").astype(I32).reshape(1)

    def exchange(a, axes):
        return lax.all_to_all(a, axes, split_axis=0, concat_axis=0, tiled=True)

    def swap(a):
        return lax.ppermute(a, "core", [(0, 1), (1, 0)])

    asked, seed_of, cnt, paper_pick = place(
        group,
        edge_owner.reshape(-1, LANES),
        edge_row.reshape(-1, LANES),
        counts.reshape(1, -1),
        next_owner.reshape(1, -1),
        next_row.reshape(1, -1),
    )
    got = exchange(asked.reshape(devs, 1, LANES), every).reshape(devs, LANES)
    rows, wanted = gather(got, table)
    fetched = exchange(rows.reshape(devs, CAP, emb), every).reshape(devs * CAP, emb)

    pre_self = jnp.dot(feats, w_self, preferred_element_type=F32)
    feats_far = swap(feats)
    papers = paper_rows(got, paper_table)
    agg_b, dpre, outgoing = forward(fetched, seed_of, cnt, pre_self, w_rel, cotangent)

    half = hidden // 2
    dpre_here = lax.dynamic_slice_in_dim(dpre, core * half, half, 1)
    dpre_there = lax.dynamic_slice_in_dim(dpre, (1 - core) * half, half, 1)
    part = weight_part(feats, feats_far, agg_b, swap(agg_b), dpre_here, swap(dpre_there))
    n_peers = lax.axis_size(peers)
    parts = exchange(part.reshape(n_peers, -1, LANES), peers)
    mine = jnp.sum(parts.astype(F32), axis=0).astype(BF16)
    arrived = exchange(outgoing.reshape(devs, CAP, emb), every).reshape(devs * CAP, emb)
    full = exchange(jnp.broadcast_to(mine[None], parts.shape), peers).reshape(-1, LANES)
    new_table, new_moment1, new_moment2 = adam(wanted, arrived, table, moment1, moment2)
    grad_self, grad_rel = spread(
        core.astype(I32).reshape(1), full, swap(full), width, emb, hidden
    )

    papers = exchange(jnp.transpose(papers, (1, 0, 2)), every)
    next_feats = functools.reduce(
        lambda a, b: a + b,
        [
            lax.dot_general(
                paper_pick[t], papers[:, t, :], (((0,), (0,)), ((), ())), preferred_element_type=F32
            )
            for t in range(FCAP)
        ],
    ).astype(BF16)
    return (new_table, new_moment1, new_moment2, grad_self, grad_rel, next_feats)


def solution(mesh):
    n_mp = mesh.shape["mp"]
    wide = Mesh(mesh.devices.reshape(-1, 2, n_mp), ("chip", "core", "mp"))
    rows = P(("chip", "core", "mp"), None)
    line = P(("chip", "core", "mp"))
    in_specs = (rows, rows, line, line, rows, rows, rows, P(), P(), rows, rows, line, rows)
    out_specs = (rows, rows, rows, P(), P(), rows)
    return jax.shard_map(shards, mesh=wide, in_specs=in_specs, out_specs=out_specs, check_vma=False)
```

```python
import functools

import jax
import jax.numpy as jnp
from jax import lax
from jax.experimental import pallas as pl
from jax.experimental.pallas import tpu as pltpu
from jax.sharding import Mesh, PartitionSpec as P

F32 = jnp.float32
BF16 = jnp.bfloat16
I32 = jnp.int32
LANES = 128
CAP = 32
FCAP = 2
GROUP = LANES // CAP
EMPTY = 4095
SELF_ROWS = 24
WEIGHT_ROWS = 32
PAPER_AT = CAP + WEIGHT_ROWS
PAPER_ROWS = 16
BUNDLE = PAPER_AT + PAPER_ROWS
VMEM = pl.BlockSpec(memory_space=pltpu.VMEM)
SMEM = pl.BlockSpec(memory_space=pltpu.SMEM)


def iota(shape, dim):
    return lax.broadcasted_iota(I32, shape, dim)


def dot(a, b, contract=((1,), (0,))):
    return lax.dot_general(a, b, (contract, ((), ())), preferred_element_type=F32)


def onehot(mask):
    return jnp.where(mask, F32(1.0), F32(0.0)).astype(BF16)

ANY = pl.BlockSpec(memory_space=pl.ANY)


def fetch(pairs, sems):
    copies = [pltpu.make_async_copy(a, b, sems.at[i]) for i, (a, b) in enumerate(pairs)]
    for c in copies:
        c.start()
    return copies


def place_kernel(
    lane_group,
    owner_in,
    row_in,
    counts_in,
    next_owner_in,
    next_row_in,
    asked,
    seed_of,
    cnt,
    paper_pick,
    owner,
    row,
    counts,
    next_owner,
    next_row,
    seed_scr,
    sems,
):
    copies = fetch(
        [
            (owner_in, owner),
            (row_in, row),
            (counts_in, counts),
            (next_owner_in, next_owner),
            (next_row_in, next_row),
        ],
        sems,
    )
    devs = LANES
    blocks = owner.shape[0]
    group = lane_group[0]
    sub = iota((devs, LANES), 0)
    lane = iota((devs, LANES), 1)
    seeds_row = LANES // (LANES * blocks // devs)
    slots_per = LANES // seeds_row
    upper = onehot(sub < lane)
    ones = jnp.ones((devs, LANES), BF16)
    scan = jnp.concatenate([upper, ones], axis=1)
    pick = onehot(sub % seeds_row == lane // slots_per)
    for c in copies:
        c.wait()
    count_row = counts[...].astype(F32)
    spread = jnp.where(
        iota((blocks, LANES), 1) // seeds_row == iota((blocks, LANES), 0), count_row, F32(0.0)
    ).astype(BF16)
    cnt_edge = dot(spread, pick)
    k_edge = (iota((blocks, LANES), 1) % slots_per).astype(F32)
    live_owner = jnp.where(k_edge < cnt_edge, owner[...], -1)
    base = jnp.zeros((devs, LANES), F32)
    acc = jnp.zeros((devs, 3 * CAP), F32)
    ksub = iota((CAP, LANES), 0).astype(F32)
    for b in range(blocks):
        hot = sub == live_owner[b : b + 1, :]
        hot_f = jnp.where(hot, F32(1.0), F32(0.0))
        hot_b = hot_f.astype(BF16)
        scanned = dot(hot_b, scan)
        slot = jnp.sum(hot_f * (scanned[:, :LANES] + base), axis=0, keepdims=True)
        base = base + scanned[:, LANES:]
        at = ksub == slot
        r = row[b : b + 1, :]
        seed1 = b * seeds_row + iota((1, LANES), 1) // slots_per + 1
        vals = jnp.concatenate(
            [
                jnp.where(at, (r // LANES).astype(F32), F32(0.0)),
                jnp.where(at, (r % LANES).astype(F32), F32(0.0)),
                jnp.where(at, seed1.astype(F32), F32(0.0)),
            ],
            axis=0,
        ).astype(BF16)
        acc = acc + dot(hot_b, vals, ((1,), (1,)))
    acc_i = acc.astype(I32)
    seeds = acc_i[:, 2 * CAP :]
    wanted = jnp.where(seeds > 0, acc_i[:, :CAP] * LANES + acc_i[:, CAP : 2 * CAP], EMPTY)

    hot = sub == next_owner[...]
    hot_f = jnp.where(hot, F32(1.0), F32(0.0))
    hot_b = hot_f.astype(BF16)
    before = dot(hot_b, upper)
    slot = jnp.sum(hot_f * before, axis=0, keepdims=True)
    nrow = next_row[...]
    for t in range(FCAP):
        paper_pick[t] = jnp.where(slot == t, hot_f, F32(0.0)).astype(BF16)
    at = iota((CAP, LANES), 0) == slot.astype(I32)
    vals = jnp.concatenate(
        [
            jnp.where(at, (nrow // LANES).astype(F32), F32(0.0)),
            jnp.where(at, (nrow % LANES).astype(F32), F32(0.0)),
        ],
        axis=0,
    ).astype(BF16)
    pacc = dot(hot_b, vals, ((1,), (1,))).astype(I32)
    paper = pacc[:, :CAP] * LANES + pacc[:, CAP:]

    quarter = lane // CAP
    wide_wanted = jnp.concatenate([wanted] * GROUP, axis=1)
    wide_paper = jnp.concatenate([paper] * GROUP, axis=1)
    asked[...] = jnp.where(
        quarter == group,
        wide_wanted,
        jnp.where(quarter == (group + 1) % GROUP, wide_paper, 0),
    )
    seed_scr[...] = jnp.where(quarter == sub % GROUP, jnp.concatenate([seeds] * GROUP, axis=1), 0)
    total = seed_scr[pl.ds(0, devs // GROUP, stride=GROUP), :]
    for i in range(1, GROUP):
        total = total + seed_scr[pl.ds(i, devs // GROUP, stride=GROUP), :]
    seed_of[...] = total
    cnt[...] = jnp.broadcast_to(count_row, (devs, LANES)).T


def place(group, owner, row, counts, next_owner, next_row):
    devs = LANES
    ins = (owner, row, counts, next_owner, next_row)
    return pl.pallas_call(
        place_kernel,
        out_shape=(
            jax.ShapeDtypeStruct((devs, LANES), I32),
            jax.ShapeDtypeStruct((devs // GROUP, LANES), I32),
            jax.ShapeDtypeStruct((devs, LANES), F32),
            jax.ShapeDtypeStruct((FCAP, devs, LANES), BF16),
        ),
        in_specs=[SMEM] + [ANY] * len(ins),
        out_specs=(VMEM, VMEM, VMEM, VMEM),
        scratch_shapes=[pltpu.VMEM(a.shape, I32) for a in ins]
        + [pltpu.VMEM((devs, LANES), I32), pltpu.SemaphoreType.DMA((len(ins),))],
        name="place",
    )(group, *ins)


def gather_kernel(got, table_in, rows, wanted_out, table, hot_scr, hi_scr, out_scr, sems, out_sems):
    devs = LANES
    lines = devs // GROUP
    part = table.shape[0] // 4
    copies = fetch(
        [
            (table_in.at[pl.ds(i * part, part), :], table.at[pl.ds(i * part, part), :])
            for i in range(4)
        ],
        sems,
    )
    quarter = iota((lines, LANES), 1) // CAP
    wanted = jnp.zeros((lines, LANES), I32)
    for i in range(GROUP):
        wanted = wanted + jnp.where(quarter == i, got[pl.ds(i, lines, stride=GROUP), :], 0)
    wanted_out[...] = wanted
    lo = (wanted % 256).T
    hi = (wanted // 256).T
    lane2 = iota((LANES, 256), 1)
    for b in range(lines):
        hot_scr[b * LANES : (b + 1) * LANES, :] = onehot(lo[:, b : b + 1] == lane2)
        hi_scr[b * LANES : (b + 1) * LANES, :] = jnp.broadcast_to(hi[:, b : b + 1], (LANES, LANES))
    for c in copies:
        c.wait()
    chunk = 512
    tiles = table.shape[0] // 512
    wide = [
        jnp.concatenate(
            [
                table[q * 512 : q * 512 + 256, :].astype(BF16),
                table[q * 512 + 256 : (q + 1) * 512, :].astype(BF16),
            ],
            axis=1,
        )
        for q in range(tiles)
    ]
    outs = []
    for c in range(out_scr.shape[0] // chunk):
        at = pl.ds(c * chunk, chunk)
        hot = hot_scr[at, :]
        high = hi_scr[at, :]
        out = jnp.zeros((chunk, LANES), F32)
        for q in range(tiles):
            both = dot(hot, wide[q])
            out = jnp.where(high == 2 * q, both[:, :LANES], out)
            out = jnp.where(high == 2 * q + 1, both[:, LANES:], out)
        out_scr[at, :] = out.astype(BF16)
        copy = pltpu.make_async_copy(out_scr.at[at, :], rows.at[at, :], out_sems.at[c])
        copy.start()
        outs.append(copy)
    for copy in outs:
        copy.wait()


def gather(got, table):
    slots = LANES * CAP
    return pl.pallas_call(
        gather_kernel,
        out_shape=(
            jax.ShapeDtypeStruct((slots, LANES), BF16),
            jax.ShapeDtypeStruct((LANES // GROUP, LANES), I32),
        ),
        in_specs=[VMEM, ANY],
        out_specs=(ANY, VMEM),
        scratch_shapes=[
            pltpu.VMEM(table.shape, F32),
            pltpu.VMEM((slots, 256), BF16),
            pltpu.VMEM((slots, LANES), I32),
            pltpu.VMEM((slots, LANES), BF16),
            pltpu.SemaphoreType.DMA((4,)),
            pltpu.SemaphoreType.DMA((slots // 512,)),
        ],
        name="gather_rows",
    )(got, table)


def paper_kernel(got, paper, rows):
    devs = LANES
    sub = iota((devs, LANES), 0)
    lane = iota((devs, LANES), 1)
    first = ((sub % GROUP + 1) % GROUP) * CAP
    width = paper.shape[1]
    for t in range(FCAP):
        asked = jnp.sum(jnp.where(lane == first + t, got[...], 0), axis=1, keepdims=True)
        hot = onehot(asked == iota((devs, paper.shape[0]), 1))
        rows[:, t * width : (t + 1) * width] = dot(hot, paper[...]).astype(BF16)


def paper_rows(got, paper):
    return pl.pallas_call(
        paper_kernel,
        out_shape=jax.ShapeDtypeStruct((LANES, FCAP * paper.shape[1]), BF16),
        in_specs=[VMEM, VMEM],
        out_specs=VMEM,
        cost_estimate=pl.CostEstimate(
            flops=2 * FCAP * LANES * paper.shape[0] * paper.shape[1],
            bytes_accessed=4 * paper.size,
            transcendentals=0,
        ),
        name="gather_papers",
    )(got, paper)


def layer_kernel(
    fetched, seed_of, cnt, pre_in, w_in, cot_in, agg_out, dpre_out, grad_out, pre_self, w_rel, cot, sems
):
    copies = fetch([(w_in, w_rel), (pre_in, pre_self), (cot_in, cot)], sems)
    devs = LANES
    lines = seed_of.shape[0]
    seed1 = iota((devs, LANES), 0) + 1
    agg = jnp.zeros((devs, LANES), F32)
    for b in range(0, lines, 2):
        match = jnp.concatenate(
            [onehot(seed1 == seed_of[b : b + 1, :]), onehot(seed1 == seed_of[b + 1 : b + 2, :])],
            axis=1,
        )
        agg = agg + dot(match, fetched[b * LANES : (b + 2) * LANES, :])
    count = cnt[...]
    agg_b = (agg / count).astype(BF16)
    agg_out[...] = agg_b
    for c in copies:
        c.wait()
    pre = pre_self[...] + dot(agg_b, w_rel[...])
    sig = jax.nn.sigmoid(pre)
    dpre = (cot[...] * sig * (1.0 + pre * (1.0 - sig))).astype(BF16)
    dpre_out[...] = dpre
    dagg = dot(dpre, w_rel[...], ((1,), (1,)))
    grad_out[...] = (dagg / count).astype(BF16)


def layer(fetched, seed_of, cnt, pre_self, w_rel, cotangent):
    seeds, hidden = cotangent.shape
    return pl.pallas_call(
        layer_kernel,
        out_shape=(
            jax.ShapeDtypeStruct((seeds, LANES), BF16),
            jax.ShapeDtypeStruct((seeds, hidden), BF16),
            jax.ShapeDtypeStruct((seeds, LANES), BF16),
        ),
        in_specs=[VMEM, VMEM, VMEM, ANY, ANY, ANY],
        out_specs=(VMEM, VMEM, VMEM),
        scratch_shapes=[
            pltpu.VMEM(pre_self.shape, F32),
            pltpu.VMEM(w_rel.shape, BF16),
            pltpu.VMEM(cotangent.shape, F32),
            pltpu.SemaphoreType.DMA((3,)),
        ],
        name="layer",
    )(fetched, seed_of, cnt, pre_self, w_rel, cotangent)


def slots_kernel(seed_of, grad, papers, bundle, out_scr, sems):
    paper_copy = pltpu.make_async_copy(
        papers, bundle.at[:, pl.ds(PAPER_AT, PAPER_ROWS), :], sems.at[0]
    )
    paper_copy.start()
    lines = seed_of.shape[0]
    seeds_t = seed_of[...].T
    lane1 = iota((LANES, LANES), 1) + 1
    copies = []
    per = 8
    for b in range(lines):
        match = onehot(seeds_t[:, b : b + 1] == lane1)
        out_scr[b * GROUP : (b + 1) * GROUP] = (
            dot(match, grad[...]).astype(BF16).reshape(GROUP, CAP, LANES)
        )
        if b % per == per - 1:
            at = pl.ds((b - per + 1) * GROUP, per * GROUP)
            copy = pltpu.make_async_copy(
                out_scr.at[at], bundle.at[at, pl.ds(0, CAP), :], sems.at[1 + b // per]
            )
            copy.start()
            copies.append(copy)
    for c in copies:
        c.wait()
    paper_copy.wait()


def slot_grads(seed_of, grad, papers):
    return pl.pallas_call(
        slots_kernel,
        out_shape=jax.ShapeDtypeStruct((LANES, BUNDLE, LANES), BF16),
        in_specs=[VMEM, VMEM, ANY],
        out_specs=ANY,
        scratch_shapes=[
            pltpu.VMEM((LANES, CAP, LANES), BF16),
            pltpu.SemaphoreType.DMA((5,)),
        ],
        cost_estimate=pl.CostEstimate(
            flops=2 * LANES * CAP * LANES * LANES, bytes_accessed=4 << 20, transcendentals=0
        ),
        name="slot_grads",
    )(seed_of, grad, papers)


def weight_kernel(feats_t, agg0, agg1, dpre0, dpre1, bundle_in, bundle, out_scr, sems):
    del bundle_in
    right = jnp.concatenate([dpre0[...], dpre1[...]], axis=0)
    aggs = jnp.concatenate([agg0[...], agg1[...]], axis=0)
    emb = aggs.shape[1]
    blocks = LANES // (right.shape[1] // LANES)
    per = emb // blocks
    where = iota((2 * emb, emb), 0)
    twice = onehot((where // (2 * per)) * per + where % per == iota((2 * emb, emb), 1))
    aggs_t = dot(twice, aggs, ((1,), (1,))).astype(BF16)
    copies = []
    rows_f = feats_t.shape[0] // blocks
    for cb in range(right.shape[1] // LANES):
        cols = right[:, cb * LANES : (cb + 1) * LANES]
        part_f = dot(feats_t[...], cols).astype(BF16)
        part_a = dot(aggs_t, cols)
        rest = part_a - part_a.astype(BF16).astype(F32)
        part_a = jnp.where(iota(part_a.shape, 0) % (2 * per) < per, part_a, rest).astype(BF16)
        for i in range(blocks):
            out_scr[cb * blocks + i] = jnp.concatenate(
                [
                    part_f[i * rows_f : (i + 1) * rows_f],
                    part_a[i * 2 * per : (i + 1) * 2 * per],
                ],
                axis=0,
            )
        at = pl.ds(cb * blocks, blocks)
        copy = pltpu.make_async_copy(
            out_scr.at[at], bundle.at[at, pl.ds(CAP, WEIGHT_ROWS), :], sems.at[cb]
        )
        copy.start()
        copies.append(copy)
    for c in copies:
        c.wait()


def weight_part(feats_t, agg0, agg1, dpre0, dpre1, bundle):
    return pl.pallas_call(
        weight_kernel,
        out_shape=jax.ShapeDtypeStruct(bundle.shape, BF16),
        in_specs=[VMEM] * 5 + [ANY],
        out_specs=ANY,
        scratch_shapes=[
            pltpu.VMEM((LANES, WEIGHT_ROWS, LANES), BF16),
            pltpu.SemaphoreType.DMA((dpre0.shape[1] // LANES,)),
        ],
        input_output_aliases={5: 0},
        name="weight_part",
    )(feats_t, agg0, agg1, dpre0, dpre1, bundle)


def sum_kernel(bundle, out, parts, out_scr, sems):
    step = LANES // 4
    copies = fetch(
        [
            (
                bundle.at[pl.ds(i * step, step), pl.ds(CAP, WEIGHT_ROWS), :],
                parts.at[pl.ds(i * step, step)],
            )
            for i in range(4)
        ],
        sems,
    )
    half = [jnp.zeros((WEIGHT_ROWS, LANES), F32) for _ in range(2)]
    for i in range(4):
        copies[i].wait()
        for d in range(i * step, (i + 1) * step):
            c = (d // GROUP) % 2
            half[c] = half[c] + parts[d].astype(F32)
    per = (WEIGHT_ROWS - SELF_ROWS) // 2
    rel = [h[SELF_ROWS : SELF_ROWS + per] + h[SELF_ROWS + per :] for h in half]
    mine = jnp.concatenate([half[0][:SELF_ROWS], half[1][:SELF_ROWS], rel[0], rel[1]], axis=0)
    mine = mine.astype(BF16)
    for i in range(out_scr.shape[0]):
        out_scr[i] = mine
    q = out_scr.shape[0] // 4
    copies = fetch(
        [(out_scr.at[pl.ds(i * q, q)], out.at[pl.ds(i * q, q)]) for i in range(4)], sems
    )
    for c in copies:
        c.wait()


def sum_parts(bundle, peers):
    rows = WEIGHT_ROWS + SELF_ROWS
    return pl.pallas_call(
        sum_kernel,
        out_shape=jax.ShapeDtypeStruct((peers, rows, LANES), BF16),
        in_specs=[ANY],
        out_specs=ANY,
        scratch_shapes=[
            pltpu.VMEM((LANES, WEIGHT_ROWS, LANES), BF16),
            pltpu.VMEM((peers, rows, LANES), BF16),
            pltpu.SemaphoreType.DMA((4,)),
        ],
        name="sum_parts",
    )(bundle)


def spread_kernel(core, mine, other, grad_self, grad_rel):
    first = core[0] == 0
    half = pl.program_id(1)
    per = grad_rel.shape[0] // 32
    chips = mine.shape[0] // GROUP
    rel = []
    for chip in range(chips):
        for c in range(2):
            for mp in range(GROUP):
                src = chip * GROUP + mp
                own = mine[src].astype(F32)
                far = other[src].astype(F32)
                got = jnp.where(first, own, far) if c == 0 else jnp.where(first, far, own)
                i = (chip * 2 + c) * GROUP + mp
                grad_self[i * SELF_ROWS : (i + 1) * SELF_ROWS, :] = jnp.where(
                    half == 0, got[:SELF_ROWS], got[SELF_ROWS : 2 * SELF_ROWS]
                )
                at = 2 * SELF_ROWS
                rel.append(jnp.where(half == 0, got[at : at + per], got[at + per : at + 2 * per]))
    grad_rel[...] = jnp.concatenate(rel, axis=0)


def spread(core, mine, other, feats, emb, hidden):
    blocks = hidden // LANES // 2
    peers, rows, _ = mine.shape
    block = pl.BlockSpec((peers // blocks, rows, LANES), lambda c, h: (c, 0, 0))
    return pl.pallas_call(
        spread_kernel,
        grid=(blocks, 2),
        out_shape=(
            jax.ShapeDtypeStruct((feats, hidden), F32),
            jax.ShapeDtypeStruct((emb, hidden), F32),
        ),
        in_specs=[SMEM, block, block],
        out_specs=(
            pl.BlockSpec((feats, LANES), lambda c, h: (0, h * blocks + c)),
            pl.BlockSpec((emb, LANES), lambda c, h: (0, h * blocks + c)),
        ),
        name="weight_out",
    )(core, mine, other)


def adam_kernel(
    wanted, bundle, table, m1, m2, new_table, new_m1, new_m2, arrived, hot_scr, side_scr, sem
):
    step = pl.program_id(0)
    lines = wanted.shape[0]

    @pl.when(step == 0)
    def _():
        copy = pltpu.make_async_copy(bundle.at[:, pl.ds(0, CAP), :], arrived, sem.at[0])
        copy.start()
        lo = wanted[...] % 256
        hi = (wanted[...] // 256).astype(F32).T
        sub = iota((256, LANES), 0)
        for b in range(lines):
            at = slice(b * LANES, (b + 1) * LANES)
            hot_scr[:, at] = onehot(sub == lo[b : b + 1, :])
            side_scr[at, :] = jnp.broadcast_to(hi[:, b : b + 1], (LANES, LANES)).astype(BF16)
        copy.wait()

    here = side_scr[...] == step.astype(F32).astype(BF16)
    mark = jnp.where(here, BF16(1.0), BF16(0.0))
    got = arrived[...].reshape(LANES * CAP, LANES)
    both = dot(hot_scr[...], jnp.concatenate([got * mark, mark], axis=1))
    grad = both[:, :LANES]
    touched = both[:, LANES:] > 0.0
    m = 0.9 * m1[...] + 0.1 * grad
    v = 0.999 * m2[...] + 0.001 * grad * grad
    update = 0.05 * (m / (1.0 - 0.9**10)) / (jnp.sqrt(v / (1.0 - 0.999**10)) + 1e-08)
    new_table[...] = jnp.where(touched, table[...] - update, table[...])
    new_m1[...] = jnp.where(touched, m, m1[...])
    new_m2[...] = jnp.where(touched, v, m2[...])


def adam(wanted, bundle, table, m1, m2):
    rows = 256
    block = pl.BlockSpec((rows, LANES), lambda i: (i, 0))
    slots = LANES * CAP
    return pl.pallas_call(
        adam_kernel,
        grid=(table.shape[0] // rows,),
        out_shape=(jax.ShapeDtypeStruct(table.shape, F32),) * 3,
        in_specs=[pl.BlockSpec(wanted.shape, lambda i: (0, 0)), ANY, block, block, block],
        out_specs=(block, block, block),
        scratch_shapes=[
            pltpu.VMEM((LANES, CAP, LANES), BF16),
            pltpu.VMEM((rows, slots), BF16),
            pltpu.VMEM((slots, LANES), BF16),
            pltpu.SemaphoreType.DMA((1,)),
        ],
        cost_estimate=pl.CostEstimate(
            flops=2 * 2 * slots * LANES * table.shape[0],
            bytes_accessed=7 << 20,
            transcendentals=0,
        ),
        name="adam",
    )(wanted, bundle, table, m1, m2)


def shards(
    feats,
    edge_owner,
    edge_row,
    counts,
    table,
    moment1,
    moment2,
    w_self,
    w_rel,
    cotangent,
    next_owner,
    next_row,
    paper_table,
):
    every = ("chip", "core", "mp")
    peers = ("chip", "mp")
    devs = lax.axis_size(every)
    seeds, width = feats.shape
    hidden = cotangent.shape[1]
    emb = table.shape[1]
    core = lax.axis_index("core")
    group = lax.axis_index("mp").astype(I32).reshape(1)

    def exchange(a, axes):
        return lax.all_to_all(a, axes, split_axis=0, concat_axis=0, tiled=True)

    def swap(a):
        return lax.ppermute(a, "core", [(0, 1), (1, 0)])

    asked, seed_of, cnt, paper_pick = place(
        group,
        edge_owner.reshape(-1, LANES),
        edge_row.reshape(-1, LANES),
        counts.reshape(1, -1),
        next_owner.reshape(1, -1),
        next_row.reshape(1, -1),
    )
    got = exchange(asked.reshape(devs, 1, LANES), every).reshape(devs, LANES)
    rows, wanted = gather(got, table)
    fetched = exchange(rows.reshape(devs, CAP, emb), every).reshape(devs * CAP, emb)

    pre_self = jnp.dot(feats, w_self, preferred_element_type=F32)
    feats_t = jnp.concatenate([feats, swap(feats)], axis=0).T
    papers = paper_rows(got, paper_table).reshape(devs, -1, LANES)
    papers = jnp.pad(papers, ((0, 0), (0, PAPER_ROWS - papers.shape[1]), (0, 0)))
    agg_b, dpre, grad = layer(fetched, seed_of, cnt, pre_self, w_rel, cotangent)

    half = hidden // 2
    dpre_here = lax.dynamic_slice_in_dim(dpre, core * half, half, 1)
    dpre_there = lax.dynamic_slice_in_dim(dpre, (1 - core) * half, half, 1)
    agg_far, dpre_far = swap(agg_b), swap(dpre_there)
    bundle = slot_grads(seed_of, grad, papers)
    bundle = weight_part(feats_t, agg_b, agg_far, dpre_here, dpre_far, bundle)
    bundle = exchange(bundle, every)
    full = exchange(sum_parts(bundle, lax.axis_size(peers)), peers)
    new_table, new_moment1, new_moment2 = adam(wanted, bundle, table, moment1, moment2)
    grad_self, grad_rel = spread(
        core.astype(I32).reshape(1), full, swap(full), width, emb, hidden
    )

    papers = bundle[:, PAPER_AT : PAPER_AT + FCAP * width // LANES, :].reshape(devs, -1)
    next_feats = functools.reduce(
        lambda a, b: a + b,
        [
            lax.dot_general(
                paper_pick[t],
                papers[:, t * width : (t + 1) * width],
                (((0,), (0,)), ((), ())),
                preferred_element_type=F32,
            )
            for t in range(FCAP)
        ],
    ).astype(BF16)
    return (new_table, new_moment1, new_moment2, grad_self, grad_rel, next_feats)


def solution(mesh):
    n_mp = mesh.shape["mp"]
    wide = Mesh(mesh.devices.reshape(-1, 2, n_mp), ("chip", "core", "mp"))
    rows = P(("chip", "core", "mp"), None)
    line = P(("chip", "core", "mp"))
    in_specs = (rows, rows, line, line, rows, rows, rows, P(), P(), rows, rows, line, rows)
    out_specs = (rows, rows, rows, P(), P(), rows)
    return jax.shard_map(shards, mesh=wide, in_specs=in_specs, out_specs=out_specs, check_vma=False)
```

```python
import functools

import jax
import jax.numpy as jnp
from jax import lax
from jax.experimental import pallas as pl
from jax.experimental.pallas import tpu as pltpu
from jax.sharding import Mesh, PartitionSpec as P

F32 = jnp.float32
BF16 = jnp.bfloat16
I32 = jnp.int32
LANES = 128
CAP = 32
FCAP = 2
GROUP = LANES // CAP
EMPTY = 4095
SELF_ROWS = 24
WEIGHT_ROWS = 32
PAPER_AT = CAP + WEIGHT_ROWS
PAPER_ROWS = 16
BUNDLE = PAPER_AT + PAPER_ROWS
VMEM = pl.BlockSpec(memory_space=pltpu.VMEM)
SMEM = pl.BlockSpec(memory_space=pltpu.SMEM)


def iota(shape, dim):
    return lax.broadcasted_iota(I32, shape, dim)


def dot(a, b, contract=((1,), (0,))):
    return lax.dot_general(a, b, (contract, ((), ())), preferred_element_type=F32)


def onehot(mask):
    return jnp.where(mask, F32(1.0), F32(0.0)).astype(BF16)

ANY = pl.BlockSpec(memory_space=pl.ANY)
HBM = pl.BlockSpec(memory_space=pltpu.HBM)


def params():
    return pltpu.CompilerParams(vmem_limit_bytes=24 * 1024 * 1024)


def fetch(pairs, sems):
    copies = [pltpu.make_async_copy(a, b, sems.at[i]) for i, (a, b) in enumerate(pairs)]
    for c in copies:
        c.start()
    return copies


def place_kernel(
    lane_group,
    owner_in,
    row_in,
    counts_in,
    next_owner_in,
    next_row_in,
    asked,
    seed_of,
    cnt,
    paper_pick,
    owner,
    row,
    counts,
    next_owner,
    next_row,
    seed_scr,
    sems,
):
    copies = fetch(
        [
            (owner_in, owner),
            (row_in, row),
            (counts_in, counts),
            (next_owner_in, next_owner),
            (next_row_in, next_row),
        ],
        sems,
    )
    devs = LANES
    blocks = owner.shape[0]
    group = lane_group[0]
    sub = iota((devs, LANES), 0)
    lane = iota((devs, LANES), 1)
    seeds_row = LANES // (LANES * blocks // devs)
    slots_per = LANES // seeds_row
    upper = onehot(sub < lane)
    ones = jnp.ones((devs, LANES), BF16)
    scan = jnp.concatenate([upper, ones], axis=1)
    pick = onehot(sub % seeds_row == lane // slots_per)
    for c in copies:
        c.wait()
    count_row = counts[...].astype(F32)
    spread = jnp.where(
        iota((blocks, LANES), 1) // seeds_row == iota((blocks, LANES), 0), count_row, F32(0.0)
    ).astype(BF16)
    cnt_edge = dot(spread, pick)
    k_edge = (iota((blocks, LANES), 1) % slots_per).astype(F32)
    live_owner = jnp.where(k_edge < cnt_edge, owner[...], -1)
    base = jnp.zeros((devs, LANES), F32)
    acc = jnp.zeros((devs, 3 * CAP), F32)
    ksub = iota((CAP, LANES), 0).astype(F32)
    for b in range(blocks):
        hot = sub == live_owner[b : b + 1, :]
        hot_f = jnp.where(hot, F32(1.0), F32(0.0))
        hot_b = hot_f.astype(BF16)
        scanned = dot(hot_b, scan)
        slot = jnp.sum(hot_f * (scanned[:, :LANES] + base), axis=0, keepdims=True)
        base = base + scanned[:, LANES:]
        at = ksub == slot
        r = row[b : b + 1, :]
        seed1 = b * seeds_row + iota((1, LANES), 1) // slots_per + 1
        vals = jnp.concatenate(
            [
                jnp.where(at, (r // LANES).astype(F32), F32(0.0)),
                jnp.where(at, (r % LANES).astype(F32), F32(0.0)),
                jnp.where(at, seed1.astype(F32), F32(0.0)),
            ],
            axis=0,
        ).astype(BF16)
        acc = acc + dot(hot_b, vals, ((1,), (1,)))
    acc_i = acc.astype(I32)
    seeds = acc_i[:, 2 * CAP :]
    wanted = jnp.where(seeds > 0, acc_i[:, :CAP] * LANES + acc_i[:, CAP : 2 * CAP], EMPTY)

    hot = sub == next_owner[...]
    hot_f = jnp.where(hot, F32(1.0), F32(0.0))
    hot_b = hot_f.astype(BF16)
    before = dot(hot_b, upper)
    slot = jnp.sum(hot_f * before, axis=0, keepdims=True)
    nrow = next_row[...]
    for t in range(FCAP):
        paper_pick[t] = jnp.where(slot == t, hot_f, F32(0.0)).astype(BF16)
    at = iota((CAP, LANES), 0) == slot.astype(I32)
    vals = jnp.concatenate(
        [
            jnp.where(at, (nrow // LANES).astype(F32), F32(0.0)),
            jnp.where(at, (nrow % LANES).astype(F32), F32(0.0)),
        ],
        axis=0,
    ).astype(BF16)
    pacc = dot(hot_b, vals, ((1,), (1,))).astype(I32)
    paper = pacc[:, :CAP] * LANES + pacc[:, CAP:]

    quarter = lane // CAP
    wide_wanted = jnp.concatenate([wanted] * GROUP, axis=1)
    wide_paper = jnp.concatenate([paper] * GROUP, axis=1)
    asked[...] = jnp.where(
        quarter == group,
        wide_wanted,
        jnp.where(quarter == (group + 1) % GROUP, wide_paper, 0),
    )
    seed_scr[...] = jnp.where(quarter == sub % GROUP, jnp.concatenate([seeds] * GROUP, axis=1), 0)
    total = seed_scr[pl.ds(0, devs // GROUP, stride=GROUP), :]
    for i in range(1, GROUP):
        total = total + seed_scr[pl.ds(i, devs // GROUP, stride=GROUP), :]
    seed_of[...] = total
    cnt[...] = jnp.broadcast_to(count_row, (devs, LANES)).T


def place(group, owner, row, counts, next_owner, next_row):
    devs = LANES
    ins = (owner, row, counts, next_owner, next_row)
    return pl.pallas_call(
        place_kernel,
        out_shape=(
            jax.ShapeDtypeStruct((devs, LANES), I32),
            jax.ShapeDtypeStruct((devs // GROUP, LANES), I32),
            jax.ShapeDtypeStruct((devs, LANES), F32),
            jax.ShapeDtypeStruct((FCAP, devs, LANES), BF16),
        ),
        in_specs=[SMEM] + [HBM] * len(ins),
        out_specs=(VMEM, VMEM, VMEM, VMEM),
        scratch_shapes=[pltpu.VMEM(a.shape, I32) for a in ins]
        + [pltpu.VMEM((devs, LANES), I32), pltpu.SemaphoreType.DMA((len(ins),))],
        name="place",
    )(group, *ins)


def gather_kernel(got, table_in, rows, wanted_out, table, hot_scr, hi_scr, out_scr, sems, out_sems):
    devs = LANES
    lines = devs // GROUP
    part = table.shape[0] // 4
    copies = fetch(
        [
            (table_in.at[pl.ds(i * part, part), :], table.at[pl.ds(i * part, part), :])
            for i in range(4)
        ],
        sems,
    )
    quarter = iota((lines, LANES), 1) // CAP
    wanted = jnp.zeros((lines, LANES), I32)
    for i in range(GROUP):
        wanted = wanted + jnp.where(quarter == i, got[pl.ds(i, lines, stride=GROUP), :], 0)
    wanted_out[...] = wanted
    lo = (wanted % 256).T
    hi = (wanted // 256).T
    lane2 = iota((LANES, 256), 1)
    for b in range(lines):
        hot_scr[b * LANES : (b + 1) * LANES, :] = onehot(lo[:, b : b + 1] == lane2)
        hi_scr[b * LANES : (b + 1) * LANES, :] = jnp.broadcast_to(hi[:, b : b + 1], (LANES, LANES))
    for c in copies:
        c.wait()
    chunk = 512
    tiles = table.shape[0] // 512
    wide = [
        jnp.concatenate(
            [
                table[q * 512 : q * 512 + 256, :].astype(BF16),
                table[q * 512 + 256 : (q + 1) * 512, :].astype(BF16),
            ],
            axis=1,
        )
        for q in range(tiles)
    ]
    outs = []
    for c in range(out_scr.shape[0] // chunk):
        at = pl.ds(c * chunk, chunk)
        hot = hot_scr[at, :]
        high = hi_scr[at, :]
        out = jnp.zeros((chunk, LANES), F32)
        for q in range(tiles):
            both = dot(hot, wide[q])
            out = jnp.where(high == 2 * q, both[:, :LANES], out)
            out = jnp.where(high == 2 * q + 1, both[:, LANES:], out)
        out_scr[at, :] = out.astype(BF16)
        copy = pltpu.make_async_copy(out_scr.at[at, :], rows.at[at, :], out_sems.at[c])
        copy.start()
        outs.append(copy)
    for copy in outs:
        copy.wait()


def gather(got, table):
    slots = LANES * CAP
    return pl.pallas_call(
        gather_kernel,
        out_shape=(
            jax.ShapeDtypeStruct((slots, LANES), BF16),
            jax.ShapeDtypeStruct((LANES // GROUP, LANES), I32),
        ),
        in_specs=[VMEM, HBM],
        out_specs=(HBM, VMEM),
        scratch_shapes=[
            pltpu.VMEM(table.shape, F32),
            pltpu.VMEM((slots, 256), BF16),
            pltpu.VMEM((slots, LANES), I32),
            pltpu.VMEM((slots, LANES), BF16),
            pltpu.SemaphoreType.DMA((4,)),
            pltpu.SemaphoreType.DMA((slots // 512,)),
        ],
        name="gather_rows",
    )(got, table)


def paper_kernel(got, paper_in, rows, paper, sems):
    copies = fetch([(paper_in, paper)], sems)
    devs = LANES
    sub = iota((devs, LANES), 0)
    lane = iota((devs, LANES), 1)
    first = ((sub % GROUP + 1) % GROUP) * CAP
    width = paper.shape[1]
    copies[0].wait()
    for t in range(FCAP):
        asked = jnp.sum(jnp.where(lane == first + t, got[...], 0), axis=1, keepdims=True)
        hot = onehot(asked == iota((devs, paper.shape[0]), 1))
        rows[:, t * width : (t + 1) * width] = dot(hot, paper[...]).astype(BF16)


def paper_rows(got, paper):
    return pl.pallas_call(
        paper_kernel,
        out_shape=jax.ShapeDtypeStruct((LANES, FCAP * paper.shape[1]), BF16),
        in_specs=[VMEM, HBM],
        out_specs=VMEM,
        scratch_shapes=[pltpu.VMEM(paper.shape, BF16), pltpu.SemaphoreType.DMA((1,))],
        cost_estimate=pl.CostEstimate(
            flops=2 * FCAP * LANES * paper.shape[0] * paper.shape[1],
            bytes_accessed=4 * paper.size,
            transcendentals=0,
        ),
        name="gather_papers",
    )(got, paper)


def prep_kernel(feats, w_self, cot_in, w_in, pre, cot, w_rel, sems):
    copies = fetch([(cot_in, cot), (w_in, w_rel)], sems)
    pre[...] = dot(feats[...], w_self[...])
    for c in copies:
        c.wait()


def prep(feats, w_self, cotangent, w_rel):
    return pl.pallas_call(
        prep_kernel,
        out_shape=(
            jax.ShapeDtypeStruct(cotangent.shape, F32),
            jax.ShapeDtypeStruct(cotangent.shape, F32),
            jax.ShapeDtypeStruct(w_rel.shape, BF16),
        ),
        in_specs=[VMEM, VMEM, ANY, ANY],
        out_specs=(VMEM, VMEM, VMEM),
        scratch_shapes=[pltpu.SemaphoreType.DMA((2,))],
        compiler_params=params(),
        cost_estimate=pl.CostEstimate(
            flops=2 * feats.size * w_self.shape[1], bytes_accessed=4 << 20, transcendentals=0
        ),
        name="prep",
    )(feats, w_self, cotangent, w_rel)


def layer_kernel(
    core,
    fetched,
    seed_of,
    cnt,
    pre_self,
    w_rel,
    cot,
    *rest,
):
    agg_out, here_out, there_out, grad_out = rest[-4:]
    devs = LANES
    lines = seed_of.shape[0]
    seed1 = iota((devs, LANES), 0) + 1
    agg = jnp.zeros((devs, LANES), F32)
    for b in range(0, lines, 2):
        match = jnp.concatenate(
            [onehot(seed1 == seed_of[b : b + 1, :]), onehot(seed1 == seed_of[b + 1 : b + 2, :])],
            axis=1,
        )
        agg = agg + dot(match, fetched[b * LANES : (b + 2) * LANES, :])
    count = cnt[...]
    agg_b = (agg / count).astype(BF16)
    agg_out[...] = agg_b
    pre = pre_self[...] + dot(agg_b, w_rel[...])
    sig = jax.nn.sigmoid(pre)
    dpre = (cot[...] * sig * (1.0 + pre * (1.0 - sig))).astype(BF16)
    half = dpre.shape[1] // 2
    first = core[0] == 0
    here_out[...] = jnp.where(first, dpre[:, :half], dpre[:, half:])
    there_out[...] = jnp.where(first, dpre[:, half:], dpre[:, :half])
    dagg = dot(dpre, w_rel[...], ((1,), (1,)))
    grad_out[...] = (dagg / count).astype(BF16)


def layer(core, fetched, seed_of, cnt, pre_self, w_rel, cotangent, *ready):
    seeds, hidden = cotangent.shape
    return pl.pallas_call(
        layer_kernel,
        out_shape=(
            jax.ShapeDtypeStruct((seeds, LANES), BF16),
            jax.ShapeDtypeStruct((seeds, hidden // 2), BF16),
            jax.ShapeDtypeStruct((seeds, hidden // 2), BF16),
            jax.ShapeDtypeStruct((seeds, LANES), BF16),
        ),
        in_specs=[SMEM] + [VMEM] * 6 + [ANY] * len(ready),
        out_specs=(VMEM, VMEM, VMEM, VMEM),
        compiler_params=params(),
        name="layer",
    )(core, fetched, seed_of, cnt, pre_self, w_rel, cotangent, *ready)


def slots_kernel(seed_of, grad, papers, bundle, out_scr, sems):
    paper_copy = pltpu.make_async_copy(
        papers, bundle.at[:, pl.ds(PAPER_AT, PAPER_ROWS), :], sems.at[0]
    )
    paper_copy.start()
    lines = seed_of.shape[0]
    seeds_t = seed_of[...].T
    lane1 = iota((LANES, LANES), 1) + 1
    copies = []
    per = 8
    for b in range(lines):
        match = onehot(seeds_t[:, b : b + 1] == lane1)
        out_scr[b * GROUP : (b + 1) * GROUP] = (
            dot(match, grad[...]).astype(BF16).reshape(GROUP, CAP, LANES)
        )
        if b % per == per - 1:
            at = pl.ds((b - per + 1) * GROUP, per * GROUP)
            copy = pltpu.make_async_copy(
                out_scr.at[at], bundle.at[at, pl.ds(0, CAP), :], sems.at[1 + b // per]
            )
            copy.start()
            copies.append(copy)
    for c in copies:
        c.wait()
    paper_copy.wait()


def slot_grads(seed_of, grad, papers):
    return pl.pallas_call(
        slots_kernel,
        out_shape=jax.ShapeDtypeStruct((LANES, BUNDLE, LANES), BF16),
        in_specs=[VMEM, VMEM, VMEM],
        out_specs=HBM,
        scratch_shapes=[
            pltpu.VMEM((LANES, CAP, LANES), BF16),
            pltpu.SemaphoreType.DMA((5,)),
        ],
        cost_estimate=pl.CostEstimate(
            flops=2 * LANES * CAP * LANES * LANES, bytes_accessed=4 << 20, transcendentals=0
        ),
        compiler_params=params(),
        name="slot_grads",
    )(seed_of, grad, papers)


def weight_kernel(feats_t, agg0, agg1, dpre0, dpre1, bundle_in, bundle, out_scr, sems):
    del bundle_in
    right = jnp.concatenate([dpre0[...], dpre1[...]], axis=0)
    aggs = jnp.concatenate([agg0[...], agg1[...]], axis=0)
    emb = aggs.shape[1]
    blocks = LANES // (right.shape[1] // LANES)
    per = emb // blocks
    where = iota((2 * emb, emb), 0)
    twice = onehot((where // (2 * per)) * per + where % per == iota((2 * emb, emb), 1))
    aggs_t = dot(twice, aggs, ((1,), (1,))).astype(BF16)
    copies = []
    rows_f = feats_t.shape[0] // blocks
    for cb in range(right.shape[1] // LANES):
        cols = right[:, cb * LANES : (cb + 1) * LANES]
        part_f = dot(feats_t[...], cols).astype(BF16)
        part_a = dot(aggs_t, cols)
        rest = part_a - part_a.astype(BF16).astype(F32)
        part_a = jnp.where(iota(part_a.shape, 0) % (2 * per) < per, part_a, rest).astype(BF16)
        for i in range(blocks):
            out_scr[cb * blocks + i] = jnp.concatenate(
                [
                    part_f[i * rows_f : (i + 1) * rows_f],
                    part_a[i * 2 * per : (i + 1) * 2 * per],
                ],
                axis=0,
            )
        at = pl.ds(cb * blocks, blocks)
        copy = pltpu.make_async_copy(
            out_scr.at[at], bundle.at[at, pl.ds(CAP, WEIGHT_ROWS), :], sems.at[cb]
        )
        copy.start()
        copies.append(copy)
    for c in copies:
        c.wait()


def weight_part(feats_t, agg0, agg1, dpre0, dpre1, bundle):
    return pl.pallas_call(
        weight_kernel,
        out_shape=jax.ShapeDtypeStruct(bundle.shape, BF16),
        in_specs=[VMEM] * 5 + [HBM],
        out_specs=HBM,
        scratch_shapes=[
            pltpu.VMEM((LANES, WEIGHT_ROWS, LANES), BF16),
            pltpu.SemaphoreType.DMA((dpre0.shape[1] // LANES,)),
        ],
        input_output_aliases={5: 0},
        compiler_params=params(),
        name="weight_part",
    )(feats_t, agg0, agg1, dpre0, dpre1, bundle)


def sum_kernel(bundle, out, parts, out_scr, sems):
    step = LANES // 4
    copies = fetch(
        [
            (
                bundle.at[pl.ds(i * step, step), pl.ds(CAP, WEIGHT_ROWS), :],
                parts.at[pl.ds(i * step, step)],
            )
            for i in range(4)
        ],
        sems,
    )
    half = [jnp.zeros((WEIGHT_ROWS, LANES), F32) for _ in range(2)]
    for i in range(4):
        copies[i].wait()
        for d in range(i * step, (i + 1) * step):
            c = (d // GROUP) % 2
            half[c] = half[c] + parts[d].astype(F32)
    per = (WEIGHT_ROWS - SELF_ROWS) // 2
    rel = [h[SELF_ROWS : SELF_ROWS + per] + h[SELF_ROWS + per :] for h in half]
    mine = jnp.concatenate([half[0][:SELF_ROWS], half[1][:SELF_ROWS], rel[0], rel[1]], axis=0)
    mine = mine.astype(BF16)
    for i in range(out_scr.shape[0]):
        out_scr[i] = mine
    q = out_scr.shape[0] // 4
    copies = fetch(
        [(out_scr.at[pl.ds(i * q, q)], out.at[pl.ds(i * q, q)]) for i in range(4)], sems
    )
    for c in copies:
        c.wait()


def sum_parts(bundle, peers):
    rows = WEIGHT_ROWS + SELF_ROWS
    return pl.pallas_call(
        sum_kernel,
        out_shape=jax.ShapeDtypeStruct((peers, rows, LANES), BF16),
        in_specs=[ANY],
        out_specs=HBM,
        scratch_shapes=[
            pltpu.VMEM((LANES, WEIGHT_ROWS, LANES), BF16),
            pltpu.VMEM((peers, rows, LANES), BF16),
            pltpu.SemaphoreType.DMA((4,)),
        ],
        compiler_params=params(),
        name="sum_parts",
    )(bundle)


def spread_kernel(core, mine, other, grad_self, grad_rel):
    first = core[0] == 0
    columns = mine.shape[0]
    per = grad_rel.shape[0] // (2 * GROUP)
    for cb in range(columns):
        rel = [[], []]
        for c in range(2):
            for mp in range(GROUP):
                own = mine[cb, 0, mp].astype(F32)
                far = other[cb, 0, mp].astype(F32)
                got = jnp.where(first, own, far) if c == 0 else jnp.where(first, far, own)
                i = c * GROUP + mp
                for h in range(2):
                    cols = slice((h * columns + cb) * LANES, (h * columns + cb + 1) * LANES)
                    grad_self[i * SELF_ROWS : (i + 1) * SELF_ROWS, cols] = got[
                        h * SELF_ROWS : (h + 1) * SELF_ROWS
                    ]
                    at = 2 * SELF_ROWS + h * per
                    rel[h].append(got[at : at + per])
        for h in range(2):
            cols = slice((h * columns + cb) * LANES, (h * columns + cb + 1) * LANES)
            grad_rel[:, cols] = jnp.concatenate(rel[h], axis=0)


def spread(core, mine, other, feats, emb, hidden):
    columns = hidden // LANES // 2
    peers, rows, _ = mine.shape
    steps = peers // columns // GROUP
    shape = (columns, steps, GROUP, rows, LANES)
    block = pl.BlockSpec((columns, 1, GROUP, rows, LANES), lambda i: (0, i, 0, 0, 0))
    return pl.pallas_call(
        spread_kernel,
        grid=(steps,),
        out_shape=(
            jax.ShapeDtypeStruct((feats, hidden), F32),
            jax.ShapeDtypeStruct((emb, hidden), F32),
        ),
        in_specs=[SMEM, block, block],
        out_specs=(
            pl.BlockSpec((feats // steps, hidden), lambda i: (i, 0)),
            pl.BlockSpec((emb // steps, hidden), lambda i: (i, 0)),
        ),
        name="weight_out",
    )(core, mine.reshape(shape), other.reshape(shape))


def after_kernel(*refs):
    pass


def after(a, *ready):
    return pl.pallas_call(
        after_kernel,
        out_shape=jax.ShapeDtypeStruct(a.shape, a.dtype),
        in_specs=[ANY] * (1 + len(ready)),
        out_specs=ANY,
        input_output_aliases={0: 0},
        name="after",
    )(a, *ready)


def adam_kernel(
    wanted, bundle, table, m1, m2, new_table, new_m1, new_m2, done, arrived, hot_scr, side_scr, sem
):
    step = pl.program_id(0)
    lines = wanted.shape[0]
    done[...] = jnp.zeros_like(done)

    @pl.when(step == 0)
    def _():
        copy = pltpu.make_async_copy(bundle.at[:, pl.ds(0, CAP), :], arrived, sem.at[0])
        copy.start()
        lo = wanted[...] % 256
        hi = (wanted[...] // 256).astype(F32).T
        sub = iota((256, LANES), 0)
        for b in range(lines):
            at = slice(b * LANES, (b + 1) * LANES)
            hot_scr[:, at] = onehot(sub == lo[b : b + 1, :])
            side_scr[at, :] = jnp.broadcast_to(hi[:, b : b + 1], (LANES, LANES)).astype(BF16)
        copy.wait()

    here = side_scr[...] == step.astype(F32).astype(BF16)
    mark = jnp.where(here, BF16(1.0), BF16(0.0))
    got = arrived[...].reshape(LANES * CAP, LANES)
    both = dot(hot_scr[...], jnp.concatenate([got * mark, mark], axis=1))
    grad = both[:, :LANES]
    touched = both[:, LANES:] > 0.0
    m = 0.9 * m1[...] + 0.1 * grad
    v = 0.999 * m2[...] + 0.001 * grad * grad
    update = 0.05 * (m / (1.0 - 0.9**10)) / (jnp.sqrt(v / (1.0 - 0.999**10)) + 1e-08)
    new_table[...] = jnp.where(touched, table[...] - update, table[...])
    new_m1[...] = jnp.where(touched, m, m1[...])
    new_m2[...] = jnp.where(touched, v, m2[...])


def adam(wanted, bundle, table, m1, m2):
    rows = 256
    block = pl.BlockSpec((rows, LANES), lambda i: (i, 0))
    slots = LANES * CAP
    return pl.pallas_call(
        adam_kernel,
        grid=(table.shape[0] // rows,),
        out_shape=(jax.ShapeDtypeStruct(table.shape, F32),) * 3
        + (jax.ShapeDtypeStruct((8, LANES), F32),),
        in_specs=[pl.BlockSpec(wanted.shape, lambda i: (0, 0)), ANY, block, block, block],
        out_specs=(block, block, block, pl.BlockSpec((8, LANES), lambda i: (0, 0))),
        scratch_shapes=[
            pltpu.VMEM((LANES, CAP, LANES), BF16),
            pltpu.VMEM((rows, slots), BF16),
            pltpu.VMEM((slots, LANES), BF16),
            pltpu.SemaphoreType.DMA((1,)),
        ],
        cost_estimate=pl.CostEstimate(
            flops=2 * 2 * slots * LANES * table.shape[0],
            bytes_accessed=7 << 20,
            transcendentals=0,
        ),
        name="adam",
    )(wanted, bundle, table, m1, m2)


def shards(
    feats,
    edge_owner,
    edge_row,
    counts,
    table,
    moment1,
    moment2,
    w_self,
    w_rel,
    cotangent,
    next_owner,
    next_row,
    paper_table,
):
    every = ("chip", "core", "mp")
    peers = ("chip", "mp")
    devs = lax.axis_size(every)
    seeds, width = feats.shape
    hidden = cotangent.shape[1]
    emb = table.shape[1]
    core = lax.axis_index("core").astype(I32).reshape(1)
    group = lax.axis_index("mp").astype(I32).reshape(1)

    def exchange(a, axes):
        return lax.all_to_all(a, axes, split_axis=0, concat_axis=0, tiled=True)

    def swap(a):
        return lax.ppermute(a, "core", [(0, 1), (1, 0)])

    asked, seed_of, cnt, paper_pick = place(
        group,
        edge_owner.reshape(-1, LANES),
        edge_row.reshape(-1, LANES),
        counts.reshape(1, -1),
        next_owner.reshape(1, -1),
        next_row.reshape(1, -1),
    )
    got = exchange(asked.reshape(devs, 1, LANES), every).reshape(devs, LANES)
    rows, wanted = gather(got, table)
    fetched = exchange(rows.reshape(devs, CAP, emb), every).reshape(devs * CAP, emb)

    pre_self, cot, w_rel = prep(feats, w_self, cotangent, w_rel)
    feats_t = jnp.concatenate([feats, swap(feats)], axis=0).T
    papers = paper_rows(got, paper_table).reshape(devs, -1, LANES)
    papers = jnp.pad(papers, ((0, 0), (0, PAPER_ROWS - papers.shape[1]), (0, 0)))
    agg_b, dpre_here, dpre_there, grad = layer(
        core, fetched, seed_of, cnt, pre_self, w_rel, cot, feats_t, papers
    )

    agg_far, dpre_far = swap(agg_b), swap(dpre_there)
    bundle = slot_grads(seed_of, grad, papers)
    bundle = weight_part(feats_t, agg_b, agg_far, dpre_here, dpre_far, bundle)
    bundle = exchange(bundle, every)
    full = exchange(sum_parts(bundle, lax.axis_size(peers)), peers)
    new_table, new_moment1, new_moment2, done = adam(wanted, bundle, table, moment1, moment2)
    papers = bundle[:, PAPER_AT : PAPER_AT + FCAP * width // LANES, :].reshape(devs, -1)
    next_feats = functools.reduce(
        lambda a, b: a + b,
        [
            lax.dot_general(
                paper_pick[t],
                papers[:, t * width : (t + 1) * width],
                (((0,), (0,)), ((), ())),
                preferred_element_type=F32,
            )
            for t in range(FCAP)
        ],
    ).astype(BF16)
    full = after(full, done, next_feats)
    grad_self, grad_rel = spread(core, full, swap(full), width, emb, hidden)
    return (new_table, new_moment1, new_moment2, grad_self, grad_rel, next_feats)


def solution(mesh):
    n_mp = mesh.shape["mp"]
    wide = Mesh(mesh.devices.reshape(-1, 2, n_mp), ("chip", "core", "mp"))
    rows = P(("chip", "core", "mp"), None)
    line = P(("chip", "core", "mp"))
    in_specs = (rows, rows, line, line, rows, rows, rows, P(), P(), rows, rows, line, rows)
    out_specs = (rows, rows, rows, P(), P(), rows)
    return jax.shard_map(shards, mesh=wide, in_specs=in_specs, out_specs=out_specs, check_vma=False)
```

```python
import functools

import jax
import jax.numpy as jnp
from jax import lax
from jax.experimental import pallas as pl
from jax.experimental.pallas import tpu as pltpu
from jax.sharding import Mesh, PartitionSpec as P

F32 = jnp.float32
BF16 = jnp.bfloat16
I32 = jnp.int32
LANES = 128
CAP = 32
FCAP = 2
GROUP = LANES // CAP
EMPTY = 4095
SELF_ROWS = 24
REL_ROWS = 4
REL_AT = CAP + SELF_ROWS
PAPER_AT = REL_AT + REL_ROWS
PAPER_ROWS = 12
TILE = 256
BUNDLE = PAPER_AT + PAPER_ROWS
VMEM = pl.BlockSpec(memory_space=pltpu.VMEM)
SMEM = pl.BlockSpec(memory_space=pltpu.SMEM)


def iota(shape, dim):
    return lax.broadcasted_iota(I32, shape, dim)


def dot(a, b, contract=((1,), (0,))):
    return lax.dot_general(a, b, (contract, ((), ())), preferred_element_type=F32)


def onehot(mask):
    return jnp.where(mask, F32(1.0), F32(0.0)).astype(BF16)

ANY = pl.BlockSpec(memory_space=pl.ANY)
HBM = pl.BlockSpec(memory_space=pltpu.HBM)


def params():
    return pltpu.CompilerParams(vmem_limit_bytes=24 * 1024 * 1024)


def in_hbm(*arrays):
    return [pltpu.with_memory_space_constraint(a, pltpu.HBM) for a in arrays]


def fetch(pairs, sems):
    copies = [pltpu.make_async_copy(a, b, sems.at[i]) for i, (a, b) in enumerate(pairs)]
    for c in copies:
        c.start()
    return copies


def place_kernel(
    lane_group,
    owner_in,
    row_in,
    counts_in,
    next_owner_in,
    next_row_in,
    table_in,
    asked,
    seed_of,
    cnt,
    paper_pick,
    wide,
    owner,
    row,
    counts,
    next_owner,
    next_row,
    table,
    seed_scr,
    sems,
):
    copies = fetch(
        [
            (owner_in, owner),
            (row_in, row),
            (counts_in, counts),
            (next_owner_in, next_owner),
            (next_row_in, next_row),
            (table_in, table),
        ],
        sems,
    )
    table_copy = copies.pop()
    devs = LANES
    blocks = owner.shape[0]
    group = lane_group[0]
    sub = iota((devs, LANES), 0)
    lane = iota((devs, LANES), 1)
    seeds_row = LANES // (LANES * blocks // devs)
    slots_per = LANES // seeds_row
    upper = onehot(sub < lane)
    ones = jnp.ones((devs, LANES), BF16)
    scan = jnp.concatenate([upper, ones], axis=1)
    pick = onehot(sub % seeds_row == lane // slots_per)
    for c in copies:
        c.wait()
    count_row = counts[...].astype(F32)
    spread = jnp.where(
        iota((blocks, LANES), 1) // seeds_row == iota((blocks, LANES), 0), count_row, F32(0.0)
    ).astype(BF16)
    cnt_edge = dot(spread, pick)
    k_edge = (iota((blocks, LANES), 1) % slots_per).astype(F32)
    live_owner = jnp.where(k_edge < cnt_edge, owner[...], -1)
    base = jnp.zeros((devs, LANES), F32)
    acc = jnp.zeros((devs, 3 * CAP), F32)
    ksub = iota((CAP, LANES), 0).astype(F32)
    for b in range(blocks):
        hot = sub == live_owner[b : b + 1, :]
        hot_f = jnp.where(hot, F32(1.0), F32(0.0))
        hot_b = hot_f.astype(BF16)
        scanned = dot(hot_b, scan)
        slot = jnp.sum(hot_f * (scanned[:, :LANES] + base), axis=0, keepdims=True)
        base = base + scanned[:, LANES:]
        at = ksub == slot
        r = row[b : b + 1, :]
        seed1 = b * seeds_row + iota((1, LANES), 1) // slots_per + 1
        vals = jnp.concatenate(
            [
                jnp.where(at, (r // LANES).astype(F32), F32(0.0)),
                jnp.where(at, (r % LANES).astype(F32), F32(0.0)),
                jnp.where(at, seed1.astype(F32), F32(0.0)),
            ],
            axis=0,
        ).astype(BF16)
        acc = acc + dot(hot_b, vals, ((1,), (1,)))
    acc_i = acc.astype(I32)
    seeds = acc_i[:, 2 * CAP :]
    wanted = jnp.where(seeds > 0, acc_i[:, :CAP] * LANES + acc_i[:, CAP : 2 * CAP], EMPTY)

    hot = sub == next_owner[...]
    hot_f = jnp.where(hot, F32(1.0), F32(0.0))
    hot_b = hot_f.astype(BF16)
    before = dot(hot_b, upper)
    slot = jnp.sum(hot_f * before, axis=0, keepdims=True)
    nrow = next_row[...]
    for t in range(FCAP):
        paper_pick[t] = jnp.where(slot == t, hot_f, F32(0.0)).astype(BF16)
    at = iota((CAP, LANES), 0) == slot.astype(I32)
    vals = jnp.concatenate(
        [
            jnp.where(at, (nrow // LANES).astype(F32), F32(0.0)),
            jnp.where(at, (nrow % LANES).astype(F32), F32(0.0)),
        ],
        axis=0,
    ).astype(BF16)
    pacc = dot(hot_b, vals, ((1,), (1,))).astype(I32)
    paper = pacc[:, :CAP] * LANES + pacc[:, CAP:]

    quarter = lane // CAP
    wide_wanted = jnp.concatenate([wanted] * GROUP, axis=1)
    wide_paper = jnp.concatenate([paper] * GROUP, axis=1)
    asked[...] = jnp.where(
        quarter == group,
        wide_wanted,
        jnp.where(quarter == (group + 1) % GROUP, wide_paper, 0),
    )
    seed_scr[...] = jnp.where(quarter == sub % GROUP, jnp.concatenate([seeds] * GROUP, axis=1), 0)
    total = seed_scr[pl.ds(0, devs // GROUP, stride=GROUP), :]
    for i in range(1, GROUP):
        total = total + seed_scr[pl.ds(i, devs // GROUP, stride=GROUP), :]
    seed_of[...] = total
    cnt[...] = jnp.broadcast_to(count_row, (devs, LANES)).T
    table_copy.wait()
    for q in range(table.shape[0] // TILE):
        wide[:, q * LANES : (q + 1) * LANES] = table[q * TILE : (q + 1) * TILE, :].astype(BF16)


def place(group, owner, row, counts, next_owner, next_row, table):
    devs = LANES
    ins = (owner, row, counts, next_owner, next_row, table)
    return pl.pallas_call(
        place_kernel,
        out_shape=(
            pltpu.HBM((devs, LANES), I32),
            jax.ShapeDtypeStruct((devs // GROUP, LANES), I32),
            jax.ShapeDtypeStruct((devs, LANES), F32),
            jax.ShapeDtypeStruct((FCAP, devs, LANES), BF16),
            pltpu.VMEM((TILE, table.shape[0] // TILE * LANES), BF16),
        ),
        in_specs=[SMEM] + [HBM] * len(ins),
        out_specs=(VMEM, VMEM, VMEM, VMEM, VMEM),
        scratch_shapes=[pltpu.VMEM(a.shape, a.dtype) for a in ins]
        + [pltpu.VMEM((devs, LANES), I32), pltpu.SemaphoreType.DMA((len(ins),))],
        compiler_params=params(),
        name="place",
    )(group, *in_hbm(*ins))


def gather_kernel(got, wide, rows, wanted_out, hot_scr, hi_scr, out_scr, out_sems):
    devs = LANES
    lines = devs // GROUP
    quarter = iota((lines, LANES), 1) // CAP
    wanted = jnp.zeros((lines, LANES), I32)
    for i in range(GROUP):
        wanted = wanted + jnp.where(quarter == i, got[pl.ds(i, lines, stride=GROUP), :], 0)
    wanted_out[...] = wanted
    lo = (wanted % TILE).T
    hi = (wanted // TILE).T
    lanes = iota((LANES, TILE), 1)
    for b in range(lines):
        hot_scr[b * LANES : (b + 1) * LANES, :] = onehot(lo[:, b : b + 1] == lanes)
        hi_scr[b * LANES : (b + 1) * LANES, :] = jnp.broadcast_to(hi[:, b : b + 1], (LANES, LANES))
    chunk = 512
    outs = []
    for c in range(out_scr.shape[0] // chunk):
        at = pl.ds(c * chunk, chunk)
        hot = hot_scr[at, :]
        high = hi_scr[at, :]
        out = jnp.zeros((chunk, LANES), F32)
        for q in range(0, wide.shape[1] // LANES, 2):
            both = dot(hot, wide[:, q * LANES : (q + 2) * LANES])
            out = jnp.where(high == q, both[:, :LANES], out)
            out = jnp.where(high == q + 1, both[:, LANES:], out)
        out_scr[at, :] = out.astype(BF16)
        copy = pltpu.make_async_copy(out_scr.at[at, :], rows.at[at, :], out_sems.at[c])
        copy.start()
        outs.append(copy)
    for copy in outs:
        copy.wait()


def gather(got, wide):
    slots = LANES * CAP
    return pl.pallas_call(
        gather_kernel,
        out_shape=(
            pltpu.HBM((slots, LANES), BF16),
            pltpu.HBM((LANES // GROUP, LANES), I32),
        ),
        in_specs=[VMEM, VMEM],
        out_specs=(HBM, VMEM),
        scratch_shapes=[
            pltpu.VMEM((slots, TILE), BF16),
            pltpu.VMEM((slots, LANES), I32),
            pltpu.VMEM((slots, LANES), BF16),
            pltpu.SemaphoreType.DMA((slots // 512,)),
        ],
        compiler_params=params(),
        name="gather_rows",
    )(got, wide)


def paper_kernel(got, paper, rows, scr):
    devs = LANES
    sub = iota((devs, LANES), 0)
    lane = iota((devs, LANES), 1)
    first = ((sub % GROUP + 1) % GROUP) * CAP
    parts = paper.shape[1] // LANES
    span = REL_ROWS + PAPER_ROWS
    for i in range(REL_ROWS):
        scr[pl.ds(i, devs, stride=span), :] = jnp.zeros((devs, LANES), F32)
    for t in range(FCAP):
        asked = jnp.sum(jnp.where(lane == first + t, got[...], 0), axis=1, keepdims=True)
        hot = onehot(asked == iota((devs, paper.shape[0]), 1))
        found = dot(hot, paper[...])
        for i in range(parts):
            scr[pl.ds(REL_ROWS + t * parts + i, devs, stride=span), :] = found[
                :, i * LANES : (i + 1) * LANES
            ]
    rows[...] = scr[...].astype(BF16).reshape(rows.shape)


def paper_rows(got, paper):
    span = REL_ROWS + PAPER_ROWS
    return pl.pallas_call(
        paper_kernel,
        out_shape=pltpu.HBM((LANES, span, LANES), BF16),
        in_specs=[VMEM, VMEM],
        out_specs=VMEM,
        scratch_shapes=[pltpu.VMEM((LANES * span, LANES), F32)],
        compiler_params=params(),
        cost_estimate=pl.CostEstimate(
            flops=2 * FCAP * LANES * paper.shape[0] * paper.shape[1],
            bytes_accessed=4 * paper.size,
            transcendentals=0,
        ),
        name="gather_papers",
    )(got, paper)


def prep_kernel(feats, w_self, pre):
    pre[...] = dot(feats[...], w_self[...])


def prep(feats, w_self):
    return pl.pallas_call(
        prep_kernel,
        out_shape=pltpu.HBM((feats.shape[0], w_self.shape[1]), F32),
        in_specs=[VMEM, VMEM],
        out_specs=VMEM,
        compiler_params=params(),
        cost_estimate=pl.CostEstimate(
            flops=2 * feats.size * w_self.shape[1], bytes_accessed=4 << 20, transcendentals=0
        ),
        name="prep",
    )(feats, w_self)


def turn_kernel(feats, far, out):
    seeds = feats.shape[0]
    out[:, :seeds] = feats[...].T
    out[:, seeds:] = far[...].T


def turn(feats, far):
    seeds, width = feats.shape
    return pl.pallas_call(
        turn_kernel,
        out_shape=pltpu.HBM((width, 2 * seeds), BF16),
        in_specs=[VMEM, VMEM],
        out_specs=VMEM,
        compiler_params=params(),
        cost_estimate=pl.CostEstimate(flops=0, bytes_accessed=8 * feats.size, transcendentals=0),
        name="turn",
    )(feats, far)


def layer_kernel(
    core,
    fetched,
    seed_of,
    cnt,
    pre_in,
    w_in,
    cot_in,
    *rest,
):
    agg_out, here_out, there_out, grad_out, pre_self, w_rel, cot, sems = rest[-8:]
    copies = fetch([(w_in, w_rel), (pre_in, pre_self), (cot_in, cot)], sems)
    devs = LANES
    lines = seed_of.shape[0]
    seed1 = iota((devs, LANES), 0) + 1
    agg = jnp.zeros((devs, LANES), F32)
    for b in range(0, lines, 2):
        match = jnp.concatenate(
            [onehot(seed1 == seed_of[b : b + 1, :]), onehot(seed1 == seed_of[b + 1 : b + 2, :])],
            axis=1,
        )
        agg = agg + dot(match, fetched[b * LANES : (b + 2) * LANES, :])
    count = cnt[...]
    agg_b = (agg / count).astype(BF16)
    agg_out[...] = agg_b
    for c in copies:
        c.wait()
    pre = pre_self[...] + dot(agg_b, w_rel[...])
    sig = jax.nn.sigmoid(pre)
    dpre = (cot[...] * sig * (1.0 + pre * (1.0 - sig))).astype(BF16)
    half = dpre.shape[1] // 2
    first = core[0] == 0
    here_out[...] = jnp.where(first, dpre[:, :half], dpre[:, half:])
    there_out[...] = jnp.where(first, dpre[:, half:], dpre[:, :half])
    dagg = dot(dpre, w_rel[...], ((1,), (1,)))
    grad_out[...] = (dagg / count).astype(BF16)


def layer(core, fetched, seed_of, cnt, pre_self, w_rel, cotangent, *ready):
    seeds, hidden = cotangent.shape
    return pl.pallas_call(
        layer_kernel,
        out_shape=(
            jax.ShapeDtypeStruct((seeds, LANES), BF16),
            jax.ShapeDtypeStruct((seeds, hidden // 2), BF16),
            jax.ShapeDtypeStruct((seeds, hidden // 2), BF16),
            jax.ShapeDtypeStruct((seeds, LANES), BF16),
        ),
        in_specs=[SMEM] + [VMEM] * 3 + [HBM] * 3 + [ANY] * len(ready),
        out_specs=(VMEM, VMEM, VMEM, VMEM),
        scratch_shapes=[
            pltpu.VMEM(pre_self.shape, F32),
            pltpu.VMEM(w_rel.shape, BF16),
            pltpu.VMEM(cotangent.shape, F32),
            pltpu.SemaphoreType.DMA((3,)),
        ],
        compiler_params=params(),
        name="layer",
    )(core, fetched, seed_of, cnt, *in_hbm(pre_self, w_rel, cotangent, *ready))


def slots_kernel(seed_of, grad, papers_in, feats_in, out, papers, feats, sems):
    copies = fetch([(papers_in, papers), (feats_in, feats)], sems)
    seeds_t = seed_of[...].T
    lane1 = iota((LANES, LANES), 1) + 1
    for b in range(seed_of.shape[0]):
        match = onehot(seeds_t[:, b : b + 1] == lane1)
        out[b * GROUP : (b + 1) * GROUP] = (
            dot(match, grad[...]).astype(BF16).reshape(GROUP, CAP, LANES)
        )
    for c in copies:
        c.wait()


def slot_grads(seed_of, grad, papers, feats_t):
    return pl.pallas_call(
        slots_kernel,
        out_shape=(
            pltpu.VMEM((LANES, CAP, LANES), BF16),
            pltpu.VMEM(papers.shape, BF16),
            pltpu.VMEM(feats_t.shape, BF16),
        ),
        in_specs=[VMEM, VMEM, HBM, HBM],
        out_specs=(VMEM, VMEM, VMEM),
        scratch_shapes=[pltpu.SemaphoreType.DMA((2,))],
        compiler_params=params(),
        cost_estimate=pl.CostEstimate(
            flops=2 * LANES * CAP * LANES * LANES, bytes_accessed=4 << 20, transcendentals=0
        ),
        name="slot_grads",
    )(seed_of, grad, *in_hbm(papers, feats_t))


def weight_kernel(feats_t, agg0, agg1, dpre0, dpre1, slots, papers, bundle):
    right = jnp.concatenate([dpre0[...], dpre1[...]], axis=0)
    aggs = jnp.concatenate([agg0[...], agg1[...]], axis=0)
    emb = aggs.shape[1]
    columns = right.shape[1] // LANES
    blocks = LANES // columns
    span = 2 * REL_ROWS
    where = iota((span * blocks, emb), 0)
    spread_rows = onehot(
        (where // span * REL_ROWS + where % span == iota((span * blocks, emb), 1))
        & (where % span < REL_ROWS)
    )
    aggs_t = dot(spread_rows, aggs, ((1,), (1,))).astype(BF16)
    for cb in range(columns):
        cols = right[:, cb * LANES : (cb + 1) * LANES]
        part_f = dot(feats_t[...], cols).astype(BF16)
        part_a = dot(aggs_t, cols)
        for i in range(blocks):
            d = cb * blocks + i
            bundle[d, :CAP, :] = slots[d]
            bundle[d, CAP:REL_AT, :] = part_f[i * SELF_ROWS : (i + 1) * SELF_ROWS]
            paper = papers[d].astype(F32)
            rel = part_a[i * span : (i + 1) * span] + paper[:span]
            bundle[d, REL_AT : REL_AT + span, :] = rel.astype(BF16)
            bundle[d, REL_AT + span :, :] = paper[span:].astype(BF16)


def weight_part(feats_t, agg0, agg1, dpre0, dpre1, slots, papers):
    return pl.pallas_call(
        weight_kernel,
        out_shape=jax.ShapeDtypeStruct((LANES, BUNDLE, LANES), BF16),
        in_specs=[VMEM] * 7,
        out_specs=VMEM,
        compiler_params=params(),
        name="weight_part",
    )(feats_t, agg0, agg1, dpre0, dpre1, slots, papers)


def sum_kernel(bundle, out, out_scr, sems):
    span = 2 * REL_ROWS
    half = [jnp.zeros((SELF_ROWS + span, LANES), F32) for _ in range(2)]
    for d in range(LANES):
        c = (d // GROUP) % 2
        half[c] = half[c] + bundle[d, CAP : REL_AT + span, :].astype(F32)
    rel = [h[SELF_ROWS : SELF_ROWS + REL_ROWS] for h in half]
    mine = jnp.concatenate([half[0][:SELF_ROWS], half[1][:SELF_ROWS], rel[0], rel[1]], axis=0)
    mine = mine.astype(BF16)
    for i in range(out_scr.shape[0]):
        out_scr[i] = mine
    q = out_scr.shape[0] // 4
    copies = fetch(
        [(out_scr.at[pl.ds(i * q, q)], out.at[pl.ds(i * q, q)]) for i in range(4)], sems
    )
    for c in copies:
        c.wait()


def sum_parts(bundle, peers):
    rows = 2 * (SELF_ROWS + REL_ROWS)
    return pl.pallas_call(
        sum_kernel,
        out_shape=pltpu.HBM((peers, rows, LANES), BF16),
        in_specs=[VMEM],
        out_specs=HBM,
        scratch_shapes=[
            pltpu.VMEM((peers, rows, LANES), BF16),
            pltpu.SemaphoreType.DMA((4,)),
        ],
        compiler_params=params(),
        name="sum_parts",
    )(bundle)


def spread_kernel(side, got, *rest):
    del side
    grad_self, grad_rel = rest[-2:]
    columns = got.shape[0]
    for cb in range(columns):
        rel = [[], []]
        for mp in range(GROUP):
            block = got[cb, 0, mp].astype(F32)
            for h in range(2):
                cols = slice((h * columns + cb) * LANES, (h * columns + cb + 1) * LANES)
                grad_self[mp * SELF_ROWS : (mp + 1) * SELF_ROWS, cols] = block[
                    h * SELF_ROWS : (h + 1) * SELF_ROWS
                ]
                at = 2 * SELF_ROWS + h * REL_ROWS
                rel[h].append(block[at : at + REL_ROWS])
        for h in range(2):
            cols = slice((h * columns + cb) * LANES, (h * columns + cb + 1) * LANES)
            grad_rel[:, cols] = jnp.concatenate(rel[h], axis=0)


def spread(side, got, feats, emb, hidden, others=()):
    columns = hidden // LANES // 2
    peers, rows, _ = got.shape
    steps = peers // columns // GROUP
    at = lambda i, side: (2 * i + side[0], 0)
    return pl.pallas_call(
        spread_kernel,
        grid_spec=pltpu.PrefetchScalarGridSpec(
            num_scalar_prefetch=1,
            grid=(steps,),
            in_specs=[
                pl.BlockSpec((columns, 1, GROUP, rows, LANES), lambda i, side: (0, i, 0, 0, 0))
            ]
            + [ANY] * len(others),
            out_specs=(
                pl.BlockSpec((feats // steps // 2, hidden), at),
                pl.BlockSpec((emb // steps // 2, hidden), at),
            ),
        ),
        out_shape=(
            jax.ShapeDtypeStruct((feats, hidden), F32),
            jax.ShapeDtypeStruct((emb, hidden), F32),
        ),
        input_output_aliases={2 + i: i for i in range(len(others))},
        compiler_params=params(),
        cost_estimate=pl.CostEstimate(
            flops=feats * hidden, bytes_accessed=3 * feats * hidden, transcendentals=0
        ),
        name="weight_out",
    )(side, got.reshape(columns, steps, GROUP, rows, LANES), *others)


def after_kernel(*refs):
    pass


def after(a, *ready):
    return pl.pallas_call(
        after_kernel,
        out_shape=jax.ShapeDtypeStruct(a.shape, a.dtype),
        in_specs=[ANY] * (1 + len(ready)),
        out_specs=ANY,
        input_output_aliases={0: 0},
        compiler_params=params(),
        name="after",
    )(a, *in_hbm(*ready))


def adam_kernel(
    wanted, bundle, table, m1, m2, new_table, new_m1, new_m2, done, arrived, hot_scr, side_scr, sem
):
    step = pl.program_id(0)
    lines = wanted.shape[0]
    done[...] = jnp.zeros_like(done)

    @pl.when(step == 0)
    def _():
        copy = pltpu.make_async_copy(bundle.at[:, pl.ds(0, CAP), :], arrived, sem.at[0])
        copy.start()
        lo = wanted[...] % 256
        hi = (wanted[...] // 256).astype(F32).T
        sub = iota((256, LANES), 0)
        for b in range(lines):
            at = slice(b * LANES, (b + 1) * LANES)
            hot_scr[:, at] = onehot(sub == lo[b : b + 1, :])
            side_scr[at, :] = jnp.broadcast_to(hi[:, b : b + 1], (LANES, LANES)).astype(BF16)
        copy.wait()

    here = side_scr[...] == step.astype(F32).astype(BF16)
    mark = jnp.where(here, BF16(1.0), BF16(0.0))
    got = arrived[...].reshape(LANES * CAP, LANES)
    both = dot(hot_scr[...], jnp.concatenate([got * mark, mark], axis=1))
    grad = both[:, :LANES]
    touched = both[:, LANES:] > 0.0
    m = 0.9 * m1[...] + 0.1 * grad
    v = 0.999 * m2[...] + 0.001 * grad * grad
    update = 0.05 * (m / (1.0 - 0.9**10)) / (jnp.sqrt(v / (1.0 - 0.999**10)) + 1e-08)
    new_table[...] = jnp.where(touched, table[...] - update, table[...])
    new_m1[...] = jnp.where(touched, m, m1[...])
    new_m2[...] = jnp.where(touched, v, m2[...])


def adam(wanted, bundle, table, m1, m2):
    rows = 256
    block = pl.BlockSpec((rows, LANES), lambda i: (i, 0))
    slots = LANES * CAP
    return pl.pallas_call(
        adam_kernel,
        grid=(table.shape[0] // rows,),
        out_shape=(jax.ShapeDtypeStruct(table.shape, F32),) * 3
        + (jax.ShapeDtypeStruct((8, LANES), F32),),
        in_specs=[pl.BlockSpec(wanted.shape, lambda i: (0, 0)), ANY, block, block, block],
        out_specs=(block, block, block, pl.BlockSpec((8, LANES), lambda i: (0, 0))),
        scratch_shapes=[
            pltpu.VMEM((LANES, CAP, LANES), BF16),
            pltpu.VMEM((rows, slots), BF16),
            pltpu.VMEM((slots, LANES), BF16),
            pltpu.SemaphoreType.DMA((1,)),
        ],
        cost_estimate=pl.CostEstimate(
            flops=2 * 2 * slots * LANES * table.shape[0],
            bytes_accessed=7 << 20,
            transcendentals=0,
        ),
        name="adam",
    )(wanted, bundle, table, m1, m2)


def shards(
    feats,
    edge_owner,
    edge_row,
    counts,
    table,
    moment1,
    moment2,
    w_self,
    w_rel,
    cotangent,
    next_owner,
    next_row,
    paper_table,
):
    every = ("chip", "core", "mp")
    peers = ("chip", "mp")
    devs = lax.axis_size(every)
    seeds, width = feats.shape
    hidden = cotangent.shape[1]
    emb = table.shape[1]
    core = lax.axis_index("core").astype(I32).reshape(1)
    group = lax.axis_index("mp").astype(I32).reshape(1)

    def exchange(a, axes):
        return lax.all_to_all(a, axes, split_axis=0, concat_axis=0, tiled=True)

    def swap(a):
        return lax.ppermute(a, "core", [(0, 1), (1, 0)])

    asked, seed_of, cnt, paper_pick, wide = place(
        group,
        edge_owner.reshape(-1, LANES),
        edge_row.reshape(-1, LANES),
        counts.reshape(1, -1),
        next_owner.reshape(1, -1),
        next_row.reshape(1, -1),
        table,
    )
    got = exchange(asked.reshape(devs, 1, LANES), every).reshape(devs, LANES)
    rows, wanted = gather(got, wide)
    fetched = exchange(rows.reshape(devs, CAP, emb), every).reshape(devs * CAP, emb)

    pre_self = prep(feats, w_self)
    feats_t = turn(feats, swap(feats))
    papers = paper_rows(got, paper_table)
    agg_b, dpre_here, dpre_there, grad = layer(
        core, fetched, seed_of, cnt, pre_self, w_rel, cotangent, feats_t, papers
    )

    agg_far, dpre_far = swap(agg_b), swap(dpre_there)
    slots, papers, feats_t = slot_grads(seed_of, grad, papers, feats_t)
    bundle = weight_part(feats_t, agg_b, agg_far, dpre_here, dpre_far, slots, papers)
    bundle = exchange(bundle, every)
    full = exchange(sum_parts(bundle, lax.axis_size(peers)), peers)
    new_table, new_moment1, new_moment2, done = adam(wanted, bundle, table, moment1, moment2)
    papers = bundle[:, PAPER_AT : PAPER_AT + FCAP * width // LANES, :].reshape(devs, -1)
    next_feats = functools.reduce(
        lambda a, b: a + b,
        [
            lax.dot_general(
                paper_pick[t],
                papers[:, t * width : (t + 1) * width],
                (((0,), (0,)), ((), ())),
                preferred_element_type=F32,
            )
            for t in range(FCAP)
        ],
    ).astype(BF16)
    full = after(full, done, next_feats)
    part = spread(core, full, width, emb, hidden)
    grad_self, grad_rel = spread(1 - core, swap(full), width, emb, hidden, part)
    return (new_table, new_moment1, new_moment2, grad_self, grad_rel, next_feats)


def solution(mesh):
    n_mp = mesh.shape["mp"]
    wide = Mesh(mesh.devices.reshape(-1, 2, n_mp), ("chip", "core", "mp"))
    rows = P(("chip", "core", "mp"), None)
    line = P(("chip", "core", "mp"))
    in_specs = (rows, rows, line, line, rows, rows, rows, P(), P(), rows, rows, line, rows)
    out_specs = (rows, rows, rows, P(), P(), rows)
    return jax.shard_map(shards, mesh=wide, in_specs=in_specs, out_specs=out_specs, check_vma=False)
```

```python
import functools

import jax
import jax.numpy as jnp
from jax import lax
from jax.experimental import pallas as pl
from jax.experimental.pallas import tpu as pltpu
from jax.sharding import Mesh, PartitionSpec as P

F32 = jnp.float32
BF16 = jnp.bfloat16
I32 = jnp.int32
LANES = 128
CAP = 32
FCAP = 2
GROUP = LANES // CAP
EMPTY = 4095
SELF_ROWS = 24
REL_ROWS = 4
REL_AT = CAP + SELF_ROWS
PAPER_AT = REL_AT + REL_ROWS
PAPER_ROWS = 12
TILE = 256
BUNDLE = PAPER_AT + PAPER_ROWS
VMEM = pl.BlockSpec(memory_space=pltpu.VMEM)
SMEM = pl.BlockSpec(memory_space=pltpu.SMEM)


def iota(shape, dim):
    return lax.broadcasted_iota(I32, shape, dim)


def dot(a, b, contract=((1,), (0,))):
    return lax.dot_general(a, b, (contract, ((), ())), preferred_element_type=F32)


def onehot(mask):
    return jnp.where(mask, F32(1.0), F32(0.0)).astype(BF16)

ANY = pl.BlockSpec(memory_space=pl.ANY)
HBM = pl.BlockSpec(memory_space=pltpu.HBM)


def params():
    return pltpu.CompilerParams(vmem_limit_bytes=24 * 1024 * 1024)


def in_hbm(*arrays):
    return [pltpu.with_memory_space_constraint(a, pltpu.HBM) for a in arrays]


def fetch(pairs, sems):
    copies = [pltpu.make_async_copy(a, b, sems.at[i]) for i, (a, b) in enumerate(pairs)]
    for c in copies:
        c.start()
    return copies


def place_kernel(
    lane_group,
    owner_in,
    row_in,
    counts_in,
    next_owner_in,
    next_row_in,
    table_in,
    asked,
    seed_of,
    cnt,
    paper_pick,
    wide,
    owner,
    row,
    counts,
    next_owner,
    next_row,
    table,
    seed_scr,
    sems,
):
    copies = fetch(
        [
            (owner_in, owner),
            (row_in, row),
            (counts_in, counts),
            (next_owner_in, next_owner),
            (next_row_in, next_row),
            (table_in, table),
        ],
        sems,
    )
    table_copy = copies.pop()
    devs = LANES
    blocks = owner.shape[0]
    group = lane_group[0]
    sub = iota((devs, LANES), 0)
    lane = iota((devs, LANES), 1)
    seeds_row = LANES // (LANES * blocks // devs)
    slots_per = LANES // seeds_row
    upper = onehot(sub < lane)
    ones = jnp.ones((devs, LANES), BF16)
    scan = jnp.concatenate([upper, ones], axis=1)
    pick = onehot(sub % seeds_row == lane // slots_per)
    for c in copies:
        c.wait()
    count_row = counts[...].astype(F32)
    spread = jnp.where(
        iota((blocks, LANES), 1) // seeds_row == iota((blocks, LANES), 0), count_row, F32(0.0)
    ).astype(BF16)
    cnt_edge = dot(spread, pick)
    k_edge = (iota((blocks, LANES), 1) % slots_per).astype(F32)
    live_owner = jnp.where(k_edge < cnt_edge, owner[...], -1)
    base = jnp.zeros((devs, LANES), F32)
    acc = jnp.zeros((devs, 3 * CAP), F32)
    ksub = iota((CAP, LANES), 0).astype(F32)
    for b in range(blocks):
        hot = sub == live_owner[b : b + 1, :]
        hot_f = jnp.where(hot, F32(1.0), F32(0.0))
        hot_b = hot_f.astype(BF16)
        scanned = dot(hot_b, scan)
        slot = jnp.sum(hot_f * (scanned[:, :LANES] + base), axis=0, keepdims=True)
        base = base + scanned[:, LANES:]
        at = ksub == slot
        r = row[b : b + 1, :]
        seed1 = b * seeds_row + iota((1, LANES), 1) // slots_per + 1
        vals = jnp.concatenate(
            [
                jnp.where(at, (r // LANES).astype(F32), F32(0.0)),
                jnp.where(at, (r % LANES).astype(F32), F32(0.0)),
                jnp.where(at, seed1.astype(F32), F32(0.0)),
            ],
            axis=0,
        ).astype(BF16)
        acc = acc + dot(hot_b, vals, ((1,), (1,)))
    acc_i = acc.astype(I32)
    seeds = acc_i[:, 2 * CAP :]
    wanted = jnp.where(seeds > 0, acc_i[:, :CAP] * LANES + acc_i[:, CAP : 2 * CAP], EMPTY)

    hot = sub == next_owner[...]
    hot_f = jnp.where(hot, F32(1.0), F32(0.0))
    hot_b = hot_f.astype(BF16)
    before = dot(hot_b, upper)
    slot = jnp.sum(hot_f * before, axis=0, keepdims=True)
    nrow = next_row[...]
    for t in range(FCAP):
        paper_pick[t] = jnp.where(slot == t, hot_f, F32(0.0)).astype(BF16)
    at = iota((CAP, LANES), 0) == slot.astype(I32)
    vals = jnp.concatenate(
        [
            jnp.where(at, (nrow // LANES).astype(F32), F32(0.0)),
            jnp.where(at, (nrow % LANES).astype(F32), F32(0.0)),
        ],
        axis=0,
    ).astype(BF16)
    pacc = dot(hot_b, vals, ((1,), (1,))).astype(I32)
    paper = pacc[:, :CAP] * LANES + pacc[:, CAP:]

    quarter = lane // CAP
    wide_wanted = jnp.concatenate([wanted] * GROUP, axis=1)
    wide_paper = jnp.concatenate([paper] * GROUP, axis=1)
    asked[...] = jnp.where(
        quarter == group,
        wide_wanted,
        jnp.where(quarter == (group + 1) % GROUP, wide_paper, 0),
    )
    seed_scr[...] = jnp.where(quarter == sub % GROUP, jnp.concatenate([seeds] * GROUP, axis=1), 0)
    total = seed_scr[pl.ds(0, devs // GROUP, stride=GROUP), :]
    for i in range(1, GROUP):
        total = total + seed_scr[pl.ds(i, devs // GROUP, stride=GROUP), :]
    seed_of[...] = total
    cnt[...] = jnp.broadcast_to(count_row, (devs, LANES)).T
    table_copy.wait()
    for q in range(table.shape[0] // TILE):
        wide[:, q * LANES : (q + 1) * LANES] = table[q * TILE : (q + 1) * TILE, :].astype(BF16)


def place(group, owner, row, counts, next_owner, next_row, table):
    devs = LANES
    ins = (owner, row, counts, next_owner, next_row, table)
    return pl.pallas_call(
        place_kernel,
        out_shape=(
            pltpu.VMEM((devs, LANES), I32),
            jax.ShapeDtypeStruct((devs // GROUP, LANES), I32),
            jax.ShapeDtypeStruct((devs, LANES), F32),
            jax.ShapeDtypeStruct((FCAP, devs, LANES), BF16),
            pltpu.VMEM((TILE, table.shape[0] // TILE * LANES), BF16),
        ),
        in_specs=[SMEM] + [HBM] * len(ins),
        out_specs=(VMEM, VMEM, VMEM, VMEM, VMEM),
        scratch_shapes=[pltpu.VMEM(a.shape, a.dtype) for a in ins]
        + [pltpu.VMEM((devs, LANES), I32), pltpu.SemaphoreType.DMA((len(ins),))],
        compiler_params=params(),
        name="place",
    )(group, *in_hbm(*ins))


def gather_kernel(got, wide, rows, wanted_out, hot_scr, hi_scr, out_scr, out_sems):
    devs = LANES
    lines = devs // GROUP
    quarter = iota((lines, LANES), 1) // CAP
    wanted = jnp.zeros((lines, LANES), I32)
    for i in range(GROUP):
        wanted = wanted + jnp.where(quarter == i, got[pl.ds(i, lines, stride=GROUP), :], 0)
    wanted_out[...] = wanted
    lo = (wanted % TILE).T
    hi = (wanted // TILE).T
    lanes = iota((LANES, TILE), 1)
    for b in range(lines):
        hot_scr[b * LANES : (b + 1) * LANES, :] = onehot(lo[:, b : b + 1] == lanes)
        hi_scr[b * LANES : (b + 1) * LANES, :] = jnp.broadcast_to(hi[:, b : b + 1], (LANES, LANES))
    chunk = 512
    outs = []
    for c in range(out_scr.shape[0] // chunk):
        at = pl.ds(c * chunk, chunk)
        hot = hot_scr[at, :]
        high = hi_scr[at, :]
        out = jnp.zeros((chunk, LANES), F32)
        for q in range(0, wide.shape[1] // LANES, 2):
            both = dot(hot, wide[:, q * LANES : (q + 2) * LANES])
            out = jnp.where(high == q, both[:, :LANES], out)
            out = jnp.where(high == q + 1, both[:, LANES:], out)
        out_scr[at, :] = out.astype(BF16)
        copy = pltpu.make_async_copy(out_scr.at[at, :], rows.at[at, :], out_sems.at[c])
        copy.start()
        outs.append(copy)
    for copy in outs:
        copy.wait()


def gather(got, wide):
    slots = LANES * CAP
    return pl.pallas_call(
        gather_kernel,
        out_shape=(
            pltpu.HBM((slots, LANES), BF16),
            pltpu.HBM((LANES // GROUP, LANES), I32),
        ),
        in_specs=[VMEM, VMEM],
        out_specs=(HBM, VMEM),
        scratch_shapes=[
            pltpu.VMEM((slots, TILE), BF16),
            pltpu.VMEM((slots, LANES), I32),
            pltpu.VMEM((slots, LANES), BF16),
            pltpu.SemaphoreType.DMA((slots // 512,)),
        ],
        compiler_params=params(),
        name="gather_rows",
    )(got, wide)


def paper_kernel(got, paper_in, rows, paper, scr, sem):
    copies = fetch([(paper_in, paper)], sem)
    devs = LANES
    sub = iota((devs, LANES), 0)
    lane = iota((devs, LANES), 1)
    first = ((sub % GROUP + 1) % GROUP) * CAP
    parts = paper.shape[1] // LANES
    span = REL_ROWS + PAPER_ROWS
    for i in range(REL_ROWS):
        scr[pl.ds(i, devs, stride=span), :] = jnp.zeros((devs, LANES), F32)
    copies[0].wait()
    for t in range(FCAP):
        asked = jnp.sum(jnp.where(lane == first + t, got[...], 0), axis=1, keepdims=True)
        hot = onehot(asked == iota((devs, paper.shape[0]), 1))
        found = dot(hot, paper[...])
        for i in range(parts):
            scr[pl.ds(REL_ROWS + t * parts + i, devs, stride=span), :] = found[
                :, i * LANES : (i + 1) * LANES
            ]
    rows[...] = scr[...].astype(BF16).reshape(rows.shape)


def paper_rows(got, paper):
    span = REL_ROWS + PAPER_ROWS
    return pl.pallas_call(
        paper_kernel,
        out_shape=pltpu.HBM((LANES, span, LANES), BF16),
        in_specs=[VMEM, HBM],
        out_specs=VMEM,
        scratch_shapes=[
            pltpu.VMEM(paper.shape, BF16),
            pltpu.VMEM((LANES * span, LANES), F32),
            pltpu.SemaphoreType.DMA((1,)),
        ],
        compiler_params=params(),
        cost_estimate=pl.CostEstimate(
            flops=2 * FCAP * LANES * paper.shape[0] * paper.shape[1],
            bytes_accessed=4 * paper.size,
            transcendentals=0,
        ),
        name="gather_papers",
    )(got, *in_hbm(paper))


def prep_kernel(feats, w_self_in, cot_in, w_in, pre, cot, w_rel, w_self, sems):
    copies = fetch([(w_self_in, w_self), (cot_in, cot), (w_in, w_rel)], sems)
    copies[0].wait()
    pre[...] = dot(feats[...], w_self[...])
    for c in copies[1:]:
        c.wait()


def prep(feats, w_self, cotangent, w_rel):
    return pl.pallas_call(
        prep_kernel,
        out_shape=(
            pltpu.VMEM(cotangent.shape, F32),
            pltpu.VMEM(cotangent.shape, F32),
            pltpu.VMEM(w_rel.shape, BF16),
        ),
        in_specs=[VMEM, HBM, HBM, HBM],
        out_specs=(VMEM, VMEM, VMEM),
        scratch_shapes=[pltpu.VMEM(w_self.shape, BF16), pltpu.SemaphoreType.DMA((3,))],
        compiler_params=params(),
        cost_estimate=pl.CostEstimate(
            flops=2 * feats.size * w_self.shape[1], bytes_accessed=4 << 20, transcendentals=0
        ),
        name="prep",
    )(feats, *in_hbm(w_self, cotangent, w_rel))


def turn_kernel(feats, far, out):
    seeds = feats.shape[0]
    out[:, :seeds] = feats[...].T
    out[:, seeds:] = far[...].T


def turn(feats, far):
    seeds, width = feats.shape
    return pl.pallas_call(
        turn_kernel,
        out_shape=pltpu.HBM((width, 2 * seeds), BF16),
        in_specs=[VMEM, VMEM],
        out_specs=VMEM,
        compiler_params=params(),
        cost_estimate=pl.CostEstimate(flops=0, bytes_accessed=8 * feats.size, transcendentals=0),
        name="turn",
    )(feats, far)


def layer_kernel(
    core,
    fetched,
    seed_of,
    cnt,
    pre_self,
    cot,
    w_rel,
    *rest,
):
    agg_out, here_out, there_out, grad_out = rest[-4:]
    devs = LANES
    lines = seed_of.shape[0]
    seed1 = iota((devs, LANES), 0) + 1
    agg = jnp.zeros((devs, LANES), F32)
    for b in range(0, lines, 2):
        match = jnp.concatenate(
            [onehot(seed1 == seed_of[b : b + 1, :]), onehot(seed1 == seed_of[b + 1 : b + 2, :])],
            axis=1,
        )
        agg = agg + dot(match, fetched[b * LANES : (b + 2) * LANES, :])
    count = cnt[...]
    agg_b = (agg / count).astype(BF16)
    agg_out[...] = agg_b
    pre = pre_self[...] + dot(agg_b, w_rel[...])
    sig = jax.nn.sigmoid(pre)
    dpre = (cot[...] * sig * (1.0 + pre * (1.0 - sig))).astype(BF16)
    half = dpre.shape[1] // 2
    first = core[0] == 0
    here_out[...] = jnp.where(first, dpre[:, :half], dpre[:, half:])
    there_out[...] = jnp.where(first, dpre[:, half:], dpre[:, :half])
    dagg = dot(dpre, w_rel[...], ((1,), (1,)))
    grad_out[...] = (dagg / count).astype(BF16)


def layer(core, fetched, seed_of, cnt, pre_self, cotangent, w_rel, *ready):
    seeds, hidden = cotangent.shape
    return pl.pallas_call(
        layer_kernel,
        out_shape=(
            jax.ShapeDtypeStruct((seeds, LANES), BF16),
            jax.ShapeDtypeStruct((seeds, hidden // 2), BF16),
            jax.ShapeDtypeStruct((seeds, hidden // 2), BF16),
            jax.ShapeDtypeStruct((seeds, LANES), BF16),
        ),
        in_specs=[SMEM] + [VMEM] * 6 + [ANY] * len(ready),
        out_specs=(VMEM, VMEM, VMEM, VMEM),
        compiler_params=params(),
        name="layer",
    )(core, fetched, seed_of, cnt, pre_self, cotangent, w_rel, *in_hbm(*ready))


def slots_kernel(seed_of, grad, papers_in, feats_in, out, papers, feats, sems):
    copies = fetch([(papers_in, papers), (feats_in, feats)], sems)
    seeds_t = seed_of[...].T
    lane1 = iota((LANES, LANES), 1) + 1
    for b in range(seed_of.shape[0]):
        match = onehot(seeds_t[:, b : b + 1] == lane1)
        out[b * GROUP : (b + 1) * GROUP] = (
            dot(match, grad[...]).astype(BF16).reshape(GROUP, CAP, LANES)
        )
    for c in copies:
        c.wait()


def slot_grads(seed_of, grad, papers, feats_t):
    return pl.pallas_call(
        slots_kernel,
        out_shape=(
            pltpu.VMEM((LANES, CAP, LANES), BF16),
            pltpu.VMEM(papers.shape, BF16),
            pltpu.VMEM(feats_t.shape, BF16),
        ),
        in_specs=[VMEM, VMEM, HBM, HBM],
        out_specs=(VMEM, VMEM, VMEM),
        scratch_shapes=[pltpu.SemaphoreType.DMA((2,))],
        compiler_params=params(),
        cost_estimate=pl.CostEstimate(
            flops=2 * LANES * CAP * LANES * LANES, bytes_accessed=4 << 20, transcendentals=0
        ),
        name="slot_grads",
    )(seed_of, grad, *in_hbm(papers, feats_t))


def weight_kernel(feats_t, agg0, agg1, dpre0, dpre1, slots, papers, bundle):
    right = jnp.concatenate([dpre0[...], dpre1[...]], axis=0)
    aggs = jnp.concatenate([agg0[...], agg1[...]], axis=0)
    emb = aggs.shape[1]
    columns = right.shape[1] // LANES
    blocks = LANES // columns
    span = 2 * REL_ROWS
    where = iota((span * blocks, emb), 0)
    spread_rows = onehot(
        (where // span * REL_ROWS + where % span == iota((span * blocks, emb), 1))
        & (where % span < REL_ROWS)
    )
    aggs_t = dot(spread_rows, aggs, ((1,), (1,))).astype(BF16)
    for cb in range(columns):
        cols = right[:, cb * LANES : (cb + 1) * LANES]
        part_f = dot(feats_t[...], cols).astype(BF16)
        part_a = dot(aggs_t, cols)
        for i in range(blocks):
            d = cb * blocks + i
            bundle[d, :CAP, :] = slots[d]
            bundle[d, CAP:REL_AT, :] = part_f[i * SELF_ROWS : (i + 1) * SELF_ROWS]
            paper = papers[d].astype(F32)
            rel = part_a[i * span : (i + 1) * span] + paper[:span]
            bundle[d, REL_AT : REL_AT + span, :] = rel.astype(BF16)
            bundle[d, REL_AT + span :, :] = paper[span:].astype(BF16)


def weight_part(feats_t, agg0, agg1, dpre0, dpre1, slots, papers):
    return pl.pallas_call(
        weight_kernel,
        out_shape=jax.ShapeDtypeStruct((LANES, BUNDLE, LANES), BF16),
        in_specs=[VMEM] * 7,
        out_specs=VMEM,
        compiler_params=params(),
        name="weight_part",
    )(feats_t, agg0, agg1, dpre0, dpre1, slots, papers)


def sum_kernel(bundle, out, out_scr, sems):
    span = 2 * REL_ROWS
    half = [jnp.zeros((SELF_ROWS + span, LANES), F32) for _ in range(2)]
    for d in range(LANES):
        c = (d // GROUP) % 2
        half[c] = half[c] + bundle[d, CAP : REL_AT + span, :].astype(F32)
    rel = [h[SELF_ROWS : SELF_ROWS + REL_ROWS] for h in half]
    mine = jnp.concatenate([half[0][:SELF_ROWS], half[1][:SELF_ROWS], rel[0], rel[1]], axis=0)
    mine = mine.astype(BF16)
    for i in range(out_scr.shape[0]):
        out_scr[i] = mine
    q = out_scr.shape[0] // 4
    copies = fetch(
        [(out_scr.at[pl.ds(i * q, q)], out.at[pl.ds(i * q, q)]) for i in range(4)], sems
    )
    for c in copies:
        c.wait()


def sum_parts(bundle, peers):
    rows = 2 * (SELF_ROWS + REL_ROWS)
    return pl.pallas_call(
        sum_kernel,
        out_shape=pltpu.HBM((peers, rows, LANES), BF16),
        in_specs=[VMEM],
        out_specs=HBM,
        scratch_shapes=[
            pltpu.VMEM((peers, rows, LANES), BF16),
            pltpu.SemaphoreType.DMA((4,)),
        ],
        compiler_params=params(),
        name="sum_parts",
    )(bundle)


def spread_kernel(side, got, *rest):
    grad_self, grad_rel, self_scr, rel_scr, sems = rest[-5:]
    columns, steps = got.shape[:2]
    copies = []
    rows_self = GROUP * SELF_ROWS
    rows_rel = GROUP * REL_ROWS
    for i in range(steps):
        for cb in range(columns):
            rel = [[], []]
            for mp in range(GROUP):
                block = got[cb, i, mp].astype(F32)
                for h in range(2):
                    cols = slice((h * columns + cb) * LANES, (h * columns + cb + 1) * LANES)
                    self_scr[i, mp * SELF_ROWS : (mp + 1) * SELF_ROWS, cols] = block[
                        h * SELF_ROWS : (h + 1) * SELF_ROWS
                    ]
                    at = 2 * SELF_ROWS + h * REL_ROWS
                    rel[h].append(block[at : at + REL_ROWS])
            for h in range(2):
                cols = slice((h * columns + cb) * LANES, (h * columns + cb + 1) * LANES)
                rel_scr[i, :, cols] = jnp.concatenate(rel[h], axis=0)
        block_at = 2 * i + side[0]
        copies += fetch(
            [
                (self_scr.at[i], grad_self.at[pl.ds(block_at * rows_self, rows_self), :]),
                (rel_scr.at[i], grad_rel.at[pl.ds(block_at * rows_rel, rows_rel), :]),
            ],
            sems.at[i],
        )
    for c in copies:
        c.wait()


def spread(side, got, feats, emb, hidden, others=()):
    columns = hidden // LANES // 2
    peers, rows, _ = got.shape
    steps = peers // columns // GROUP
    return pl.pallas_call(
        spread_kernel,
        out_shape=(
            pltpu.HBM((feats, hidden), F32),
            pltpu.HBM((emb, hidden), F32),
        ),
        in_specs=[SMEM, VMEM] + [HBM] * len(others),
        out_specs=(HBM, HBM),
        scratch_shapes=[
            pltpu.VMEM((steps, GROUP * SELF_ROWS, hidden), F32),
            pltpu.VMEM((steps, GROUP * REL_ROWS, hidden), F32),
            pltpu.SemaphoreType.DMA((steps, 2)),
        ],
        input_output_aliases={2 + i: i for i in range(len(others))},
        compiler_params=params(),
        cost_estimate=pl.CostEstimate(
            flops=feats * hidden, bytes_accessed=3 * feats * hidden, transcendentals=0
        ),
        name="weight_out",
    )(side, got.reshape(columns, steps, GROUP, rows, LANES), *others)


def after_kernel(*refs):
    pass


def after(a, *ready):
    return pl.pallas_call(
        after_kernel,
        out_shape=jax.ShapeDtypeStruct(a.shape, a.dtype),
        in_specs=[ANY] * (1 + len(ready)),
        out_specs=ANY,
        input_output_aliases={0: 0},
        compiler_params=params(),
        name="after",
    )(a, *in_hbm(*ready))


def adam_kernel(
    wanted, bundle, table, m1, m2, new_table, new_m1, new_m2, done, arrived, hot_scr, side_scr, sem
):
    step = pl.program_id(0)
    lines = wanted.shape[0]
    done[...] = jnp.zeros_like(done)

    @pl.when(step == 0)
    def _():
        copy = pltpu.make_async_copy(bundle.at[:, pl.ds(0, CAP), :], arrived, sem.at[0])
        copy.start()
        lo = wanted[...] % 256
        hi = (wanted[...] // 256).astype(F32).T
        sub = iota((256, LANES), 0)
        for b in range(lines):
            at = slice(b * LANES, (b + 1) * LANES)
            hot_scr[:, at] = onehot(sub == lo[b : b + 1, :])
            side_scr[at, :] = jnp.broadcast_to(hi[:, b : b + 1], (LANES, LANES)).astype(BF16)
        copy.wait()

    here = side_scr[...] == step.astype(F32).astype(BF16)
    mark = jnp.where(here, BF16(1.0), BF16(0.0))
    got = arrived[...].reshape(LANES * CAP, LANES)
    both = dot(hot_scr[...], jnp.concatenate([got * mark, mark], axis=1))
    grad = both[:, :LANES]
    touched = both[:, LANES:] > 0.0
    m = 0.9 * m1[...] + 0.1 * grad
    v = 0.999 * m2[...] + 0.001 * grad * grad
    update = 0.05 * (m / (1.0 - 0.9**10)) / (jnp.sqrt(v / (1.0 - 0.999**10)) + 1e-08)
    new_table[...] = jnp.where(touched, table[...] - update, table[...])
    new_m1[...] = jnp.where(touched, m, m1[...])
    new_m2[...] = jnp.where(touched, v, m2[...])


def adam(wanted, bundle, table, m1, m2):
    rows = 256
    block = pl.BlockSpec((rows, LANES), lambda i: (i, 0))
    slots = LANES * CAP
    return pl.pallas_call(
        adam_kernel,
        grid=(table.shape[0] // rows,),
        out_shape=(jax.ShapeDtypeStruct(table.shape, F32),) * 3
        + (jax.ShapeDtypeStruct((8, LANES), F32),),
        in_specs=[pl.BlockSpec(wanted.shape, lambda i: (0, 0)), ANY, block, block, block],
        out_specs=(block, block, block, pl.BlockSpec((8, LANES), lambda i: (0, 0))),
        scratch_shapes=[
            pltpu.VMEM((LANES, CAP, LANES), BF16),
            pltpu.VMEM((rows, slots), BF16),
            pltpu.VMEM((slots, LANES), BF16),
            pltpu.SemaphoreType.DMA((1,)),
        ],
        cost_estimate=pl.CostEstimate(
            flops=2 * 2 * slots * LANES * table.shape[0],
            bytes_accessed=7 << 20,
            transcendentals=0,
        ),
        name="adam",
    )(wanted, bundle, table, m1, m2)


def shards(
    feats,
    edge_owner,
    edge_row,
    counts,
    table,
    moment1,
    moment2,
    w_self,
    w_rel,
    cotangent,
    next_owner,
    next_row,
    paper_table,
):
    every = ("chip", "core", "mp")
    peers = ("chip", "mp")
    devs = lax.axis_size(every)
    seeds, width = feats.shape
    hidden = cotangent.shape[1]
    emb = table.shape[1]
    core = lax.axis_index("core").astype(I32).reshape(1)
    group = lax.axis_index("mp").astype(I32).reshape(1)

    def exchange(a, axes):
        return lax.all_to_all(a, axes, split_axis=0, concat_axis=0, tiled=True)

    def swap(a):
        return lax.ppermute(a, "core", [(0, 1), (1, 0)])

    asked, seed_of, cnt, paper_pick, wide = place(
        group,
        edge_owner.reshape(-1, LANES),
        edge_row.reshape(-1, LANES),
        counts.reshape(1, -1),
        next_owner.reshape(1, -1),
        next_row.reshape(1, -1),
        table,
    )
    got = exchange(asked.reshape(devs, 1, LANES), every).reshape(devs, LANES)
    rows, wanted = gather(got, wide)
    fetched = exchange(rows.reshape(devs, CAP, emb), every).reshape(devs * CAP, emb)

    pre_self, cot, w_rel = prep(feats, w_self, cotangent, w_rel)
    feats_t = turn(feats, swap(feats))
    papers = paper_rows(got, paper_table)
    agg_b, dpre_here, dpre_there, grad = layer(
        core, fetched, seed_of, cnt, pre_self, cot, w_rel, feats_t, papers
    )

    agg_far, dpre_far = swap(agg_b), swap(dpre_there)
    slots, papers, feats_t = slot_grads(seed_of, grad, papers, feats_t)
    bundle = weight_part(feats_t, agg_b, agg_far, dpre_here, dpre_far, slots, papers)
    bundle = exchange(bundle, every)
    full = exchange(sum_parts(bundle, lax.axis_size(peers)), peers)
    new_table, new_moment1, new_moment2, done = adam(wanted, bundle, table, moment1, moment2)
    papers = bundle[:, PAPER_AT : PAPER_AT + FCAP * width // LANES, :].reshape(devs, -1)
    next_feats = functools.reduce(
        lambda a, b: a + b,
        [
            lax.dot_general(
                paper_pick[t],
                papers[:, t * width : (t + 1) * width],
                (((0,), (0,)), ((), ())),
                preferred_element_type=F32,
            )
            for t in range(FCAP)
        ],
    ).astype(BF16)
    full = after(full, done, next_feats)
    part = spread(core, full, width, emb, hidden)
    grad_self, grad_rel = spread(1 - core, swap(full), width, emb, hidden, part)
    return (new_table, new_moment1, new_moment2, grad_self, grad_rel, next_feats)


def solution(mesh):
    n_mp = mesh.shape["mp"]
    wide = Mesh(mesh.devices.reshape(-1, 2, n_mp), ("chip", "core", "mp"))
    rows = P(("chip", "core", "mp"), None)
    line = P(("chip", "core", "mp"))
    in_specs = (rows, rows, line, line, rows, rows, rows, P(), P(), rows, rows, line, rows)
    out_specs = (rows, rows, rows, P(), P(), rows)
    return jax.shard_map(shards, mesh=wide, in_specs=in_specs, out_specs=out_specs, check_vma=False)
```

```python
import functools

import jax
import jax.numpy as jnp
from jax import lax
from jax.experimental import pallas as pl
from jax.experimental.pallas import tpu as pltpu
from jax.sharding import Mesh, PartitionSpec as P

F32 = jnp.float32
BF16 = jnp.bfloat16
I32 = jnp.int32
LANES = 128
CAP = 32
FCAP = 2
GROUP = LANES // CAP
EMPTY = 4095
SELF_ROWS = 24
REL_ROWS = 4
REL_AT = CAP + SELF_ROWS
PAPER_AT = REL_AT + REL_ROWS
PAPER_ROWS = 12
TILE = 256
BUNDLE = PAPER_AT + PAPER_ROWS
VMEM = pl.BlockSpec(memory_space=pltpu.VMEM)
SMEM = pl.BlockSpec(memory_space=pltpu.SMEM)


def iota(shape, dim):
    return lax.broadcasted_iota(I32, shape, dim)


def dot(a, b, contract=((1,), (0,))):
    return lax.dot_general(a, b, (contract, ((), ())), preferred_element_type=F32)


def onehot(mask):
    return jnp.where(mask, F32(1.0), F32(0.0)).astype(BF16)

ANY = pl.BlockSpec(memory_space=pl.ANY)
HBM = pl.BlockSpec(memory_space=pltpu.HBM)


def params():
    return pltpu.CompilerParams(vmem_limit_bytes=24 * 1024 * 1024)


def in_hbm(*arrays):
    return [pltpu.with_memory_space_constraint(a, pltpu.HBM) for a in arrays]


def fetch(pairs, sems):
    copies = [pltpu.make_async_copy(a, b, sems.at[i]) for i, (a, b) in enumerate(pairs)]
    for c in copies:
        c.start()
    return copies


def place_kernel(
    lane_group,
    owner_in,
    row_in,
    counts_in,
    next_owner_in,
    next_row_in,
    table_in,
    asked,
    seed_of,
    cnt,
    paper_pick,
    wide,
    owner,
    row,
    counts,
    next_owner,
    next_row,
    table,
    seed_scr,
    sems,
):
    copies = fetch(
        [
            (owner_in, owner),
            (row_in, row),
            (counts_in, counts),
            (next_owner_in, next_owner),
            (next_row_in, next_row),
            (table_in, table),
        ],
        sems,
    )
    table_copy = copies.pop()
    devs = LANES
    blocks = owner.shape[0]
    group = lane_group[0]
    sub = iota((devs, LANES), 0)
    lane = iota((devs, LANES), 1)
    seeds_row = LANES // (LANES * blocks // devs)
    slots_per = LANES // seeds_row
    upper = onehot(sub < lane)
    ones = jnp.ones((devs, LANES), BF16)
    scan = jnp.concatenate([upper, ones], axis=1)
    pick = onehot(sub % seeds_row == lane // slots_per)
    for c in copies:
        c.wait()
    count_row = counts[...].astype(F32)
    spread = jnp.where(
        iota((blocks, LANES), 1) // seeds_row == iota((blocks, LANES), 0), count_row, F32(0.0)
    ).astype(BF16)
    cnt_edge = dot(spread, pick)
    k_edge = (iota((blocks, LANES), 1) % slots_per).astype(F32)
    live_owner = jnp.where(k_edge < cnt_edge, owner[...], -1)
    base = jnp.zeros((devs, LANES), F32)
    hots, values = [], []
    ksub = iota((CAP, LANES), 0).astype(F32)
    for b in range(blocks):
        hot = sub == live_owner[b : b + 1, :]
        hot_f = jnp.where(hot, F32(1.0), F32(0.0))
        hot_b = hot_f.astype(BF16)
        scanned = dot(hot_b, scan)
        slot = jnp.sum(hot_f * (scanned[:, :LANES] + base), axis=0, keepdims=True)
        base = base + scanned[:, LANES:]
        at = ksub == slot
        r = row[b : b + 1, :]
        seed1 = b * seeds_row + iota((1, LANES), 1) // slots_per + 1
        vals = jnp.concatenate(
            [
                jnp.where(at, (r // LANES).astype(F32), F32(0.0)),
                jnp.where(at, (r % LANES).astype(F32), F32(0.0)),
                jnp.where(at, seed1.astype(F32), F32(0.0)),
            ],
            axis=0,
        ).astype(BF16)
        hots.append(hot_b)
        values.append(vals)
    values = jnp.concatenate(values, axis=1)
    acc_i = dot(jnp.concatenate(hots, axis=1), values, ((1,), (1,))).astype(I32)
    seeds = acc_i[:, 2 * CAP :]
    wanted = jnp.where(seeds > 0, acc_i[:, :CAP] * LANES + acc_i[:, CAP : 2 * CAP], EMPTY)

    hot = sub == next_owner[...]
    hot_f = jnp.where(hot, F32(1.0), F32(0.0))
    hot_b = hot_f.astype(BF16)
    before = dot(hot_b, upper)
    slot = jnp.sum(hot_f * before, axis=0, keepdims=True)
    nrow = next_row[...]
    for t in range(FCAP):
        paper_pick[t] = jnp.where(slot == t, hot_f, F32(0.0)).astype(BF16)
    at = iota((CAP, LANES), 0) == slot.astype(I32)
    vals = jnp.concatenate(
        [
            jnp.where(at, (nrow // LANES).astype(F32), F32(0.0)),
            jnp.where(at, (nrow % LANES).astype(F32), F32(0.0)),
        ],
        axis=0,
    ).astype(BF16)
    pacc = dot(hot_b, vals, ((1,), (1,))).astype(I32)
    paper = pacc[:, :CAP] * LANES + pacc[:, CAP:]

    quarter = lane // CAP
    wide_wanted = jnp.concatenate([wanted] * GROUP, axis=1)
    wide_paper = jnp.concatenate([paper] * GROUP, axis=1)
    asked[...] = jnp.where(
        quarter == group,
        wide_wanted,
        jnp.where(quarter == (group + 1) % GROUP, wide_paper, 0),
    )
    seed_scr[...] = jnp.where(quarter == sub % GROUP, jnp.concatenate([seeds] * GROUP, axis=1), 0)
    total = seed_scr[pl.ds(0, devs // GROUP, stride=GROUP), :]
    for i in range(1, GROUP):
        total = total + seed_scr[pl.ds(i, devs // GROUP, stride=GROUP), :]
    seed_of[...] = total
    cnt[...] = jnp.broadcast_to(count_row, (devs, LANES)).T
    table_copy.wait()
    for q in range(table.shape[0] // TILE):
        wide[:, q * LANES : (q + 1) * LANES] = table[q * TILE : (q + 1) * TILE, :].astype(BF16)


def place(group, owner, row, counts, next_owner, next_row, table):
    devs = LANES
    ins = (owner, row, counts, next_owner, next_row, table)
    return pl.pallas_call(
        place_kernel,
        out_shape=(
            pltpu.VMEM((devs, LANES), I32),
            jax.ShapeDtypeStruct((devs // GROUP, LANES), I32),
            jax.ShapeDtypeStruct((devs, LANES), F32),
            jax.ShapeDtypeStruct((FCAP, devs, LANES), BF16),
            pltpu.VMEM((TILE, table.shape[0] // TILE * LANES), BF16),
        ),
        in_specs=[SMEM] + [HBM] * len(ins),
        out_specs=(VMEM, VMEM, VMEM, VMEM, VMEM),
        scratch_shapes=[pltpu.VMEM(a.shape, a.dtype) for a in ins]
        + [pltpu.VMEM((devs, LANES), I32), pltpu.SemaphoreType.DMA((len(ins),))],
        compiler_params=params(),
        name="place",
    )(group, *in_hbm(*ins))


def gather_kernel(got, wide, rows, wanted_out, hot_scr, hi_scr, out_scr, out_sems):
    devs = LANES
    lines = devs // GROUP
    quarter = iota((lines, LANES), 1) // CAP
    wanted = jnp.zeros((lines, LANES), I32)
    for i in range(GROUP):
        wanted = wanted + jnp.where(quarter == i, got[pl.ds(i, lines, stride=GROUP), :], 0)
    wanted_out[...] = wanted
    lo = (wanted % TILE).T
    hi = (wanted // TILE).T
    lanes = iota((LANES, TILE), 1)
    for b in range(lines):
        hot_scr[b * LANES : (b + 1) * LANES, :] = onehot(lo[:, b : b + 1] == lanes)
        hi_scr[b * LANES : (b + 1) * LANES, :] = jnp.broadcast_to(hi[:, b : b + 1], (LANES, LANES))
    chunk = 512
    outs = []
    for c in range(out_scr.shape[0] // chunk):
        at = pl.ds(c * chunk, chunk)
        hot = hot_scr[at, :]
        high = hi_scr[at, :]
        out = jnp.zeros((chunk, LANES), F32)
        for q in range(0, wide.shape[1] // LANES, 2):
            both = dot(hot, wide[:, q * LANES : (q + 2) * LANES])
            out = jnp.where(high == q, both[:, :LANES], out)
            out = jnp.where(high == q + 1, both[:, LANES:], out)
        out_scr[at, :] = out.astype(BF16)
        copy = pltpu.make_async_copy(out_scr.at[at, :], rows.at[at, :], out_sems.at[c])
        copy.start()
        outs.append(copy)
    for copy in outs:
        copy.wait()


def gather(got, wide):
    slots = LANES * CAP
    return pl.pallas_call(
        gather_kernel,
        out_shape=(
            pltpu.HBM((slots, LANES), BF16),
            pltpu.HBM((LANES // GROUP, LANES), I32),
        ),
        in_specs=[VMEM, VMEM],
        out_specs=(HBM, VMEM),
        scratch_shapes=[
            pltpu.VMEM((slots, TILE), BF16),
            pltpu.VMEM((slots, LANES), I32),
            pltpu.VMEM((slots, LANES), BF16),
            pltpu.SemaphoreType.DMA((slots // 512,)),
        ],
        compiler_params=params(),
        name="gather_rows",
    )(got, wide)


def paper_kernel(got, paper_in, rows, paper, scr, sem):
    copies = fetch([(paper_in, paper)], sem)
    devs = LANES
    sub = iota((devs, LANES), 0)
    lane = iota((devs, LANES), 1)
    first = ((sub % GROUP + 1) % GROUP) * CAP
    parts = paper.shape[1] // LANES
    span = REL_ROWS + PAPER_ROWS
    for i in range(REL_ROWS):
        scr[pl.ds(i, devs, stride=span), :] = jnp.zeros((devs, LANES), F32)
    copies[0].wait()
    for t in range(FCAP):
        asked = jnp.sum(jnp.where(lane == first + t, got[...], 0), axis=1, keepdims=True)
        hot = onehot(asked == iota((devs, paper.shape[0]), 1))
        found = dot(hot, paper[...])
        for i in range(parts):
            scr[pl.ds(REL_ROWS + t * parts + i, devs, stride=span), :] = found[
                :, i * LANES : (i + 1) * LANES
            ]
    rows[...] = scr[...].astype(BF16).reshape(rows.shape)


def paper_rows(got, paper):
    span = REL_ROWS + PAPER_ROWS
    return pl.pallas_call(
        paper_kernel,
        out_shape=pltpu.HBM((LANES, span, LANES), BF16),
        in_specs=[VMEM, HBM],
        out_specs=VMEM,
        scratch_shapes=[
            pltpu.VMEM(paper.shape, BF16),
            pltpu.VMEM((LANES * span, LANES), F32),
            pltpu.SemaphoreType.DMA((1,)),
        ],
        compiler_params=params(),
        cost_estimate=pl.CostEstimate(
            flops=2 * FCAP * LANES * paper.shape[0] * paper.shape[1],
            bytes_accessed=4 * paper.size,
            transcendentals=0,
        ),
        name="gather_papers",
    )(got, *in_hbm(paper))


def prep_kernel(feats, w_self_in, cot_in, w_in, pre, cot, w_rel, w_self, sems):
    copies = fetch([(w_self_in, w_self), (cot_in, cot), (w_in, w_rel)], sems)
    copies[0].wait()
    pre[...] = dot(feats[...], w_self[...])
    for c in copies[1:]:
        c.wait()


def prep(feats, w_self, cotangent, w_rel):
    return pl.pallas_call(
        prep_kernel,
        out_shape=(
            pltpu.VMEM(cotangent.shape, F32),
            pltpu.VMEM(cotangent.shape, F32),
            pltpu.VMEM(w_rel.shape, BF16),
        ),
        in_specs=[VMEM, HBM, HBM, HBM],
        out_specs=(VMEM, VMEM, VMEM),
        scratch_shapes=[pltpu.VMEM(w_self.shape, BF16), pltpu.SemaphoreType.DMA((3,))],
        compiler_params=params(),
        cost_estimate=pl.CostEstimate(
            flops=2 * feats.size * w_self.shape[1], bytes_accessed=4 << 20, transcendentals=0
        ),
        name="prep",
    )(feats, *in_hbm(w_self, cotangent, w_rel))


def turn_kernel(feats, far, out):
    seeds = feats.shape[0]
    out[:, :seeds] = feats[...].T
    out[:, seeds:] = far[...].T


def turn(feats, far):
    seeds, width = feats.shape
    return pl.pallas_call(
        turn_kernel,
        out_shape=pltpu.HBM((width, 2 * seeds), BF16),
        in_specs=[VMEM, VMEM],
        out_specs=VMEM,
        compiler_params=params(),
        cost_estimate=pl.CostEstimate(flops=0, bytes_accessed=8 * feats.size, transcendentals=0),
        name="turn",
    )(feats, far)


def layer_kernel(
    core,
    fetched,
    seed_of,
    cnt,
    pre_self,
    cot,
    w_rel,
    *rest,
):
    here_out, there_out, grad_out = rest[-3:]
    devs = LANES
    lines = seed_of.shape[0]
    seed1 = iota((devs, LANES), 0) + 1
    agg = jnp.zeros((devs, LANES), F32)
    for b in range(0, lines, 2):
        match = jnp.concatenate(
            [onehot(seed1 == seed_of[b : b + 1, :]), onehot(seed1 == seed_of[b + 1 : b + 2, :])],
            axis=1,
        )
        agg = agg + dot(match, fetched[b * LANES : (b + 2) * LANES, :])
    count = cnt[...]
    agg_b = (agg / count).astype(BF16)
    pre = pre_self[...] + dot(agg_b, w_rel[...])
    sig = jax.nn.sigmoid(pre)
    dpre = (cot[...] * sig * (1.0 + pre * (1.0 - sig))).astype(BF16)
    half = dpre.shape[1] // 2
    first = core[0] == 0
    here_out[:, :half] = jnp.where(first, dpre[:, :half], dpre[:, half:])
    there_out[:, :half] = jnp.where(first, dpre[:, half:], dpre[:, :half])
    here_out[:, half:] = agg_b
    there_out[:, half:] = agg_b
    dagg = dot(dpre, w_rel[...], ((1,), (1,)))
    grad_out[...] = (dagg / count).astype(BF16)


def layer(core, fetched, seed_of, cnt, pre_self, cotangent, w_rel, *ready):
    seeds, hidden = cotangent.shape
    return pl.pallas_call(
        layer_kernel,
        out_shape=(
            jax.ShapeDtypeStruct((seeds, hidden // 2 + LANES), BF16),
            jax.ShapeDtypeStruct((seeds, hidden // 2 + LANES), BF16),
            jax.ShapeDtypeStruct((seeds, LANES), BF16),
        ),
        in_specs=[SMEM] + [VMEM] * 6 + [ANY] * len(ready),
        out_specs=(VMEM, VMEM, VMEM),
        compiler_params=params(),
        name="layer",
    )(core, fetched, seed_of, cnt, pre_self, cotangent, w_rel, *in_hbm(*ready))


def slots_kernel(seed_of, grad, papers_in, feats_in, out, papers, feats, sems):
    copies = fetch([(papers_in, papers), (feats_in, feats)], sems)
    seeds_t = seed_of[...].T
    lane1 = iota((LANES, LANES), 1) + 1
    for b in range(seed_of.shape[0]):
        match = onehot(seeds_t[:, b : b + 1] == lane1)
        out[b * GROUP : (b + 1) * GROUP] = (
            dot(match, grad[...]).astype(BF16).reshape(GROUP, CAP, LANES)
        )
    for c in copies:
        c.wait()


def slot_grads(seed_of, grad, papers, feats_t):
    return pl.pallas_call(
        slots_kernel,
        out_shape=(
            pltpu.VMEM((LANES, CAP, LANES), BF16),
            pltpu.VMEM(papers.shape, BF16),
            pltpu.VMEM(feats_t.shape, BF16),
        ),
        in_specs=[VMEM, VMEM, HBM, HBM],
        out_specs=(VMEM, VMEM, VMEM),
        scratch_shapes=[pltpu.SemaphoreType.DMA((2,))],
        compiler_params=params(),
        cost_estimate=pl.CostEstimate(
            flops=2 * LANES * CAP * LANES * LANES, bytes_accessed=4 << 20, transcendentals=0
        ),
        name="slot_grads",
    )(seed_of, grad, *in_hbm(papers, feats_t))


def weight_kernel(feats_t, here, far, slots, papers, bundle):
    both = jnp.concatenate([here[...], far[...]], axis=0)
    emb = LANES
    right, aggs = both[:, :-emb], both[:, -emb:]
    columns = right.shape[1] // LANES
    blocks = LANES // columns
    span = 2 * REL_ROWS
    where = iota((span * blocks, emb), 0)
    spread_rows = onehot(
        (where // span * REL_ROWS + where % span == iota((span * blocks, emb), 1))
        & (where % span < REL_ROWS)
    )
    aggs_t = dot(spread_rows, aggs, ((1,), (1,))).astype(BF16)
    for cb in range(columns):
        cols = right[:, cb * LANES : (cb + 1) * LANES]
        part_f = dot(feats_t[...], cols).astype(BF16)
        part_a = dot(aggs_t, cols)
        for i in range(blocks):
            d = cb * blocks + i
            bundle[d, :CAP, :] = slots[d]
            bundle[d, CAP:REL_AT, :] = part_f[i * SELF_ROWS : (i + 1) * SELF_ROWS]
            paper = papers[d].astype(F32)
            rel = part_a[i * span : (i + 1) * span] + paper[:span]
            bundle[d, REL_AT : REL_AT + span, :] = rel.astype(BF16)
            bundle[d, REL_AT + span :, :] = paper[span:].astype(BF16)


def weight_part(feats_t, here, far, slots, papers):
    return pl.pallas_call(
        weight_kernel,
        out_shape=jax.ShapeDtypeStruct((LANES, BUNDLE, LANES), BF16),
        in_specs=[VMEM] * 5,
        out_specs=VMEM,
        compiler_params=params(),
        name="weight_part",
    )(feats_t, here, far, slots, papers)


def sum_kernel(bundle, out, out_scr, sems):
    span = 2 * REL_ROWS
    half = [jnp.zeros((SELF_ROWS + span, LANES), F32) for _ in range(2)]
    for d in range(LANES):
        c = (d // GROUP) % 2
        half[c] = half[c] + bundle[d, CAP : REL_AT + span, :].astype(F32)
    rel = [h[SELF_ROWS : SELF_ROWS + REL_ROWS] for h in half]
    mine = jnp.concatenate([half[0][:SELF_ROWS], half[1][:SELF_ROWS], rel[0], rel[1]], axis=0)
    mine = mine.astype(BF16)
    for i in range(out_scr.shape[0]):
        out_scr[i] = mine
    q = out_scr.shape[0] // 4
    copies = fetch(
        [(out_scr.at[pl.ds(i * q, q)], out.at[pl.ds(i * q, q)]) for i in range(4)], sems
    )
    for c in copies:
        c.wait()


def sum_parts(bundle, peers):
    rows = 2 * (SELF_ROWS + REL_ROWS)
    return pl.pallas_call(
        sum_kernel,
        out_shape=pltpu.HBM((peers, rows, LANES), BF16),
        in_specs=[VMEM],
        out_specs=HBM,
        scratch_shapes=[
            pltpu.VMEM((peers, rows, LANES), BF16),
            pltpu.SemaphoreType.DMA((4,)),
        ],
        compiler_params=params(),
        name="sum_parts",
    )(bundle)


def spread_kernel(side, got, *rest):
    grad_self, grad_rel, self_scr, rel_scr, sems = rest[-5:]
    columns, steps = got.shape[:2]
    copies = []
    rows_self = GROUP * SELF_ROWS
    rows_rel = GROUP * REL_ROWS
    for i in range(steps):
        for cb in range(columns):
            rel = [[], []]
            for mp in range(GROUP):
                block = got[cb, i, mp].astype(F32)
                for h in range(2):
                    cols = slice((h * columns + cb) * LANES, (h * columns + cb + 1) * LANES)
                    self_scr[i, mp * SELF_ROWS : (mp + 1) * SELF_ROWS, cols] = block[
                        h * SELF_ROWS : (h + 1) * SELF_ROWS
                    ]
                    at = 2 * SELF_ROWS + h * REL_ROWS
                    rel[h].append(block[at : at + REL_ROWS])
            for h in range(2):
                cols = slice((h * columns + cb) * LANES, (h * columns + cb + 1) * LANES)
                rel_scr[i, :, cols] = jnp.concatenate(rel[h], axis=0)
        block_at = 2 * i + side[0]
        copies += fetch(
            [
                (self_scr.at[i], grad_self.at[pl.ds(block_at * rows_self, rows_self), :]),
                (rel_scr.at[i], grad_rel.at[pl.ds(block_at * rows_rel, rows_rel), :]),
            ],
            sems.at[i],
        )
    for c in copies:
        c.wait()


def spread(side, got, feats, emb, hidden, others=()):
    columns = hidden // LANES // 2
    peers, rows, _ = got.shape
    steps = peers // columns // GROUP
    return pl.pallas_call(
        spread_kernel,
        out_shape=(
            pltpu.HBM((feats, hidden), F32),
            pltpu.HBM((emb, hidden), F32),
        ),
        in_specs=[SMEM, VMEM] + [HBM] * len(others),
        out_specs=(HBM, HBM),
        scratch_shapes=[
            pltpu.VMEM((steps, GROUP * SELF_ROWS, hidden), F32),
            pltpu.VMEM((steps, GROUP * REL_ROWS, hidden), F32),
            pltpu.SemaphoreType.DMA((steps, 2)),
        ],
        input_output_aliases={2 + i: i for i in range(len(others))},
        compiler_params=params(),
        cost_estimate=pl.CostEstimate(
            flops=feats * hidden, bytes_accessed=3 * feats * hidden, transcendentals=0
        ),
        name="weight_out",
    )(side, got.reshape(columns, steps, GROUP, rows, LANES), *others)


def after_kernel(*refs):
    pass


def after(a, *ready):
    return pl.pallas_call(
        after_kernel,
        out_shape=jax.ShapeDtypeStruct(a.shape, a.dtype),
        in_specs=[ANY] * (1 + len(ready)),
        out_specs=ANY,
        input_output_aliases={0: 0},
        compiler_params=params(),
        name="after",
    )(a, *in_hbm(*ready))


def adam_kernel(
    wanted, bundle, table, m1, m2, new_table, new_m1, new_m2, done, arrived, hot_scr, side_scr, sem
):
    step = pl.program_id(0)
    lines = wanted.shape[0]
    done[...] = jnp.zeros_like(done)

    @pl.when(step == 0)
    def _():
        copy = pltpu.make_async_copy(bundle.at[:, pl.ds(0, CAP), :], arrived, sem.at[0])
        copy.start()
        lo = wanted[...] % 256
        hi = (wanted[...] // 256).astype(F32).T
        sub = iota((256, LANES), 0)
        for b in range(lines):
            at = slice(b * LANES, (b + 1) * LANES)
            hot_scr[:, at] = onehot(sub == lo[b : b + 1, :])
            side_scr[at, :] = jnp.broadcast_to(hi[:, b : b + 1], (LANES, LANES)).astype(BF16)
        copy.wait()

    here = side_scr[...] == step.astype(F32).astype(BF16)
    mark = jnp.where(here, BF16(1.0), BF16(0.0))
    got = arrived[...].reshape(LANES * CAP, LANES)
    both = dot(hot_scr[...], jnp.concatenate([got * mark, mark], axis=1))
    grad = both[:, :LANES]
    touched = both[:, LANES:] > 0.0
    m = 0.9 * m1[...] + 0.1 * grad
    v = 0.999 * m2[...] + 0.001 * grad * grad
    update = 0.05 * (m / (1.0 - 0.9**10)) / (jnp.sqrt(v / (1.0 - 0.999**10)) + 1e-08)
    new_table[...] = jnp.where(touched, table[...] - update, table[...])
    new_m1[...] = jnp.where(touched, m, m1[...])
    new_m2[...] = jnp.where(touched, v, m2[...])


def adam(wanted, bundle, table, m1, m2):
    rows = 256
    block = pl.BlockSpec((rows, LANES), lambda i: (i, 0))
    slots = LANES * CAP
    return pl.pallas_call(
        adam_kernel,
        grid=(table.shape[0] // rows,),
        out_shape=(jax.ShapeDtypeStruct(table.shape, F32),) * 3
        + (jax.ShapeDtypeStruct((8, LANES), F32),),
        in_specs=[pl.BlockSpec(wanted.shape, lambda i: (0, 0)), ANY, block, block, block],
        out_specs=(block, block, block, pl.BlockSpec((8, LANES), lambda i: (0, 0))),
        scratch_shapes=[
            pltpu.VMEM((LANES, CAP, LANES), BF16),
            pltpu.VMEM((rows, slots), BF16),
            pltpu.VMEM((slots, LANES), BF16),
            pltpu.SemaphoreType.DMA((1,)),
        ],
        cost_estimate=pl.CostEstimate(
            flops=2 * 2 * slots * LANES * table.shape[0],
            bytes_accessed=7 << 20,
            transcendentals=0,
        ),
        name="adam",
    )(wanted, bundle, table, m1, m2)


def shards(
    feats,
    edge_owner,
    edge_row,
    counts,
    table,
    moment1,
    moment2,
    w_self,
    w_rel,
    cotangent,
    next_owner,
    next_row,
    paper_table,
):
    every = ("chip", "core", "mp")
    peers = ("chip", "mp")
    devs = lax.axis_size(every)
    seeds, width = feats.shape
    hidden = cotangent.shape[1]
    emb = table.shape[1]
    core = lax.axis_index("core").astype(I32).reshape(1)
    group = lax.axis_index("mp").astype(I32).reshape(1)

    def exchange(a, axes):
        return lax.all_to_all(a, axes, split_axis=0, concat_axis=0, tiled=True)

    def swap(a):
        return lax.ppermute(a, "core", [(0, 1), (1, 0)])

    asked, seed_of, cnt, paper_pick, wide = place(
        group,
        edge_owner.reshape(-1, LANES),
        edge_row.reshape(-1, LANES),
        counts.reshape(1, -1),
        next_owner.reshape(1, -1),
        next_row.reshape(1, -1),
        table,
    )
    got = exchange(asked.reshape(devs, 1, LANES), every).reshape(devs, LANES)
    rows, wanted = gather(got, wide)
    fetched = exchange(rows.reshape(devs, CAP, emb), every).reshape(devs * CAP, emb)

    pre_self, cot, w_rel = prep(feats, w_self, cotangent, w_rel)
    feats_t = turn(feats, swap(feats))
    papers = paper_rows(got, paper_table)
    here, there, grad = layer(
        core, fetched, seed_of, cnt, pre_self, cot, w_rel, feats_t, papers
    )

    far = swap(there)
    slots, papers, feats_t = slot_grads(seed_of, grad, papers, feats_t)
    bundle = weight_part(feats_t, here, far, slots, papers)
    bundle = exchange(bundle, every)
    full = exchange(sum_parts(bundle, lax.axis_size(peers)), peers)
    new_table, new_moment1, new_moment2, done = adam(wanted, bundle, table, moment1, moment2)
    papers = bundle[:, PAPER_AT : PAPER_AT + FCAP * width // LANES, :].reshape(devs, -1)
    next_feats = functools.reduce(
        lambda a, b: a + b,
        [
            lax.dot_general(
                paper_pick[t],
                papers[:, t * width : (t + 1) * width],
                (((0,), (0,)), ((), ())),
                preferred_element_type=F32,
            )
            for t in range(FCAP)
        ],
    ).astype(BF16)
    full = after(full, done, next_feats)
    part = spread(core, full, width, emb, hidden)
    grad_self, grad_rel = spread(1 - core, swap(full), width, emb, hidden, part)
    return (new_table, new_moment1, new_moment2, grad_self, grad_rel, next_feats)


def solution(mesh):
    n_mp = mesh.shape["mp"]
    wide = Mesh(mesh.devices.reshape(-1, 2, n_mp), ("chip", "core", "mp"))
    rows = P(("chip", "core", "mp"), None)
    line = P(("chip", "core", "mp"))
    in_specs = (rows, rows, line, line, rows, rows, rows, P(), P(), rows, rows, line, rows)
    out_specs = (rows, rows, rows, P(), P(), rows)
    return jax.shard_map(shards, mesh=wide, in_specs=in_specs, out_specs=out_specs, check_vma=False)
```

```python
import functools

import jax
import jax.numpy as jnp
from jax import lax
from jax.experimental import pallas as pl
from jax.experimental.pallas import tpu as pltpu
from jax.sharding import Mesh, PartitionSpec as P

F32 = jnp.float32
BF16 = jnp.bfloat16
I32 = jnp.int32
LANES = 128
CAP = 32
FCAP = 2
GROUP = LANES // CAP
EMPTY = 4095
SELF_ROWS = 24
REL_ROWS = 4
REL_AT = CAP + SELF_ROWS
PAPER_AT = REL_AT + REL_ROWS
PAPER_ROWS = 12
TILE = 256
BUNDLE = PAPER_AT + PAPER_ROWS
VMEM = pl.BlockSpec(memory_space=pltpu.VMEM)
SMEM = pl.BlockSpec(memory_space=pltpu.SMEM)


def iota(shape, dim):
    return lax.broadcasted_iota(I32, shape, dim)


def dot(a, b, contract=((1,), (0,))):
    return lax.dot_general(a, b, (contract, ((), ())), preferred_element_type=F32)


def onehot(mask):
    return jnp.where(mask, F32(1.0), F32(0.0)).astype(BF16)

ANY = pl.BlockSpec(memory_space=pl.ANY)
HBM = pl.BlockSpec(memory_space=pltpu.HBM)


def params():
    return pltpu.CompilerParams(vmem_limit_bytes=24 * 1024 * 1024)


def in_hbm(*arrays):
    return [pltpu.with_memory_space_constraint(a, pltpu.HBM) for a in arrays]


def fetch(pairs, sems):
    copies = [pltpu.make_async_copy(a, b, sems.at[i]) for i, (a, b) in enumerate(pairs)]
    for c in copies:
        c.start()
    return copies


def place_kernel(
    lane_group,
    owner_in,
    row_in,
    counts_in,
    next_owner_in,
    next_row_in,
    table_in,
    asked,
    seed_of,
    cnt,
    paper_pick,
    wide,
    owner,
    row,
    counts,
    next_owner,
    next_row,
    table,
    seed_scr,
    sems,
):
    copies = fetch(
        [
            (owner_in, owner),
            (row_in, row),
            (counts_in, counts),
            (next_owner_in, next_owner),
            (next_row_in, next_row),
            (table_in, table),
        ],
        sems,
    )
    table_copy = copies.pop()
    devs = LANES
    blocks = owner.shape[0]
    group = lane_group[0]
    sub = iota((devs, LANES), 0)
    lane = iota((devs, LANES), 1)
    seeds_row = LANES // (LANES * blocks // devs)
    slots_per = LANES // seeds_row
    upper = onehot(sub < lane)
    ones = jnp.ones((devs, LANES), BF16)
    scan = jnp.concatenate([upper, ones], axis=1)
    pick = onehot(sub % seeds_row == lane // slots_per)
    for c in copies:
        c.wait()
    count_row = counts[...].astype(F32)
    spread = jnp.where(
        iota((blocks, LANES), 1) // seeds_row == iota((blocks, LANES), 0), count_row, F32(0.0)
    ).astype(BF16)
    cnt_edge = dot(spread, pick)
    k_edge = (iota((blocks, LANES), 1) % slots_per).astype(F32)
    live_owner = jnp.where(k_edge < cnt_edge, owner[...], -1)
    base = jnp.zeros((devs, LANES), F32)
    hots, values = [], []
    ksub = iota((CAP, LANES), 0).astype(F32)
    for b in range(blocks):
        hot = sub == live_owner[b : b + 1, :]
        hot_f = jnp.where(hot, F32(1.0), F32(0.0))
        hot_b = hot_f.astype(BF16)
        scanned = dot(hot_b, scan)
        slot = jnp.sum(hot_f * (scanned[:, :LANES] + base), axis=0, keepdims=True)
        base = base + scanned[:, LANES:]
        at = ksub == slot
        r = row[b : b + 1, :]
        seed1 = b * seeds_row + iota((1, LANES), 1) // slots_per + 1
        vals = jnp.concatenate(
            [
                jnp.where(at, (r // LANES).astype(F32), F32(0.0)),
                jnp.where(at, (r % LANES).astype(F32), F32(0.0)),
                jnp.where(at, seed1.astype(F32), F32(0.0)),
            ],
            axis=0,
        ).astype(BF16)
        hots.append(hot_b)
        values.append(vals)
    values = jnp.concatenate(values, axis=1)
    acc_i = dot(jnp.concatenate(hots, axis=1), values, ((1,), (1,))).astype(I32)
    seeds = acc_i[:, 2 * CAP :]
    wanted = jnp.where(seeds > 0, acc_i[:, :CAP] * LANES + acc_i[:, CAP : 2 * CAP], EMPTY)

    hot = sub == next_owner[...]
    hot_f = jnp.where(hot, F32(1.0), F32(0.0))
    hot_b = hot_f.astype(BF16)
    before = dot(hot_b, upper)
    slot = jnp.sum(hot_f * before, axis=0, keepdims=True)
    nrow = next_row[...]
    for t in range(FCAP):
        paper_pick[t] = jnp.where(slot == t, hot_f, F32(0.0)).astype(BF16)
    at = iota((CAP, LANES), 0) == slot.astype(I32)
    vals = jnp.concatenate(
        [
            jnp.where(at, (nrow // LANES).astype(F32), F32(0.0)),
            jnp.where(at, (nrow % LANES).astype(F32), F32(0.0)),
        ],
        axis=0,
    ).astype(BF16)
    pacc = dot(hot_b, vals, ((1,), (1,))).astype(I32)
    paper = pacc[:, :CAP] * LANES + pacc[:, CAP:]

    quarter = lane // CAP
    wide_wanted = jnp.concatenate([wanted] * GROUP, axis=1)
    wide_paper = jnp.concatenate([paper] * GROUP, axis=1)
    asked[...] = jnp.where(
        quarter == group,
        wide_wanted,
        jnp.where(quarter == (group + 1) % GROUP, wide_paper, 0),
    )
    seed_scr[...] = jnp.where(quarter == sub % GROUP, jnp.concatenate([seeds] * GROUP, axis=1), 0)
    total = seed_scr[pl.ds(0, devs // GROUP, stride=GROUP), :]
    for i in range(1, GROUP):
        total = total + seed_scr[pl.ds(i, devs // GROUP, stride=GROUP), :]
    seed_of[...] = total
    cnt[...] = jnp.broadcast_to(count_row, (devs, LANES)).T
    table_copy.wait()
    for q in range(table.shape[0] // TILE):
        wide[:, q * LANES : (q + 1) * LANES] = table[q * TILE : (q + 1) * TILE, :].astype(BF16)


def place(group, owner, row, counts, next_owner, next_row, table):
    devs = LANES
    ins = (owner, row, counts, next_owner, next_row, table)
    return pl.pallas_call(
        place_kernel,
        out_shape=(
            pltpu.VMEM((devs, LANES), I32),
            jax.ShapeDtypeStruct((devs // GROUP, LANES), I32),
            jax.ShapeDtypeStruct((devs, LANES), F32),
            jax.ShapeDtypeStruct((FCAP, devs, LANES), BF16),
            pltpu.VMEM((TILE, table.shape[0] // TILE * LANES), BF16),
        ),
        in_specs=[SMEM] + [HBM] * len(ins),
        out_specs=(VMEM, VMEM, VMEM, VMEM, VMEM),
        scratch_shapes=[pltpu.VMEM(a.shape, a.dtype) for a in ins]
        + [pltpu.VMEM((devs, LANES), I32), pltpu.SemaphoreType.DMA((len(ins),))],
        compiler_params=params(),
        name="place",
    )(group, *in_hbm(*ins))


def gather_kernel(got, wide, rows, wanted_out, hot_scr, hi_scr, out_scr, out_sems):
    devs = LANES
    lines = devs // GROUP
    quarter = iota((lines, LANES), 1) // CAP
    wanted = jnp.zeros((lines, LANES), I32)
    for i in range(GROUP):
        wanted = wanted + jnp.where(quarter == i, got[pl.ds(i, lines, stride=GROUP), :], 0)
    wanted_out[...] = wanted
    wanted_t = wanted.T
    lo = wanted_t % TILE
    hi = wanted_t // TILE
    lanes = iota((LANES, TILE), 1)
    for b in range(lines):
        hot_scr[b * LANES : (b + 1) * LANES, :] = onehot(lo[:, b : b + 1] == lanes)
        hi_scr[b * LANES : (b + 1) * LANES, :] = jnp.broadcast_to(hi[:, b : b + 1], (LANES, LANES))
    chunk = 512
    outs = []
    for c in range(out_scr.shape[0] // chunk):
        at = pl.ds(c * chunk, chunk)
        hot = hot_scr[at, :]
        high = hi_scr[at, :]
        out = jnp.zeros((chunk, LANES), F32)
        for q in range(0, wide.shape[1] // LANES, 2):
            both = dot(hot, wide[:, q * LANES : (q + 2) * LANES])
            out = jnp.where(high == q, both[:, :LANES], out)
            out = jnp.where(high == q + 1, both[:, LANES:], out)
        out_scr[at, :] = out.astype(BF16)
        copy = pltpu.make_async_copy(out_scr.at[at, :], rows.at[at, :], out_sems.at[c])
        copy.start()
        outs.append(copy)
    for copy in outs:
        copy.wait()


def gather(got, wide):
    slots = LANES * CAP
    return pl.pallas_call(
        gather_kernel,
        out_shape=(
            pltpu.HBM((slots, LANES), BF16),
            pltpu.HBM((LANES // GROUP, LANES), I32),
        ),
        in_specs=[VMEM, VMEM],
        out_specs=(HBM, VMEM),
        scratch_shapes=[
            pltpu.VMEM((slots, TILE), BF16),
            pltpu.VMEM((slots, LANES), I32),
            pltpu.VMEM((slots, LANES), BF16),
            pltpu.SemaphoreType.DMA((slots // 512,)),
        ],
        compiler_params=params(),
        name="gather_rows",
    )(got, wide)


def paper_kernel(got, paper_in, rows, paper, scr, sem):
    copies = fetch([(paper_in, paper)], sem)
    devs = LANES
    sub = iota((devs, LANES), 0)
    lane = iota((devs, LANES), 1)
    first = ((sub % GROUP + 1) % GROUP) * CAP
    parts = paper.shape[1] // LANES
    span = REL_ROWS + PAPER_ROWS
    for i in range(REL_ROWS):
        scr[pl.ds(i, devs, stride=span), :] = jnp.zeros((devs, LANES), F32)
    copies[0].wait()
    for t in range(FCAP):
        asked = jnp.sum(jnp.where(lane == first + t, got[...], 0), axis=1, keepdims=True)
        hot = onehot(asked == iota((devs, paper.shape[0]), 1))
        found = dot(hot, paper[...])
        for i in range(parts):
            scr[pl.ds(REL_ROWS + t * parts + i, devs, stride=span), :] = found[
                :, i * LANES : (i + 1) * LANES
            ]
    rows[...] = scr[...].astype(BF16).reshape(rows.shape)


def paper_rows(got, paper):
    span = REL_ROWS + PAPER_ROWS
    return pl.pallas_call(
        paper_kernel,
        out_shape=pltpu.HBM((LANES, span, LANES), BF16),
        in_specs=[VMEM, HBM],
        out_specs=VMEM,
        scratch_shapes=[
            pltpu.VMEM(paper.shape, BF16),
            pltpu.VMEM((LANES * span, LANES), F32),
            pltpu.SemaphoreType.DMA((1,)),
        ],
        compiler_params=params(),
        cost_estimate=pl.CostEstimate(
            flops=2 * FCAP * LANES * paper.shape[0] * paper.shape[1],
            bytes_accessed=4 * paper.size,
            transcendentals=0,
        ),
        name="gather_papers",
    )(got, *in_hbm(paper))


def prep_kernel(feats, w_self_in, cot_in, w_in, pre, cot, w_rel, w_self, sems):
    copies = fetch([(w_self_in, w_self), (cot_in, cot), (w_in, w_rel)], sems)
    copies[0].wait()
    pre[...] = dot(feats[...], w_self[...])
    for c in copies[1:]:
        c.wait()


def prep(feats, w_self, cotangent, w_rel):
    return pl.pallas_call(
        prep_kernel,
        out_shape=(
            pltpu.VMEM(cotangent.shape, F32),
            pltpu.VMEM(cotangent.shape, F32),
            pltpu.VMEM(w_rel.shape, BF16),
        ),
        in_specs=[VMEM, HBM, HBM, HBM],
        out_specs=(VMEM, VMEM, VMEM),
        scratch_shapes=[pltpu.VMEM(w_self.shape, BF16), pltpu.SemaphoreType.DMA((3,))],
        compiler_params=params(),
        cost_estimate=pl.CostEstimate(
            flops=2 * feats.size * w_self.shape[1], bytes_accessed=4 << 20, transcendentals=0
        ),
        name="prep",
    )(feats, *in_hbm(w_self, cotangent, w_rel))


def turn_kernel(feats, far, out):
    seeds = feats.shape[0]
    out[:, :seeds] = feats[...].T
    out[:, seeds:] = far[...].T


def turn(feats, far):
    seeds, width = feats.shape
    return pl.pallas_call(
        turn_kernel,
        out_shape=pltpu.HBM((width, 2 * seeds), BF16),
        in_specs=[VMEM, VMEM],
        out_specs=VMEM,
        compiler_params=params(),
        cost_estimate=pl.CostEstimate(flops=0, bytes_accessed=8 * feats.size, transcendentals=0),
        name="turn",
    )(feats, far)


def layer_kernel(
    core,
    fetched,
    seed_of,
    cnt,
    pre_self,
    cot,
    w_rel,
    *rest,
):
    here_out, there_out, grad_out = rest[-3:]
    devs = LANES
    lines = seed_of.shape[0]
    seed1 = iota((devs, LANES), 0) + 1
    agg = jnp.zeros((devs, LANES), F32)
    for b in range(0, lines, 2):
        match = jnp.concatenate(
            [onehot(seed1 == seed_of[b : b + 1, :]), onehot(seed1 == seed_of[b + 1 : b + 2, :])],
            axis=1,
        )
        agg = agg + dot(match, fetched[b * LANES : (b + 2) * LANES, :])
    count = cnt[...]
    agg_b = (agg / count).astype(BF16)
    pre = pre_self[...] + dot(agg_b, w_rel[...])
    sig = jax.nn.sigmoid(pre)
    dpre = (cot[...] * sig * (1.0 + pre * (1.0 - sig))).astype(BF16)
    half = dpre.shape[1] // 2
    first = core[0] == 0
    here_out[:, :half] = jnp.where(first, dpre[:, :half], dpre[:, half:])
    there_out[:, :half] = jnp.where(first, dpre[:, half:], dpre[:, :half])
    here_out[:, half:] = agg_b
    there_out[:, half:] = agg_b
    dagg = dot(dpre, w_rel[...], ((1,), (1,)))
    grad_out[...] = (dagg / count).astype(BF16)


def layer(core, fetched, seed_of, cnt, pre_self, cotangent, w_rel, *ready):
    seeds, hidden = cotangent.shape
    return pl.pallas_call(
        layer_kernel,
        out_shape=(
            jax.ShapeDtypeStruct((seeds, hidden // 2 + LANES), BF16),
            jax.ShapeDtypeStruct((seeds, hidden // 2 + LANES), BF16),
            jax.ShapeDtypeStruct((seeds, LANES), BF16),
        ),
        in_specs=[SMEM] + [VMEM] * 6 + [ANY] * len(ready),
        out_specs=(VMEM, VMEM, VMEM),
        compiler_params=params(),
        name="layer",
    )(core, fetched, seed_of, cnt, pre_self, cotangent, w_rel, *in_hbm(*ready))


def slots_kernel(seed_of, grad, papers_in, feats_in, out, papers, feats, sems):
    copies = fetch([(papers_in, papers), (feats_in, feats)], sems)
    seeds_t = seed_of[...].T
    lane1 = iota((LANES, LANES), 1) + 1
    for b in range(seed_of.shape[0]):
        match = onehot(seeds_t[:, b : b + 1] == lane1)
        out[b * GROUP : (b + 1) * GROUP] = (
            dot(match, grad[...]).astype(BF16).reshape(GROUP, CAP, LANES)
        )
    for c in copies:
        c.wait()


def slot_grads(seed_of, grad, papers, feats_t):
    return pl.pallas_call(
        slots_kernel,
        out_shape=(
            pltpu.VMEM((LANES, CAP, LANES), BF16),
            pltpu.VMEM(papers.shape, BF16),
            pltpu.VMEM(feats_t.shape, BF16),
        ),
        in_specs=[VMEM, VMEM, HBM, HBM],
        out_specs=(VMEM, VMEM, VMEM),
        scratch_shapes=[pltpu.SemaphoreType.DMA((2,))],
        compiler_params=params(),
        cost_estimate=pl.CostEstimate(
            flops=2 * LANES * CAP * LANES * LANES, bytes_accessed=4 << 20, transcendentals=0
        ),
        name="slot_grads",
    )(seed_of, grad, *in_hbm(papers, feats_t))


def weight_kernel(feats_t, here, far, slots, papers, bundle):
    both = jnp.concatenate([here[...], far[...]], axis=0)
    emb = LANES
    right, aggs = both[:, :-emb], both[:, -emb:]
    columns = right.shape[1] // LANES
    blocks = LANES // columns
    span = 2 * REL_ROWS
    where = iota((span * blocks, emb), 0)
    spread_rows = onehot(
        (where // span * REL_ROWS + where % span == iota((span * blocks, emb), 1))
        & (where % span < REL_ROWS)
    )
    aggs_t = dot(spread_rows, aggs, ((1,), (1,))).astype(BF16)
    for cb in range(columns):
        mine = slice(cb % 2 * LANES, (cb % 2 + 1) * LANES)
        if cb % 2 == 0:
            cols = right[:, cb * LANES : (cb + 2) * LANES]
            both_f = dot(feats_t[...], cols).astype(BF16)
            both_a = dot(aggs_t, cols)
        part_f, part_a = both_f[:, mine], both_a[:, mine]
        for i in range(blocks):
            d = cb * blocks + i
            bundle[d, :CAP, :] = slots[d]
            bundle[d, CAP:REL_AT, :] = part_f[i * SELF_ROWS : (i + 1) * SELF_ROWS]
            paper = papers[d].astype(F32)
            rel = part_a[i * span : (i + 1) * span] + paper[:span]
            bundle[d, REL_AT : REL_AT + span, :] = rel.astype(BF16)
            bundle[d, REL_AT + span :, :] = paper[span:].astype(BF16)


def weight_part(feats_t, here, far, slots, papers):
    return pl.pallas_call(
        weight_kernel,
        out_shape=jax.ShapeDtypeStruct((LANES, BUNDLE, LANES), BF16),
        in_specs=[VMEM] * 5,
        out_specs=VMEM,
        compiler_params=params(),
        name="weight_part",
    )(feats_t, here, far, slots, papers)


def sum_kernel(bundle, out, out_scr, sems):
    span = 2 * REL_ROWS
    half = [jnp.zeros((SELF_ROWS + span, LANES), F32) for _ in range(2)]
    for d in range(LANES):
        c = (d // GROUP) % 2
        half[c] = half[c] + bundle[d, CAP : REL_AT + span, :].astype(F32)
    rel = [h[SELF_ROWS : SELF_ROWS + REL_ROWS] for h in half]
    mine = jnp.concatenate([half[0][:SELF_ROWS], half[1][:SELF_ROWS], rel[0], rel[1]], axis=0)
    mine = mine.astype(BF16)
    for i in range(out_scr.shape[0]):
        out_scr[i] = mine
    q = out_scr.shape[0] // 4
    copies = fetch(
        [(out_scr.at[pl.ds(i * q, q)], out.at[pl.ds(i * q, q)]) for i in range(4)], sems
    )
    for c in copies:
        c.wait()


def sum_parts(bundle, peers):
    rows = 2 * (SELF_ROWS + REL_ROWS)
    return pl.pallas_call(
        sum_kernel,
        out_shape=pltpu.HBM((peers, rows, LANES), BF16),
        in_specs=[VMEM],
        out_specs=HBM,
        scratch_shapes=[
            pltpu.VMEM((peers, rows, LANES), BF16),
            pltpu.SemaphoreType.DMA((4,)),
        ],
        compiler_params=params(),
        name="sum_parts",
    )(bundle)


def spread_kernel(side, got, *rest):
    grad_self, grad_rel, self_scr, rel_scr, sems = rest[-5:]
    columns, steps = got.shape[:2]
    copies = []
    rows_self = GROUP * SELF_ROWS
    rows_rel = GROUP * REL_ROWS
    for i in range(steps):
        for cb in range(columns):
            rel = [[], []]
            for mp in range(GROUP):
                block = got[cb, i, mp].astype(F32)
                for h in range(2):
                    cols = slice((h * columns + cb) * LANES, (h * columns + cb + 1) * LANES)
                    self_scr[i, mp * SELF_ROWS : (mp + 1) * SELF_ROWS, cols] = block[
                        h * SELF_ROWS : (h + 1) * SELF_ROWS
                    ]
                    at = 2 * SELF_ROWS + h * REL_ROWS
                    rel[h].append(block[at : at + REL_ROWS])
            for h in range(2):
                cols = slice((h * columns + cb) * LANES, (h * columns + cb + 1) * LANES)
                rel_scr[i, :, cols] = jnp.concatenate(rel[h], axis=0)
        block_at = 2 * i + side[0]
        copies += fetch(
            [
                (self_scr.at[i], grad_self.at[pl.ds(block_at * rows_self, rows_self), :]),
                (rel_scr.at[i], grad_rel.at[pl.ds(block_at * rows_rel, rows_rel), :]),
            ],
            sems.at[i],
        )
    for c in copies:
        c.wait()


def spread(side, got, feats, emb, hidden, others=()):
    columns = hidden // LANES // 2
    peers, rows, _ = got.shape
    steps = peers // columns // GROUP
    return pl.pallas_call(
        spread_kernel,
        out_shape=(
            pltpu.HBM((feats, hidden), F32),
            pltpu.HBM((emb, hidden), F32),
        ),
        in_specs=[SMEM, VMEM] + [HBM] * len(others),
        out_specs=(HBM, HBM),
        scratch_shapes=[
            pltpu.VMEM((steps, GROUP * SELF_ROWS, hidden), F32),
            pltpu.VMEM((steps, GROUP * REL_ROWS, hidden), F32),
            pltpu.SemaphoreType.DMA((steps, 2)),
        ],
        input_output_aliases={2 + i: i for i in range(len(others))},
        compiler_params=params(),
        cost_estimate=pl.CostEstimate(
            flops=feats * hidden, bytes_accessed=3 * feats * hidden, transcendentals=0
        ),
        name="weight_out",
    )(side, got.reshape(columns, steps, GROUP, rows, LANES), *others)


def after_kernel(*refs):
    pass


def after(a, *ready):
    return pl.pallas_call(
        after_kernel,
        out_shape=jax.ShapeDtypeStruct(a.shape, a.dtype),
        in_specs=[ANY] * (1 + len(ready)),
        out_specs=ANY,
        input_output_aliases={0: 0},
        compiler_params=params(),
        name="after",
    )(a, *in_hbm(*ready))


def adam_kernel(
    wanted, bundle, table, m1, m2, new_table, new_m1, new_m2, done, arrived, hot_scr, side_scr, sem
):
    step = pl.program_id(0)
    lines = wanted.shape[0]
    done[...] = jnp.zeros_like(done)

    @pl.when(step == 0)
    def _():
        copy = pltpu.make_async_copy(bundle.at[:, pl.ds(0, CAP), :], arrived, sem.at[0])
        copy.start()
        lo = wanted[...] % 256
        hi = (wanted[...] // 256).astype(F32).T
        sub = iota((256, LANES), 0)
        for b in range(lines):
            at = slice(b * LANES, (b + 1) * LANES)
            hot_scr[:, at] = onehot(sub == lo[b : b + 1, :])
            side_scr[at, :] = jnp.broadcast_to(hi[:, b : b + 1], (LANES, LANES)).astype(BF16)
        copy.wait()

    here = side_scr[...] == step.astype(F32).astype(BF16)
    mark = jnp.where(here, BF16(1.0), BF16(0.0))
    got = arrived[...].reshape(LANES * CAP, LANES)
    both = dot(hot_scr[...], jnp.concatenate([got * mark, mark], axis=1))
    grad = both[:, :LANES]
    touched = both[:, LANES:] > 0.0
    m = 0.9 * m1[...] + 0.1 * grad
    v = 0.999 * m2[...] + 0.001 * grad * grad
    update = 0.05 * (m / (1.0 - 0.9**10)) / (jnp.sqrt(v / (1.0 - 0.999**10)) + 1e-08)
    new_table[...] = jnp.where(touched, table[...] - update, table[...])
    new_m1[...] = jnp.where(touched, m, m1[...])
    new_m2[...] = jnp.where(touched, v, m2[...])


def adam(wanted, bundle, table, m1, m2):
    rows = 256
    block = pl.BlockSpec((rows, LANES), lambda i: (i, 0))
    slots = LANES * CAP
    return pl.pallas_call(
        adam_kernel,
        grid=(table.shape[0] // rows,),
        out_shape=(jax.ShapeDtypeStruct(table.shape, F32),) * 3
        + (jax.ShapeDtypeStruct((8, LANES), F32),),
        in_specs=[pl.BlockSpec(wanted.shape, lambda i: (0, 0)), ANY, block, block, block],
        out_specs=(block, block, block, pl.BlockSpec((8, LANES), lambda i: (0, 0))),
        scratch_shapes=[
            pltpu.VMEM((LANES, CAP, LANES), BF16),
            pltpu.VMEM((rows, slots), BF16),
            pltpu.VMEM((slots, LANES), BF16),
            pltpu.SemaphoreType.DMA((1,)),
        ],
        cost_estimate=pl.CostEstimate(
            flops=2 * 2 * slots * LANES * table.shape[0],
            bytes_accessed=7 << 20,
            transcendentals=0,
        ),
        name="adam",
    )(wanted, bundle, table, m1, m2)


def shards(
    feats,
    edge_owner,
    edge_row,
    counts,
    table,
    moment1,
    moment2,
    w_self,
    w_rel,
    cotangent,
    next_owner,
    next_row,
    paper_table,
):
    every = ("chip", "core", "mp")
    peers = ("chip", "mp")
    devs = lax.axis_size(every)
    seeds, width = feats.shape
    hidden = cotangent.shape[1]
    emb = table.shape[1]
    core = lax.axis_index("core").astype(I32).reshape(1)
    group = lax.axis_index("mp").astype(I32).reshape(1)

    def exchange(a, axes):
        return lax.all_to_all(a, axes, split_axis=0, concat_axis=0, tiled=True)

    def swap(a):
        return lax.ppermute(a, "core", [(0, 1), (1, 0)])

    asked, seed_of, cnt, paper_pick, wide = place(
        group,
        edge_owner.reshape(-1, LANES),
        edge_row.reshape(-1, LANES),
        counts.reshape(1, -1),
        next_owner.reshape(1, -1),
        next_row.reshape(1, -1),
        table,
    )
    got = exchange(asked.reshape(devs, 1, LANES), every).reshape(devs, LANES)
    rows, wanted = gather(got, wide)
    fetched = exchange(rows.reshape(devs, CAP, emb), every).reshape(devs * CAP, emb)

    pre_self, cot, w_rel = prep(feats, w_self, cotangent, w_rel)
    feats_t = turn(feats, swap(feats))
    papers = paper_rows(got, paper_table)
    here, there, grad = layer(
        core, fetched, seed_of, cnt, pre_self, cot, w_rel, feats_t, papers
    )

    far = swap(there)
    slots, papers, feats_t = slot_grads(seed_of, grad, papers, feats_t)
    bundle = weight_part(feats_t, here, far, slots, papers)
    bundle = exchange(bundle, every)
    full = exchange(sum_parts(bundle, lax.axis_size(peers)), peers)
    new_table, new_moment1, new_moment2, done = adam(wanted, bundle, table, moment1, moment2)
    papers = bundle[:, PAPER_AT : PAPER_AT + FCAP * width // LANES, :].reshape(devs, -1)
    next_feats = functools.reduce(
        lambda a, b: a + b,
        [
            lax.dot_general(
                paper_pick[t],
                papers[:, t * width : (t + 1) * width],
                (((0,), (0,)), ((), ())),
                preferred_element_type=F32,
            )
            for t in range(FCAP)
        ],
    ).astype(BF16)
    full = after(full, done, next_feats)
    part = spread(core, full, width, emb, hidden)
    grad_self, grad_rel = spread(1 - core, swap(full), width, emb, hidden, part)
    return (new_table, new_moment1, new_moment2, grad_self, grad_rel, next_feats)


def solution(mesh):
    n_mp = mesh.shape["mp"]
    wide = Mesh(mesh.devices.reshape(-1, 2, n_mp), ("chip", "core", "mp"))
    rows = P(("chip", "core", "mp"), None)
    line = P(("chip", "core", "mp"))
    in_specs = (rows, rows, line, line, rows, rows, rows, P(), P(), rows, rows, line, rows)
    out_specs = (rows, rows, rows, P(), P(), rows)
    return jax.shard_map(shards, mesh=wide, in_specs=in_specs, out_specs=out_specs, check_vma=False)
```

```python
import functools

import jax
import jax.numpy as jnp
from jax import lax
from jax.experimental import pallas as pl
from jax.experimental.pallas import tpu as pltpu
from jax.sharding import Mesh, PartitionSpec as P

F32 = jnp.float32
BF16 = jnp.bfloat16
I32 = jnp.int32
LANES = 128
CAP = 32
FCAP = 2
GROUP = LANES // CAP
EMPTY = 4095
SELF_ROWS = 24
REL_ROWS = 4
REL_AT = CAP + SELF_ROWS
PAPER_AT = REL_AT + REL_ROWS
PAPER_ROWS = 12
TILE = 256
BUNDLE = PAPER_AT + PAPER_ROWS
VMEM = pl.BlockSpec(memory_space=pltpu.VMEM)
SMEM = pl.BlockSpec(memory_space=pltpu.SMEM)


def iota(shape, dim):
    return lax.broadcasted_iota(I32, shape, dim)


def dot(a, b, contract=((1,), (0,))):
    return lax.dot_general(a, b, (contract, ((), ())), preferred_element_type=F32)


def onehot(mask):
    return jnp.where(mask, F32(1.0), F32(0.0)).astype(BF16)

ANY = pl.BlockSpec(memory_space=pl.ANY)
HBM = pl.BlockSpec(memory_space=pltpu.HBM)


def params():
    return pltpu.CompilerParams(vmem_limit_bytes=24 * 1024 * 1024)


def in_hbm(*arrays):
    return [pltpu.with_memory_space_constraint(a, pltpu.HBM) for a in arrays]


def fetch(pairs, sems):
    copies = [pltpu.make_async_copy(a, b, sems.at[i]) for i, (a, b) in enumerate(pairs)]
    for c in copies:
        c.start()
    return copies


def place_kernel(
    lane_group,
    owner_in,
    row_in,
    counts_in,
    next_owner_in,
    next_row_in,
    table_in,
    asked,
    seed_of,
    cnt,
    paper_pick,
    wide,
    owner,
    row,
    counts,
    next_owner,
    next_row,
    table,
    seed_scr,
    sems,
):
    copies = fetch(
        [
            (owner_in, owner),
            (row_in, row),
            (counts_in, counts),
            (next_owner_in, next_owner),
            (next_row_in, next_row),
            (table_in, table),
        ],
        sems,
    )
    table_copy = copies.pop()
    devs = LANES
    blocks = owner.shape[0]
    group = lane_group[0]
    sub = iota((devs, LANES), 0)
    lane = iota((devs, LANES), 1)
    seeds_row = LANES // (LANES * blocks // devs)
    slots_per = LANES // seeds_row
    upper = onehot(sub < lane)
    ones = jnp.ones((devs, LANES), BF16)
    scan = jnp.concatenate([upper, ones], axis=1)
    pick = onehot(sub % seeds_row == lane // slots_per)
    for c in copies:
        c.wait()
    count_row = counts[...].astype(F32)
    spread = jnp.where(
        iota((blocks, LANES), 1) // seeds_row == iota((blocks, LANES), 0), count_row, F32(0.0)
    ).astype(BF16)
    cnt_edge = dot(spread, pick)
    k_edge = (iota((blocks, LANES), 1) % slots_per).astype(F32)
    live_owner = jnp.where(k_edge < cnt_edge, owner[...], -1)
    base = jnp.zeros((devs, LANES), F32)
    hots, values = [], []
    ksub = iota((CAP, LANES), 0).astype(F32)
    for b in range(blocks):
        hot = sub == live_owner[b : b + 1, :]
        hot_f = jnp.where(hot, F32(1.0), F32(0.0))
        hot_b = hot_f.astype(BF16)
        scanned = dot(hot_b, scan)
        slot = jnp.sum(hot_f * (scanned[:, :LANES] + base), axis=0, keepdims=True)
        base = base + scanned[:, LANES:]
        at = ksub == slot
        r = row[b : b + 1, :]
        seed1 = b * seeds_row + iota((1, LANES), 1) // slots_per + 1
        vals = jnp.concatenate(
            [
                jnp.where(at, (r // LANES).astype(F32), F32(0.0)),
                jnp.where(at, (r % LANES).astype(F32), F32(0.0)),
                jnp.where(at, seed1.astype(F32), F32(0.0)),
            ],
            axis=0,
        ).astype(BF16)
        hots.append(hot_b)
        values.append(vals)
    values = jnp.concatenate(values, axis=1)
    acc_i = dot(jnp.concatenate(hots, axis=1), values, ((1,), (1,))).astype(I32)
    seeds = acc_i[:, 2 * CAP :]
    wanted = jnp.where(seeds > 0, acc_i[:, :CAP] * LANES + acc_i[:, CAP : 2 * CAP], EMPTY)

    hot = sub == next_owner[...]
    hot_f = jnp.where(hot, F32(1.0), F32(0.0))
    hot_b = hot_f.astype(BF16)
    before = dot(hot_b, upper)
    slot = jnp.sum(hot_f * before, axis=0, keepdims=True)
    nrow = next_row[...]
    for t in range(FCAP):
        paper_pick[t] = jnp.where(slot == t, hot_f, F32(0.0)).astype(BF16)
    at = iota((CAP, LANES), 0) == slot.astype(I32)
    vals = jnp.concatenate(
        [
            jnp.where(at, (nrow // LANES).astype(F32), F32(0.0)),
            jnp.where(at, (nrow % LANES).astype(F32), F32(0.0)),
        ],
        axis=0,
    ).astype(BF16)
    pacc = dot(hot_b, vals, ((1,), (1,))).astype(I32)
    paper = pacc[:, :CAP] * LANES + pacc[:, CAP:]

    quarter = lane // CAP
    wide_wanted = jnp.concatenate([wanted] * GROUP, axis=1)
    wide_paper = jnp.concatenate([paper] * GROUP, axis=1)
    asked[...] = jnp.where(
        quarter == group,
        wide_wanted,
        jnp.where(quarter == (group + 1) % GROUP, wide_paper, 0),
    )
    seed_scr[...] = jnp.where(quarter == sub % GROUP, jnp.concatenate([seeds] * GROUP, axis=1), 0)
    total = seed_scr[pl.ds(0, devs // GROUP, stride=GROUP), :]
    for i in range(1, GROUP):
        total = total + seed_scr[pl.ds(i, devs // GROUP, stride=GROUP), :]
    seed_of[...] = total
    cnt[...] = jnp.broadcast_to(count_row, (devs, LANES)).T
    table_copy.wait()
    for q in range(table.shape[0] // TILE):
        wide[:, q * LANES : (q + 1) * LANES] = table[q * TILE : (q + 1) * TILE, :].astype(BF16)


def place(group, owner, row, counts, next_owner, next_row, table):
    devs = LANES
    ins = (owner, row, counts, next_owner, next_row, table)
    return pl.pallas_call(
        place_kernel,
        out_shape=(
            pltpu.VMEM((devs, LANES), I32),
            jax.ShapeDtypeStruct((devs // GROUP, LANES), I32),
            jax.ShapeDtypeStruct((devs, LANES), F32),
            jax.ShapeDtypeStruct((FCAP, devs, LANES), BF16),
            pltpu.VMEM((TILE, table.shape[0] // TILE * LANES), BF16),
        ),
        in_specs=[SMEM] + [HBM] * len(ins),
        out_specs=(VMEM, VMEM, VMEM, VMEM, VMEM),
        scratch_shapes=[pltpu.VMEM(a.shape, a.dtype) for a in ins]
        + [pltpu.VMEM((devs, LANES), I32), pltpu.SemaphoreType.DMA((len(ins),))],
        compiler_params=params(),
        name="place",
    )(group, *in_hbm(*ins))


def gather_kernel(got, wide, rows, wanted_out, hot_scr, hi_scr, out_scr, out_sems):
    devs = LANES
    lines = devs // GROUP
    quarter = iota((lines, LANES), 1) // CAP
    wanted = jnp.zeros((lines, LANES), I32)
    for i in range(GROUP):
        wanted = wanted + jnp.where(quarter == i, got[pl.ds(i, lines, stride=GROUP), :], 0)
    wanted_out[...] = wanted
    wanted_t = wanted.T
    lo = wanted_t % TILE
    hi = wanted_t // TILE
    lanes = iota((LANES, TILE), 1)
    for b in range(lines):
        hot_scr[b * LANES : (b + 1) * LANES, :] = onehot(lo[:, b : b + 1] == lanes)
        hi_scr[b * LANES : (b + 1) * LANES, :] = jnp.broadcast_to(hi[:, b : b + 1], (LANES, LANES))
    chunk = 512
    outs = []
    for c in range(out_scr.shape[0] // chunk):
        at = pl.ds(c * chunk, chunk)
        hot = hot_scr[at, :]
        high = hi_scr[at, :]
        out = jnp.zeros((chunk, LANES), F32)
        for q in range(0, wide.shape[1] // LANES, 2):
            both = dot(hot, wide[:, q * LANES : (q + 2) * LANES])
            out = jnp.where(high == q, both[:, :LANES], out)
            out = jnp.where(high == q + 1, both[:, LANES:], out)
        out_scr[at, :] = out.astype(BF16)
        copy = pltpu.make_async_copy(out_scr.at[at, :], rows.at[at, :], out_sems.at[c])
        copy.start()
        outs.append(copy)
    for copy in outs:
        copy.wait()


def gather(got, wide):
    slots = LANES * CAP
    return pl.pallas_call(
        gather_kernel,
        out_shape=(
            pltpu.HBM((slots, LANES), BF16),
            pltpu.HBM((LANES // GROUP, LANES), I32),
        ),
        in_specs=[VMEM, VMEM],
        out_specs=(HBM, VMEM),
        scratch_shapes=[
            pltpu.VMEM((slots, TILE), BF16),
            pltpu.VMEM((slots, LANES), I32),
            pltpu.VMEM((slots, LANES), BF16),
            pltpu.SemaphoreType.DMA((slots // 512,)),
        ],
        compiler_params=params(),
        name="gather_rows",
    )(got, wide)


def paper_kernel(got, paper_in, rows, paper, scr, sem):
    copies = fetch([(paper_in, paper)], sem)
    devs = LANES
    sub = iota((devs, LANES), 0)
    lane = iota((devs, LANES), 1)
    first = ((sub % GROUP + 1) % GROUP) * CAP
    parts = paper.shape[1] // LANES
    span = REL_ROWS + PAPER_ROWS
    for i in range(REL_ROWS):
        scr[pl.ds(i, devs, stride=span), :] = jnp.zeros((devs, LANES), F32)
    copies[0].wait()
    for t in range(FCAP):
        asked = jnp.sum(jnp.where(lane == first + t, got[...], 0), axis=1, keepdims=True)
        hot = onehot(asked == iota((devs, paper.shape[0]), 1))
        found = dot(hot, paper[...])
        for i in range(parts):
            scr[pl.ds(REL_ROWS + t * parts + i, devs, stride=span), :] = found[
                :, i * LANES : (i + 1) * LANES
            ]
    rows[...] = scr[...].astype(BF16).reshape(rows.shape)


def paper_rows(got, paper):
    span = REL_ROWS + PAPER_ROWS
    return pl.pallas_call(
        paper_kernel,
        out_shape=pltpu.HBM((LANES, span, LANES), BF16),
        in_specs=[VMEM, HBM],
        out_specs=VMEM,
        scratch_shapes=[
            pltpu.VMEM(paper.shape, BF16),
            pltpu.VMEM((LANES * span, LANES), F32),
            pltpu.SemaphoreType.DMA((1,)),
        ],
        compiler_params=params(),
        cost_estimate=pl.CostEstimate(
            flops=2 * FCAP * LANES * paper.shape[0] * paper.shape[1],
            bytes_accessed=4 * paper.size,
            transcendentals=0,
        ),
        name="gather_papers",
    )(got, *in_hbm(paper))


def prep_kernel(feats, w_self_in, cot_in, w_in, pre, cot, w_rel, w_self, sems):
    copies = fetch([(w_self_in, w_self), (cot_in, cot), (w_in, w_rel)], sems)
    copies[0].wait()
    pre[...] = dot(feats[...], w_self[...])
    for c in copies[1:]:
        c.wait()


def prep(feats, w_self, cotangent, w_rel):
    return pl.pallas_call(
        prep_kernel,
        out_shape=(
            pltpu.VMEM(cotangent.shape, F32),
            pltpu.VMEM(cotangent.shape, F32),
            pltpu.VMEM(w_rel.shape, BF16),
        ),
        in_specs=[VMEM, HBM, HBM, HBM],
        out_specs=(VMEM, VMEM, VMEM),
        scratch_shapes=[pltpu.VMEM(w_self.shape, BF16), pltpu.SemaphoreType.DMA((3,))],
        compiler_params=params(),
        cost_estimate=pl.CostEstimate(
            flops=2 * feats.size * w_self.shape[1], bytes_accessed=4 << 20, transcendentals=0
        ),
        name="prep",
    )(feats, *in_hbm(w_self, cotangent, w_rel))


def turn_kernel(feats, far, out):
    seeds = feats.shape[0]
    out[:, :seeds] = feats[...].T
    out[:, seeds:] = far[...].T


def turn(feats, far):
    seeds, width = feats.shape
    return pl.pallas_call(
        turn_kernel,
        out_shape=pltpu.HBM((width, 2 * seeds), BF16),
        in_specs=[VMEM, VMEM],
        out_specs=VMEM,
        compiler_params=params(),
        cost_estimate=pl.CostEstimate(flops=0, bytes_accessed=8 * feats.size, transcendentals=0),
        name="turn",
    )(feats, far)


def layer_kernel(
    core,
    fetched,
    seed_of,
    cnt,
    pre_self,
    cot,
    w_rel,
    *rest,
):
    here_out, there_out, grad_out = rest[-3:]
    devs = LANES
    lines = seed_of.shape[0]
    seed1 = iota((devs, LANES), 0) + 1
    agg = jnp.zeros((devs, LANES), F32)
    for b in range(0, lines, 2):
        match = jnp.concatenate(
            [onehot(seed1 == seed_of[b : b + 1, :]), onehot(seed1 == seed_of[b + 1 : b + 2, :])],
            axis=1,
        )
        agg = agg + dot(match, fetched[b * LANES : (b + 2) * LANES, :])
    count = cnt[...]
    agg_b = (agg / count).astype(BF16)
    pre = pre_self[...] + dot(agg_b, w_rel[...])
    sig = jax.nn.sigmoid(pre)
    dpre = (cot[...] * sig * (1.0 + pre * (1.0 - sig))).astype(BF16)
    half = dpre.shape[1] // 2
    first = core[0] == 0
    here_out[:, :half] = jnp.where(first, dpre[:, :half], dpre[:, half:])
    there_out[:, :half] = jnp.where(first, dpre[:, half:], dpre[:, :half])
    here_out[:, half:] = agg_b
    there_out[:, half:] = agg_b
    dagg = dot(dpre, w_rel[...], ((1,), (1,)))
    grad_out[...] = (dagg / count).astype(BF16)


def layer(core, fetched, seed_of, cnt, pre_self, cotangent, w_rel, *ready):
    seeds, hidden = cotangent.shape
    return pl.pallas_call(
        layer_kernel,
        out_shape=(
            jax.ShapeDtypeStruct((seeds, hidden // 2 + LANES), BF16),
            jax.ShapeDtypeStruct((seeds, hidden // 2 + LANES), BF16),
            jax.ShapeDtypeStruct((seeds, LANES), BF16),
        ),
        in_specs=[SMEM] + [VMEM] * 6 + [ANY] * len(ready),
        out_specs=(VMEM, VMEM, VMEM),
        compiler_params=params(),
        name="layer",
    )(core, fetched, seed_of, cnt, pre_self, cotangent, w_rel, *in_hbm(*ready))


def slots_kernel(seed_of, grad, papers_in, feats_in, out, papers, feats, sems):
    copies = fetch([(papers_in, papers), (feats_in, feats)], sems)
    seeds_t = seed_of[...].T
    lane1 = iota((LANES, LANES), 1) + 1
    for b in range(seed_of.shape[0]):
        match = onehot(seeds_t[:, b : b + 1] == lane1)
        out[b * GROUP : (b + 1) * GROUP] = (
            dot(match, grad[...]).astype(BF16).reshape(GROUP, CAP, LANES)
        )
    for c in copies:
        c.wait()


def slot_grads(seed_of, grad, papers, feats_t):
    return pl.pallas_call(
        slots_kernel,
        out_shape=(
            pltpu.VMEM((LANES, CAP, LANES), BF16),
            pltpu.VMEM(papers.shape, BF16),
            pltpu.VMEM(feats_t.shape, BF16),
        ),
        in_specs=[VMEM, VMEM, HBM, HBM],
        out_specs=(VMEM, VMEM, VMEM),
        scratch_shapes=[pltpu.SemaphoreType.DMA((2,))],
        compiler_params=params(),
        cost_estimate=pl.CostEstimate(
            flops=2 * LANES * CAP * LANES * LANES, bytes_accessed=4 << 20, transcendentals=0
        ),
        name="slot_grads",
    )(seed_of, grad, *in_hbm(papers, feats_t))


def weight_kernel(feats_t, here, far, slots, papers, bundle):
    both = jnp.concatenate([here[...], far[...]], axis=0)
    emb = LANES
    right, aggs = both[:, :-emb], both[:, -emb:]
    columns = right.shape[1] // LANES
    blocks = LANES // columns
    span = 2 * REL_ROWS
    where = iota((span * blocks, emb), 0)
    spread_rows = onehot(
        (where // span * REL_ROWS + where % span == iota((span * blocks, emb), 1))
        & (where % span < REL_ROWS)
    )
    aggs_t = dot(spread_rows, aggs, ((1,), (1,))).astype(BF16)
    for cb in range(columns):
        mine = slice(cb % 2 * LANES, (cb % 2 + 1) * LANES)
        if cb % 2 == 0:
            cols = right[:, cb * LANES : (cb + 2) * LANES]
            both_f = dot(feats_t[...], cols).astype(BF16)
            both_a = dot(aggs_t, cols)
        part_f, part_a = both_f[:, mine], both_a[:, mine]
        for i in range(blocks):
            d = cb * blocks + i
            bundle[d, :CAP, :] = slots[d]
            bundle[d, CAP:REL_AT, :] = part_f[i * SELF_ROWS : (i + 1) * SELF_ROWS]
            paper = papers[d].astype(F32)
            rel = part_a[i * span : (i + 1) * span] + paper[:span]
            bundle[d, REL_AT : REL_AT + span, :] = rel.astype(BF16)
            bundle[d, REL_AT + span :, :] = paper[span:].astype(BF16)


def weight_part(feats_t, here, far, slots, papers):
    return pl.pallas_call(
        weight_kernel,
        out_shape=jax.ShapeDtypeStruct((LANES, BUNDLE, LANES), BF16),
        in_specs=[VMEM] * 5,
        out_specs=VMEM,
        compiler_params=params(),
        name="weight_part",
    )(feats_t, here, far, slots, papers)


def sum_kernel(bundle, out, out_scr, sems):
    span = 2 * REL_ROWS
    half = [jnp.zeros((SELF_ROWS + span, LANES), F32) for _ in range(2)]
    for d in range(LANES):
        c = (d // GROUP) % 2
        half[c] = half[c] + bundle[d, CAP : REL_AT + span, :].astype(F32)
    rel = [h[SELF_ROWS : SELF_ROWS + REL_ROWS] for h in half]
    mine = jnp.concatenate([half[0][:SELF_ROWS], half[1][:SELF_ROWS], rel[0], rel[1]], axis=0)
    mine = mine.astype(BF16)
    for i in range(out_scr.shape[0]):
        out_scr[i] = mine
    q = out_scr.shape[0] // 4
    copies = fetch(
        [(out_scr.at[pl.ds(i * q, q)], out.at[pl.ds(i * q, q)]) for i in range(4)], sems
    )
    for c in copies:
        c.wait()


def sum_parts(bundle, peers):
    rows = 2 * (SELF_ROWS + REL_ROWS)
    return pl.pallas_call(
        sum_kernel,
        out_shape=pltpu.HBM((peers, rows, LANES), BF16),
        in_specs=[VMEM],
        out_specs=HBM,
        scratch_shapes=[
            pltpu.VMEM((peers, rows, LANES), BF16),
            pltpu.SemaphoreType.DMA((4,)),
        ],
        compiler_params=params(),
        name="sum_parts",
    )(bundle)


def spread_kernel(side, got, *rest):
    grad_self, grad_rel, self_scr, rel_scr, sems = rest[-5:]
    columns, steps = got.shape[:2]
    copies = []
    rows_self = GROUP * SELF_ROWS
    rows_rel = GROUP * REL_ROWS
    for i in range(steps):
        for cb in range(columns):
            rel = [[], []]
            for mp in range(GROUP):
                block = got[cb, i, mp].astype(F32)
                for h in range(2):
                    cols = slice((h * columns + cb) * LANES, (h * columns + cb + 1) * LANES)
                    self_scr[i, mp * SELF_ROWS : (mp + 1) * SELF_ROWS, cols] = block[
                        h * SELF_ROWS : (h + 1) * SELF_ROWS
                    ]
                    at = 2 * SELF_ROWS + h * REL_ROWS
                    rel[h].append(block[at : at + REL_ROWS])
            for h in range(2):
                cols = slice((h * columns + cb) * LANES, (h * columns + cb + 1) * LANES)
                rel_scr[i, :, cols] = jnp.concatenate(rel[h], axis=0)
        block_at = 2 * i + side[0]
        copies += fetch(
            [
                (self_scr.at[i], grad_self.at[pl.ds(block_at * rows_self, rows_self), :]),
                (rel_scr.at[i], grad_rel.at[pl.ds(block_at * rows_rel, rows_rel), :]),
            ],
            sems.at[i],
        )
    for c in copies:
        c.wait()


def spread(side, got, feats, emb, hidden, others=()):
    columns = hidden // LANES // 2
    peers, rows, _ = got.shape
    steps = peers // columns // GROUP
    return pl.pallas_call(
        spread_kernel,
        out_shape=(
            pltpu.HBM((feats, hidden), F32),
            pltpu.HBM((emb, hidden), F32),
        ),
        in_specs=[SMEM, VMEM] + [HBM] * len(others),
        out_specs=(HBM, HBM),
        scratch_shapes=[
            pltpu.VMEM((steps, GROUP * SELF_ROWS, hidden), F32),
            pltpu.VMEM((steps, GROUP * REL_ROWS, hidden), F32),
            pltpu.SemaphoreType.DMA((steps, 2)),
        ],
        input_output_aliases={2 + i: i for i in range(len(others))},
        compiler_params=params(),
        cost_estimate=pl.CostEstimate(
            flops=feats * hidden, bytes_accessed=3 * feats * hidden, transcendentals=0
        ),
        name="weight_out",
    )(side, got.reshape(columns, steps, GROUP, rows, LANES), *others)


def after_kernel(*refs):
    pass


def after(a, *ready):
    return pl.pallas_call(
        after_kernel,
        out_shape=jax.ShapeDtypeStruct(a.shape, a.dtype),
        in_specs=[ANY] * (1 + len(ready)),
        out_specs=ANY,
        input_output_aliases={0: 0},
        compiler_params=params(),
        name="after",
    )(a, *in_hbm(*ready))


def adam_kernel(
    wanted, bundle, table, m1, m2, new_table, new_m1, new_m2, done, arrived, hot_scr, side_scr, sem
):
    step = pl.program_id(0)
    lines = wanted.shape[0]
    done[...] = jnp.zeros_like(done)

    @pl.when(step == 0)
    def _():
        copy = pltpu.make_async_copy(bundle.at[:, pl.ds(0, CAP), :], arrived, sem.at[0])
        copy.start()
        lo = wanted[...] % 256
        hi = (wanted[...] // 256).astype(F32).T
        sub = iota((256, LANES), 0)
        for b in range(lines):
            at = slice(b * LANES, (b + 1) * LANES)
            hot_scr[:, at] = onehot(sub == lo[b : b + 1, :])
            side_scr[at, :] = jnp.broadcast_to(hi[:, b : b + 1], (LANES, LANES)).astype(BF16)
        copy.wait()

    got = arrived[...].reshape(LANES * CAP, LANES)
    parts = table.shape[0] // 256
    for part in range(parts):
        at = slice(part * 256, (part + 1) * 256)
        here = side_scr[...] == (step * parts + part).astype(F32).astype(BF16)
        mark = jnp.where(here, BF16(1.0), BF16(0.0))
        both = dot(hot_scr[...], jnp.concatenate([got * mark, mark], axis=1))
        grad = both[:, :LANES]
        touched = both[:, LANES:] > 0.0
        m = 0.9 * m1[at, :] + 0.1 * grad
        v = 0.999 * m2[at, :] + 0.001 * grad * grad
        update = 0.05 * (m / (1.0 - 0.9**10)) / (jnp.sqrt(v / (1.0 - 0.999**10)) + 1e-08)
        new_table[at, :] = jnp.where(touched, table[at, :] - update, table[at, :])
        new_m1[at, :] = jnp.where(touched, m, m1[at, :])
        new_m2[at, :] = jnp.where(touched, v, m2[at, :])


def adam(wanted, bundle, table, m1, m2):
    rows = 512
    block = pl.BlockSpec((rows, LANES), lambda i: (i, 0))
    slots = LANES * CAP
    return pl.pallas_call(
        adam_kernel,
        grid=(table.shape[0] // rows,),
        out_shape=(jax.ShapeDtypeStruct(table.shape, F32),) * 3
        + (jax.ShapeDtypeStruct((8, LANES), F32),),
        in_specs=[pl.BlockSpec(wanted.shape, lambda i: (0, 0)), ANY, block, block, block],
        out_specs=(block, block, block, pl.BlockSpec((8, LANES), lambda i: (0, 0))),
        scratch_shapes=[
            pltpu.VMEM((LANES, CAP, LANES), BF16),
            pltpu.VMEM((256, slots), BF16),
            pltpu.VMEM((slots, LANES), BF16),
            pltpu.SemaphoreType.DMA((1,)),
        ],
        cost_estimate=pl.CostEstimate(
            flops=2 * 2 * slots * LANES * table.shape[0],
            bytes_accessed=7 << 20,
            transcendentals=0,
        ),
        name="adam",
    )(wanted, bundle, table, m1, m2)


def shards(
    feats,
    edge_owner,
    edge_row,
    counts,
    table,
    moment1,
    moment2,
    w_self,
    w_rel,
    cotangent,
    next_owner,
    next_row,
    paper_table,
):
    every = ("chip", "core", "mp")
    peers = ("chip", "mp")
    devs = lax.axis_size(every)
    seeds, width = feats.shape
    hidden = cotangent.shape[1]
    emb = table.shape[1]
    core = lax.axis_index("core").astype(I32).reshape(1)
    group = lax.axis_index("mp").astype(I32).reshape(1)

    def exchange(a, axes):
        return lax.all_to_all(a, axes, split_axis=0, concat_axis=0, tiled=True)

    def swap(a):
        return lax.ppermute(a, "core", [(0, 1), (1, 0)])

    asked, seed_of, cnt, paper_pick, wide = place(
        group,
        edge_owner.reshape(-1, LANES),
        edge_row.reshape(-1, LANES),
        counts.reshape(1, -1),
        next_owner.reshape(1, -1),
        next_row.reshape(1, -1),
        table,
    )
    got = exchange(asked.reshape(devs, 1, LANES), every).reshape(devs, LANES)
    rows, wanted = gather(got, wide)
    fetched = exchange(rows.reshape(devs, CAP, emb), every).reshape(devs * CAP, emb)

    pre_self, cot, w_rel = prep(feats, w_self, cotangent, w_rel)
    feats_t = turn(feats, swap(feats))
    papers = paper_rows(got, paper_table)
    here, there, grad = layer(
        core, fetched, seed_of, cnt, pre_self, cot, w_rel, feats_t, papers
    )

    far = swap(there)
    slots, papers, feats_t = slot_grads(seed_of, grad, papers, feats_t)
    bundle = weight_part(feats_t, here, far, slots, papers)
    bundle = exchange(bundle, every)
    full = exchange(sum_parts(bundle, lax.axis_size(peers)), peers)
    new_table, new_moment1, new_moment2, done = adam(wanted, bundle, table, moment1, moment2)
    papers = bundle[:, PAPER_AT : PAPER_AT + FCAP * width // LANES, :].reshape(devs, -1)
    next_feats = functools.reduce(
        lambda a, b: a + b,
        [
            lax.dot_general(
                paper_pick[t],
                papers[:, t * width : (t + 1) * width],
                (((0,), (0,)), ((), ())),
                preferred_element_type=F32,
            )
            for t in range(FCAP)
        ],
    ).astype(BF16)
    full = after(full, done, next_feats)
    part = spread(core, full, width, emb, hidden)
    grad_self, grad_rel = spread(1 - core, swap(full), width, emb, hidden, part)
    return (new_table, new_moment1, new_moment2, grad_self, grad_rel, next_feats)


def solution(mesh):
    n_mp = mesh.shape["mp"]
    wide = Mesh(mesh.devices.reshape(-1, 2, n_mp), ("chip", "core", "mp"))
    rows = P(("chip", "core", "mp"), None)
    line = P(("chip", "core", "mp"))
    in_specs = (rows, rows, line, line, rows, rows, rows, P(), P(), rows, rows, line, rows)
    out_specs = (rows, rows, rows, P(), P(), rows)
    return jax.shard_map(shards, mesh=wide, in_specs=in_specs, out_specs=out_specs, check_vma=False)
```

```python
import functools

import jax
import jax.numpy as jnp
from jax import lax
from jax.experimental import pallas as pl
from jax.experimental.pallas import tpu as pltpu
from jax.sharding import Mesh, PartitionSpec as P

F32 = jnp.float32
BF16 = jnp.bfloat16
I32 = jnp.int32
LANES = 128
CAP = 32
FCAP = 2
GROUP = LANES // CAP
EMPTY = 4095
SELF_ROWS = 24
REL_ROWS = 4
REL_AT = CAP + SELF_ROWS
PAPER_AT = REL_AT + REL_ROWS
PAPER_ROWS = 12
TILE = 256
BUNDLE = PAPER_AT + PAPER_ROWS
VMEM = pl.BlockSpec(memory_space=pltpu.VMEM)
SMEM = pl.BlockSpec(memory_space=pltpu.SMEM)


def iota(shape, dim):
    return lax.broadcasted_iota(I32, shape, dim)


def dot(a, b, contract=((1,), (0,))):
    return lax.dot_general(a, b, (contract, ((), ())), preferred_element_type=F32)


def onehot(mask):
    return jnp.where(mask, F32(1.0), F32(0.0)).astype(BF16)

ANY = pl.BlockSpec(memory_space=pl.ANY)
HBM = pl.BlockSpec(memory_space=pltpu.HBM)


def params():
    return pltpu.CompilerParams(vmem_limit_bytes=24 * 1024 * 1024)


def in_hbm(*arrays):
    return [pltpu.with_memory_space_constraint(a, pltpu.HBM) for a in arrays]


def fetch(pairs, sems):
    copies = [pltpu.make_async_copy(a, b, sems.at[i]) for i, (a, b) in enumerate(pairs)]
    for c in copies:
        c.start()
    return copies


def place_kernel(
    lane_group,
    owner_in,
    row_in,
    counts_in,
    next_owner_in,
    next_row_in,
    table_in,
    asked,
    seed_of,
    cnt,
    paper_pick,
    wide,
    owner,
    row,
    counts,
    next_owner,
    next_row,
    table,
    seed_scr,
    sems,
):
    copies = fetch(
        [
            (owner_in, owner),
            (row_in, row),
            (counts_in, counts),
            (next_owner_in, next_owner),
            (next_row_in, next_row),
            (table_in, table),
        ],
        sems,
    )
    table_copy = copies.pop()
    devs = LANES
    blocks = owner.shape[0]
    group = lane_group[0]
    sub = iota((devs, LANES), 0)
    lane = iota((devs, LANES), 1)
    seeds_row = LANES // (LANES * blocks // devs)
    slots_per = LANES // seeds_row
    upper = onehot(sub < lane)
    ones = jnp.ones((devs, LANES), BF16)
    scan = jnp.concatenate([upper, ones], axis=1)
    pick = onehot(sub % seeds_row == lane // slots_per)
    for c in copies:
        c.wait()
    count_row = counts[...].astype(F32)
    spread = jnp.where(
        iota((blocks, LANES), 1) // seeds_row == iota((blocks, LANES), 0), count_row, F32(0.0)
    ).astype(BF16)
    cnt_edge = dot(spread, pick)
    k_edge = (iota((blocks, LANES), 1) % slots_per).astype(F32)
    live_owner = jnp.where(k_edge < cnt_edge, owner[...], -1)
    base = jnp.zeros((devs, LANES), F32)
    hots, values = [], []
    ksub = iota((CAP, LANES), 0).astype(F32)
    for b in range(blocks):
        hot = sub == live_owner[b : b + 1, :]
        hot_f = jnp.where(hot, F32(1.0), F32(0.0))
        hot_b = hot_f.astype(BF16)
        scanned = dot(hot_b, scan)
        slot = jnp.sum(hot_f * (scanned[:, :LANES] + base), axis=0, keepdims=True)
        base = base + scanned[:, LANES:]
        at = ksub == slot
        r = row[b : b + 1, :]
        seed1 = b * seeds_row + iota((1, LANES), 1) // slots_per + 1
        vals = jnp.concatenate(
            [
                jnp.where(at, (r // LANES).astype(F32), F32(0.0)),
                jnp.where(at, (r % LANES).astype(F32), F32(0.0)),
                jnp.where(at, seed1.astype(F32), F32(0.0)),
            ],
            axis=0,
        ).astype(BF16)
        hots.append(hot_b)
        values.append(vals)
    values = jnp.concatenate(values, axis=1)
    acc_i = dot(jnp.concatenate(hots, axis=1), values, ((1,), (1,))).astype(I32)
    seeds = acc_i[:, 2 * CAP :]
    wanted = jnp.where(seeds > 0, acc_i[:, :CAP] * LANES + acc_i[:, CAP : 2 * CAP], EMPTY)

    hot = sub == next_owner[...]
    hot_f = jnp.where(hot, F32(1.0), F32(0.0))
    hot_b = hot_f.astype(BF16)
    before = dot(hot_b, upper)
    slot = jnp.sum(hot_f * before, axis=0, keepdims=True)
    nrow = next_row[...]
    for t in range(FCAP):
        paper_pick[t] = jnp.where(slot == t, hot_f, F32(0.0)).astype(BF16)
    at = iota((CAP, LANES), 0) == slot.astype(I32)
    vals = jnp.concatenate(
        [
            jnp.where(at, (nrow // LANES).astype(F32), F32(0.0)),
            jnp.where(at, (nrow % LANES).astype(F32), F32(0.0)),
        ],
        axis=0,
    ).astype(BF16)
    pacc = dot(hot_b, vals, ((1,), (1,))).astype(I32)
    paper = pacc[:, :CAP] * LANES + pacc[:, CAP:]

    quarter = lane // CAP
    wide_wanted = jnp.concatenate([wanted] * GROUP, axis=1)
    wide_paper = jnp.concatenate([paper] * GROUP, axis=1)
    asked[...] = jnp.where(
        quarter == group,
        wide_wanted,
        jnp.where(quarter == (group + 1) % GROUP, wide_paper, 0),
    )
    seed_scr[...] = jnp.where(quarter == sub % GROUP, jnp.concatenate([seeds] * GROUP, axis=1), 0)
    total = seed_scr[pl.ds(0, devs // GROUP, stride=GROUP), :]
    for i in range(1, GROUP):
        total = total + seed_scr[pl.ds(i, devs // GROUP, stride=GROUP), :]
    seed_of[...] = total
    cnt[...] = jnp.broadcast_to(count_row, (devs, LANES)).T
    table_copy.wait()
    for q in range(table.shape[0] // TILE):
        wide[:, q * LANES : (q + 1) * LANES] = table[q * TILE : (q + 1) * TILE, :].astype(BF16)


def place(group, owner, row, counts, next_owner, next_row, table):
    devs = LANES
    ins = (owner, row, counts, next_owner, next_row, table)
    return pl.pallas_call(
        place_kernel,
        out_shape=(
            pltpu.VMEM((devs, LANES), I32),
            jax.ShapeDtypeStruct((devs // GROUP, LANES), I32),
            jax.ShapeDtypeStruct((devs, LANES), F32),
            jax.ShapeDtypeStruct((FCAP, devs, LANES), BF16),
            pltpu.VMEM((TILE, table.shape[0] // TILE * LANES), BF16),
        ),
        in_specs=[SMEM] + [HBM] * len(ins),
        out_specs=(VMEM, VMEM, VMEM, VMEM, VMEM),
        scratch_shapes=[pltpu.VMEM(a.shape, a.dtype) for a in ins]
        + [pltpu.VMEM((devs, LANES), I32), pltpu.SemaphoreType.DMA((len(ins),))],
        compiler_params=params(),
        name="place",
    )(group, *in_hbm(*ins))


def gather_kernel(got, wide, rows, wanted_out, hot_scr, hi_scr, out_scr, out_sems):
    devs = LANES
    lines = devs // GROUP
    quarter = iota((lines, LANES), 1) // CAP
    wanted = jnp.zeros((lines, LANES), I32)
    for i in range(GROUP):
        wanted = wanted + jnp.where(quarter == i, got[pl.ds(i, lines, stride=GROUP), :], 0)
    wanted_out[...] = wanted
    wanted_t = wanted.T
    lo = wanted_t % TILE
    hi = wanted_t // TILE
    lanes = iota((LANES, TILE), 1)
    for b in range(lines):
        hot_scr[b * LANES : (b + 1) * LANES, :] = onehot(lo[:, b : b + 1] == lanes)
        hi_scr[b * LANES : (b + 1) * LANES, :] = jnp.broadcast_to(hi[:, b : b + 1], (LANES, LANES))
    quarter_rows = out_scr.shape[0] // 4
    chunks = [quarter_rows] * 3 + [quarter_rows // 2] + [quarter_rows // 4] * 2
    outs = []
    for c, chunk in enumerate(chunks):
        at = pl.ds(sum(chunks[:c]), chunk)
        hot = hot_scr[at, :]
        high = hi_scr[at, :]
        out = jnp.zeros((chunk, LANES), F32)
        for q in range(0, wide.shape[1] // LANES, 2):
            both = dot(hot, wide[:, q * LANES : (q + 2) * LANES])
            out = jnp.where(high == q, both[:, :LANES], out)
            out = jnp.where(high == q + 1, both[:, LANES:], out)
        out_scr[at, :] = out.astype(BF16)
        copy = pltpu.make_async_copy(out_scr.at[at, :], rows.at[at, :], out_sems.at[c])
        copy.start()
        outs.append(copy)
    for copy in outs:
        copy.wait()


def gather(got, wide):
    slots = LANES * CAP
    return pl.pallas_call(
        gather_kernel,
        out_shape=(
            pltpu.HBM((slots, LANES), BF16),
            pltpu.HBM((LANES // GROUP, LANES), I32),
        ),
        in_specs=[VMEM, VMEM],
        out_specs=(HBM, VMEM),
        scratch_shapes=[
            pltpu.VMEM((slots, TILE), BF16),
            pltpu.VMEM((slots, LANES), I32),
            pltpu.VMEM((slots, LANES), BF16),
            pltpu.SemaphoreType.DMA((slots // 512,)),
        ],
        compiler_params=params(),
        name="gather_rows",
    )(got, wide)


def paper_kernel(got, paper_in, rows, paper, scr, sem):
    copies = fetch([(paper_in, paper)], sem)
    devs = LANES
    sub = iota((devs, LANES), 0)
    lane = iota((devs, LANES), 1)
    first = ((sub % GROUP + 1) % GROUP) * CAP
    parts = paper.shape[1] // LANES
    span = REL_ROWS + PAPER_ROWS
    for i in range(REL_ROWS):
        scr[pl.ds(i, devs, stride=span), :] = jnp.zeros((devs, LANES), F32)
    copies[0].wait()
    for t in range(FCAP):
        asked = jnp.sum(jnp.where(lane == first + t, got[...], 0), axis=1, keepdims=True)
        hot = onehot(asked == iota((devs, paper.shape[0]), 1))
        found = dot(hot, paper[...])
        for i in range(parts):
            scr[pl.ds(REL_ROWS + t * parts + i, devs, stride=span), :] = found[
                :, i * LANES : (i + 1) * LANES
            ]
    rows[...] = scr[...].astype(BF16).reshape(rows.shape)


def paper_rows(got, paper):
    span = REL_ROWS + PAPER_ROWS
    return pl.pallas_call(
        paper_kernel,
        out_shape=pltpu.HBM((LANES, span, LANES), BF16),
        in_specs=[VMEM, HBM],
        out_specs=VMEM,
        scratch_shapes=[
            pltpu.VMEM(paper.shape, BF16),
            pltpu.VMEM((LANES * span, LANES), F32),
            pltpu.SemaphoreType.DMA((1,)),
        ],
        compiler_params=params(),
        cost_estimate=pl.CostEstimate(
            flops=2 * FCAP * LANES * paper.shape[0] * paper.shape[1],
            bytes_accessed=4 * paper.size,
            transcendentals=0,
        ),
        name="gather_papers",
    )(got, *in_hbm(paper))


def prep_kernel(feats, w_self_in, cot_in, w_in, pre, cot, w_rel, w_self, sems):
    copies = fetch([(w_self_in, w_self), (cot_in, cot), (w_in, w_rel)], sems)
    copies[0].wait()
    pre[...] = dot(feats[...], w_self[...])
    for c in copies[1:]:
        c.wait()


def prep(feats, w_self, cotangent, w_rel):
    return pl.pallas_call(
        prep_kernel,
        out_shape=(
            pltpu.VMEM(cotangent.shape, F32),
            pltpu.VMEM(cotangent.shape, F32),
            pltpu.VMEM(w_rel.shape, BF16),
        ),
        in_specs=[VMEM, HBM, HBM, HBM],
        out_specs=(VMEM, VMEM, VMEM),
        scratch_shapes=[pltpu.VMEM(w_self.shape, BF16), pltpu.SemaphoreType.DMA((3,))],
        compiler_params=params(),
        cost_estimate=pl.CostEstimate(
            flops=2 * feats.size * w_self.shape[1], bytes_accessed=4 << 20, transcendentals=0
        ),
        name="prep",
    )(feats, *in_hbm(w_self, cotangent, w_rel))


def turn_kernel(feats, far, out):
    seeds = feats.shape[0]
    out[:, :seeds] = feats[...].T
    out[:, seeds:] = far[...].T


def turn(feats, far):
    seeds, width = feats.shape
    return pl.pallas_call(
        turn_kernel,
        out_shape=pltpu.HBM((width, 2 * seeds), BF16),
        in_specs=[VMEM, VMEM],
        out_specs=VMEM,
        compiler_params=params(),
        cost_estimate=pl.CostEstimate(flops=0, bytes_accessed=8 * feats.size, transcendentals=0),
        name="turn",
    )(feats, far)


def layer_kernel(
    core,
    fetched,
    seed_of,
    cnt,
    pre_self,
    cot,
    w_rel,
    *rest,
):
    here_out, there_out, grad_out = rest[-3:]
    devs = LANES
    lines = seed_of.shape[0]
    seed1 = iota((devs, LANES), 0) + 1
    agg = jnp.zeros((devs, LANES), F32)
    for b in range(0, lines, 2):
        match = jnp.concatenate(
            [onehot(seed1 == seed_of[b : b + 1, :]), onehot(seed1 == seed_of[b + 1 : b + 2, :])],
            axis=1,
        )
        agg = agg + dot(match, fetched[b * LANES : (b + 2) * LANES, :])
    count = cnt[...]
    agg_b = (agg / count).astype(BF16)
    pre = pre_self[...] + dot(agg_b, w_rel[...])
    sig = jax.nn.sigmoid(pre)
    dpre = (cot[...] * sig * (1.0 + pre * (1.0 - sig))).astype(BF16)
    half = dpre.shape[1] // 2
    first = core[0] == 0
    here_out[:, :half] = jnp.where(first, dpre[:, :half], dpre[:, half:])
    there_out[:, :half] = jnp.where(first, dpre[:, half:], dpre[:, :half])
    here_out[:, half:] = agg_b
    there_out[:, half:] = agg_b
    dagg = dot(dpre, w_rel[...], ((1,), (1,)))
    grad_out[...] = (dagg / count).astype(BF16)


def layer(core, fetched, seed_of, cnt, pre_self, cotangent, w_rel, *ready):
    seeds, hidden = cotangent.shape
    return pl.pallas_call(
        layer_kernel,
        out_shape=(
            jax.ShapeDtypeStruct((seeds, hidden // 2 + LANES), BF16),
            jax.ShapeDtypeStruct((seeds, hidden // 2 + LANES), BF16),
            jax.ShapeDtypeStruct((seeds, LANES), BF16),
        ),
        in_specs=[SMEM] + [VMEM] * 6 + [ANY] * len(ready),
        out_specs=(VMEM, VMEM, VMEM),
        compiler_params=params(),
        name="layer",
    )(core, fetched, seed_of, cnt, pre_self, cotangent, w_rel, *in_hbm(*ready))


def slots_kernel(seed_of, grad, papers_in, feats_in, out, papers, feats, sems):
    copies = fetch([(papers_in, papers), (feats_in, feats)], sems)
    seeds_t = seed_of[...].T
    lane1 = iota((LANES, LANES), 1) + 1
    for b in range(seed_of.shape[0]):
        match = onehot(seeds_t[:, b : b + 1] == lane1)
        out[b * GROUP : (b + 1) * GROUP] = (
            dot(match, grad[...]).astype(BF16).reshape(GROUP, CAP, LANES)
        )
    for c in copies:
        c.wait()


def slot_grads(seed_of, grad, papers, feats_t):
    return pl.pallas_call(
        slots_kernel,
        out_shape=(
            pltpu.VMEM((LANES, CAP, LANES), BF16),
            pltpu.VMEM(papers.shape, BF16),
            pltpu.VMEM(feats_t.shape, BF16),
        ),
        in_specs=[VMEM, VMEM, HBM, HBM],
        out_specs=(VMEM, VMEM, VMEM),
        scratch_shapes=[pltpu.SemaphoreType.DMA((2,))],
        compiler_params=params(),
        cost_estimate=pl.CostEstimate(
            flops=2 * LANES * CAP * LANES * LANES, bytes_accessed=4 << 20, transcendentals=0
        ),
        name="slot_grads",
    )(seed_of, grad, *in_hbm(papers, feats_t))


def weight_kernel(feats_t, here, far, slots, papers, bundle):
    both = jnp.concatenate([here[...], far[...]], axis=0)
    emb = LANES
    right, aggs = both[:, :-emb], both[:, -emb:]
    columns = right.shape[1] // LANES
    blocks = LANES // columns
    span = 2 * REL_ROWS
    where = iota((span * blocks, emb), 0)
    spread_rows = onehot(
        (where // span * REL_ROWS + where % span == iota((span * blocks, emb), 1))
        & (where % span < REL_ROWS)
    )
    aggs_t = dot(spread_rows, aggs, ((1,), (1,))).astype(BF16)
    for cb in range(columns):
        mine = slice(cb % 2 * LANES, (cb % 2 + 1) * LANES)
        if cb % 2 == 0:
            cols = right[:, cb * LANES : (cb + 2) * LANES]
            both_f = dot(feats_t[...], cols).astype(BF16)
            both_a = dot(aggs_t, cols)
        part_f, part_a = both_f[:, mine], both_a[:, mine]
        for i in range(blocks):
            d = cb * blocks + i
            bundle[d, :CAP, :] = slots[d]
            bundle[d, CAP:REL_AT, :] = part_f[i * SELF_ROWS : (i + 1) * SELF_ROWS]
            paper = papers[d].astype(F32)
            rel = part_a[i * span : (i + 1) * span] + paper[:span]
            bundle[d, REL_AT : REL_AT + span, :] = rel.astype(BF16)
            bundle[d, REL_AT + span :, :] = paper[span:].astype(BF16)


def weight_part(feats_t, here, far, slots, papers):
    return pl.pallas_call(
        weight_kernel,
        out_shape=jax.ShapeDtypeStruct((LANES, BUNDLE, LANES), BF16),
        in_specs=[VMEM] * 5,
        out_specs=VMEM,
        compiler_params=params(),
        name="weight_part",
    )(feats_t, here, far, slots, papers)


def sum_kernel(bundle, out, out_scr, sems):
    span = 2 * REL_ROWS
    half = [jnp.zeros((SELF_ROWS + span, LANES), F32) for _ in range(2)]
    for d in range(LANES):
        c = (d // GROUP) % 2
        half[c] = half[c] + bundle[d, CAP : REL_AT + span, :].astype(F32)
    rel = [h[SELF_ROWS : SELF_ROWS + REL_ROWS] for h in half]
    mine = jnp.concatenate([half[0][:SELF_ROWS], half[1][:SELF_ROWS], rel[0], rel[1]], axis=0)
    mine = mine.astype(BF16)
    for i in range(out_scr.shape[0]):
        out_scr[i] = mine
    copy = fetch([(out_scr, out)], sems)[0]
    copy.wait()


def sum_parts(bundle, peers):
    rows = 2 * (SELF_ROWS + REL_ROWS)
    return pl.pallas_call(
        sum_kernel,
        out_shape=pltpu.HBM((peers, rows, LANES), BF16),
        in_specs=[VMEM],
        out_specs=HBM,
        scratch_shapes=[
            pltpu.VMEM((peers, rows, LANES), BF16),
            pltpu.SemaphoreType.DMA((1,)),
        ],
        compiler_params=params(),
        name="sum_parts",
    )(bundle)


def spread_kernel(side, got, *rest):
    grad_self, grad_rel, self_scr, rel_scr, sems = rest[-5:]
    columns, steps = got.shape[:2]
    copies = []
    rows_self = GROUP * SELF_ROWS
    rows_rel = GROUP * REL_ROWS
    for i in range(steps):
        for cb in range(columns):
            rel = [[], []]
            for mp in range(GROUP):
                block = got[cb, i, mp].astype(F32)
                for h in range(2):
                    cols = slice((h * columns + cb) * LANES, (h * columns + cb + 1) * LANES)
                    self_scr[i, mp * SELF_ROWS : (mp + 1) * SELF_ROWS, cols] = block[
                        h * SELF_ROWS : (h + 1) * SELF_ROWS
                    ]
                    at = 2 * SELF_ROWS + h * REL_ROWS
                    rel[h].append(block[at : at + REL_ROWS])
            for h in range(2):
                cols = slice((h * columns + cb) * LANES, (h * columns + cb + 1) * LANES)
                rel_scr[i, :, cols] = jnp.concatenate(rel[h], axis=0)
        block_at = 2 * i + side[0]
        copies += fetch(
            [
                (self_scr.at[i], grad_self.at[pl.ds(block_at * rows_self, rows_self), :]),
                (rel_scr.at[i], grad_rel.at[pl.ds(block_at * rows_rel, rows_rel), :]),
            ],
            sems.at[i],
        )
    for c in copies:
        c.wait()


def spread(side, got, feats, emb, hidden, others=()):
    columns = hidden // LANES // 2
    peers, rows, _ = got.shape
    steps = peers // columns // GROUP
    return pl.pallas_call(
        spread_kernel,
        out_shape=(
            pltpu.HBM((feats, hidden), F32),
            pltpu.HBM((emb, hidden), F32),
        ),
        in_specs=[SMEM, VMEM] + [HBM] * len(others),
        out_specs=(HBM, HBM),
        scratch_shapes=[
            pltpu.VMEM((steps, GROUP * SELF_ROWS, hidden), F32),
            pltpu.VMEM((steps, GROUP * REL_ROWS, hidden), F32),
            pltpu.SemaphoreType.DMA((steps, 2)),
        ],
        input_output_aliases={2 + i: i for i in range(len(others))},
        compiler_params=params(),
        cost_estimate=pl.CostEstimate(
            flops=feats * hidden, bytes_accessed=3 * feats * hidden, transcendentals=0
        ),
        name="weight_out",
    )(side, got.reshape(columns, steps, GROUP, rows, LANES), *others)


def after_kernel(*refs):
    pass


def after(a, *ready):
    return pl.pallas_call(
        after_kernel,
        out_shape=jax.ShapeDtypeStruct(a.shape, a.dtype),
        in_specs=[ANY] * (1 + len(ready)),
        out_specs=ANY,
        input_output_aliases={0: 0},
        compiler_params=params(),
        name="after",
    )(a, *in_hbm(*ready))


def adam_kernel(
    wanted, bundle, table, m1, m2, new_table, new_m1, new_m2, done, arrived, hot_scr, side_scr, sem
):
    step = pl.program_id(0)
    lines = wanted.shape[0]
    done[...] = jnp.zeros_like(done)

    @pl.when(step == 0)
    def _():
        copy = pltpu.make_async_copy(bundle.at[:, pl.ds(0, CAP), :], arrived, sem.at[0])
        copy.start()
        lo = wanted[...] % 256
        hi = (wanted[...] // 256).astype(F32).T
        sub = iota((256, LANES), 0)
        for b in range(lines):
            at = slice(b * LANES, (b + 1) * LANES)
            hot_scr[:, at] = onehot(sub == lo[b : b + 1, :])
            side_scr[at, :] = jnp.broadcast_to(hi[:, b : b + 1], (LANES, LANES)).astype(BF16)
        copy.wait()

    here = side_scr[...] == step.astype(F32).astype(BF16)
    mark = jnp.where(here, BF16(1.0), BF16(0.0))
    got = arrived[...].reshape(LANES * CAP, LANES)
    both = dot(hot_scr[...], jnp.concatenate([got * mark, mark], axis=1))
    grad = both[:, :LANES]
    touched = both[:, LANES:] > 0.0
    m = 0.9 * m1[...] + 0.1 * grad
    v = 0.999 * m2[...] + 0.001 * grad * grad
    update = 0.05 * (m / (1.0 - 0.9**10)) / (jnp.sqrt(v / (1.0 - 0.999**10)) + 1e-08)
    new_table[...] = jnp.where(touched, table[...] - update, table[...])
    new_m1[...] = jnp.where(touched, m, m1[...])
    new_m2[...] = jnp.where(touched, v, m2[...])


def adam(wanted, bundle, table, m1, m2):
    rows = 256
    block = pl.BlockSpec((rows, LANES), lambda i: (i, 0))
    slots = LANES * CAP
    return pl.pallas_call(
        adam_kernel,
        grid=(table.shape[0] // rows,),
        out_shape=(jax.ShapeDtypeStruct(table.shape, F32),) * 3
        + (jax.ShapeDtypeStruct((8, LANES), F32),),
        in_specs=[pl.BlockSpec(wanted.shape, lambda i: (0, 0)), ANY, block, block, block],
        out_specs=(block, block, block, pl.BlockSpec((8, LANES), lambda i: (0, 0))),
        scratch_shapes=[
            pltpu.VMEM((LANES, CAP, LANES), BF16),
            pltpu.VMEM((rows, slots), BF16),
            pltpu.VMEM((slots, LANES), BF16),
            pltpu.SemaphoreType.DMA((1,)),
        ],
        cost_estimate=pl.CostEstimate(
            flops=2 * 2 * slots * LANES * table.shape[0],
            bytes_accessed=7 << 20,
            transcendentals=0,
        ),
        name="adam",
    )(wanted, bundle, table, m1, m2)


def shards(
    feats,
    edge_owner,
    edge_row,
    counts,
    table,
    moment1,
    moment2,
    w_self,
    w_rel,
    cotangent,
    next_owner,
    next_row,
    paper_table,
):
    every = ("chip", "core", "mp")
    peers = ("chip", "mp")
    devs = lax.axis_size(every)
    seeds, width = feats.shape
    hidden = cotangent.shape[1]
    emb = table.shape[1]
    core = lax.axis_index("core").astype(I32).reshape(1)
    group = lax.axis_index("mp").astype(I32).reshape(1)

    def exchange(a, axes):
        return lax.all_to_all(a, axes, split_axis=0, concat_axis=0, tiled=True)

    def swap(a):
        return lax.ppermute(a, "core", [(0, 1), (1, 0)])

    asked, seed_of, cnt, paper_pick, wide = place(
        group,
        edge_owner.reshape(-1, LANES),
        edge_row.reshape(-1, LANES),
        counts.reshape(1, -1),
        next_owner.reshape(1, -1),
        next_row.reshape(1, -1),
        table,
    )
    got = exchange(asked.reshape(devs, 1, LANES), every).reshape(devs, LANES)
    rows, wanted = gather(got, wide)
    fetched = exchange(rows.reshape(devs, CAP, emb), every).reshape(devs * CAP, emb)

    pre_self, cot, w_rel = prep(feats, w_self, cotangent, w_rel)
    feats_t = turn(feats, swap(feats))
    papers = paper_rows(got, paper_table)
    here, there, grad = layer(
        core, fetched, seed_of, cnt, pre_self, cot, w_rel, feats_t, papers
    )

    far = swap(there)
    slots, papers, feats_t = slot_grads(seed_of, grad, papers, feats_t)
    bundle = weight_part(feats_t, here, far, slots, papers)
    bundle = exchange(bundle, every)
    full = exchange(sum_parts(bundle, lax.axis_size(peers)), peers)
    new_table, new_moment1, new_moment2, done = adam(wanted, bundle, table, moment1, moment2)
    papers = bundle[:, PAPER_AT : PAPER_AT + FCAP * width // LANES, :].reshape(devs, -1)
    next_feats = functools.reduce(
        lambda a, b: a + b,
        [
            lax.dot_general(
                paper_pick[t],
                papers[:, t * width : (t + 1) * width],
                (((0,), (0,)), ((), ())),
                preferred_element_type=F32,
            )
            for t in range(FCAP)
        ],
    ).astype(BF16)
    full = after(full, done, next_feats)
    part = spread(core, full, width, emb, hidden)
    grad_self, grad_rel = spread(1 - core, swap(full), width, emb, hidden, part)
    return (new_table, new_moment1, new_moment2, grad_self, grad_rel, next_feats)


def solution(mesh):
    n_mp = mesh.shape["mp"]
    wide = Mesh(mesh.devices.reshape(-1, 2, n_mp), ("chip", "core", "mp"))
    rows = P(("chip", "core", "mp"), None)
    line = P(("chip", "core", "mp"))
    in_specs = (rows, rows, line, line, rows, rows, rows, P(), P(), rows, rows, line, rows)
    out_specs = (rows, rows, rows, P(), P(), rows)
    return jax.shard_map(shards, mesh=wide, in_specs=in_specs, out_specs=out_specs, check_vma=False)
```

```python
import functools

import jax
import jax.numpy as jnp
from jax import lax
from jax.experimental import pallas as pl
from jax.experimental.pallas import tpu as pltpu
from jax.sharding import Mesh, PartitionSpec as P

F32 = jnp.float32
BF16 = jnp.bfloat16
I32 = jnp.int32
LANES = 128
CAP = 32
FCAP = 2
GROUP = LANES // CAP
EMPTY = 4095
SELF_ROWS = 24
REL_ROWS = 4
REL_AT = CAP + SELF_ROWS
PAPER_AT = REL_AT + REL_ROWS
PAPER_ROWS = 12
TILE = 256
BUNDLE = PAPER_AT + PAPER_ROWS
VMEM = pl.BlockSpec(memory_space=pltpu.VMEM)
SMEM = pl.BlockSpec(memory_space=pltpu.SMEM)


def iota(shape, dim):
    return lax.broadcasted_iota(I32, shape, dim)


def dot(a, b, contract=((1,), (0,))):
    return lax.dot_general(a, b, (contract, ((), ())), preferred_element_type=F32)


def onehot(mask):
    return jnp.where(mask, F32(1.0), F32(0.0)).astype(BF16)

ANY = pl.BlockSpec(memory_space=pl.ANY)
HBM = pl.BlockSpec(memory_space=pltpu.HBM)


def params():
    return pltpu.CompilerParams(vmem_limit_bytes=24 * 1024 * 1024)


def in_hbm(*arrays):
    return [pltpu.with_memory_space_constraint(a, pltpu.HBM) for a in arrays]


def fetch(pairs, sems):
    copies = [pltpu.make_async_copy(a, b, sems.at[i]) for i, (a, b) in enumerate(pairs)]
    for c in copies:
        c.start()
    return copies


def place_kernel(
    lane_group,
    owner_in,
    row_in,
    counts_in,
    next_owner_in,
    next_row_in,
    table_in,
    asked,
    seed_of,
    cnt,
    paper_pick,
    wide,
    owner,
    row,
    counts,
    next_owner,
    next_row,
    table,
    seed_scr,
    sems,
):
    copies = fetch(
        [
            (owner_in, owner),
            (row_in, row),
            (counts_in, counts),
            (next_owner_in, next_owner),
            (next_row_in, next_row),
            (table_in, table),
        ],
        sems,
    )
    table_copy = copies.pop()
    devs = LANES
    blocks = owner.shape[0]
    group = lane_group[0]
    sub = iota((devs, LANES), 0)
    lane = iota((devs, LANES), 1)
    seeds_row = LANES // (LANES * blocks // devs)
    slots_per = LANES // seeds_row
    upper = onehot(sub < lane)
    ones = jnp.ones((devs, LANES), BF16)
    scan = jnp.concatenate([upper, ones], axis=1)
    pick = onehot(sub % seeds_row == lane // slots_per)
    for c in copies:
        c.wait()
    count_row = counts[...].astype(F32)
    spread = jnp.where(
        iota((blocks, LANES), 1) // seeds_row == iota((blocks, LANES), 0), count_row, F32(0.0)
    ).astype(BF16)
    cnt_edge = dot(spread, pick)
    k_edge = (iota((blocks, LANES), 1) % slots_per).astype(F32)
    live_owner = jnp.where(k_edge < cnt_edge, owner[...], -1)
    base = jnp.zeros((devs, LANES), F32)
    hots, values = [], []
    ksub = iota((CAP, LANES), 0).astype(F32)
    for b in range(blocks):
        hot = sub == live_owner[b : b + 1, :]
        hot_f = jnp.where(hot, F32(1.0), F32(0.0))
        hot_b = hot_f.astype(BF16)
        scanned = dot(hot_b, scan)
        slot = jnp.sum(hot_f * (scanned[:, :LANES] + base), axis=0, keepdims=True)
        base = base + scanned[:, LANES:]
        at = ksub == slot
        r = row[b : b + 1, :]
        seed1 = b * seeds_row + iota((1, LANES), 1) // slots_per + 1
        vals = jnp.concatenate(
            [
                jnp.where(at, (r // LANES).astype(F32), F32(0.0)),
                jnp.where(at, (r % LANES).astype(F32), F32(0.0)),
                jnp.where(at, seed1.astype(F32), F32(0.0)),
            ],
            axis=0,
        ).astype(BF16)
        hots.append(hot_b)
        values.append(vals)
    values = jnp.concatenate(values, axis=1)
    acc_i = dot(jnp.concatenate(hots, axis=1), values, ((1,), (1,))).astype(I32)
    seeds = acc_i[:, 2 * CAP :]
    wanted = jnp.where(seeds > 0, acc_i[:, :CAP] * LANES + acc_i[:, CAP : 2 * CAP], EMPTY)

    hot = sub == next_owner[...]
    hot_f = jnp.where(hot, F32(1.0), F32(0.0))
    hot_b = hot_f.astype(BF16)
    before = dot(hot_b, upper)
    slot = jnp.sum(hot_f * before, axis=0, keepdims=True)
    nrow = next_row[...]
    for t in range(FCAP):
        paper_pick[t] = jnp.where(slot == t, hot_f, F32(0.0)).astype(BF16)
    at = iota((CAP, LANES), 0) == slot.astype(I32)
    vals = jnp.concatenate(
        [
            jnp.where(at, (nrow // LANES).astype(F32), F32(0.0)),
            jnp.where(at, (nrow % LANES).astype(F32), F32(0.0)),
        ],
        axis=0,
    ).astype(BF16)
    pacc = dot(hot_b, vals, ((1,), (1,))).astype(I32)
    paper = pacc[:, :CAP] * LANES + pacc[:, CAP:]

    quarter = lane // CAP
    wide_wanted = jnp.concatenate([wanted] * GROUP, axis=1)
    wide_paper = jnp.concatenate([paper] * GROUP, axis=1)
    asked[...] = jnp.where(
        quarter == group,
        wide_wanted,
        jnp.where(quarter == (group + 1) % GROUP, wide_paper, 0),
    )
    seed_scr[...] = jnp.where(quarter == sub % GROUP, jnp.concatenate([seeds] * GROUP, axis=1), 0)
    total = seed_scr[pl.ds(0, devs // GROUP, stride=GROUP), :]
    for i in range(1, GROUP):
        total = total + seed_scr[pl.ds(i, devs // GROUP, stride=GROUP), :]
    seed_of[...] = total
    cnt[...] = jnp.broadcast_to(count_row, (devs, LANES)).T
    table_copy.wait()
    for q in range(table.shape[0] // TILE):
        wide[:, q * LANES : (q + 1) * LANES] = table[q * TILE : (q + 1) * TILE, :].astype(BF16)


def place(group, owner, row, counts, next_owner, next_row, table):
    devs = LANES
    ins = (owner, row, counts, next_owner, next_row, table)
    return pl.pallas_call(
        place_kernel,
        out_shape=(
            pltpu.VMEM((devs, LANES), I32),
            jax.ShapeDtypeStruct((devs // GROUP, LANES), I32),
            jax.ShapeDtypeStruct((devs, LANES), F32),
            jax.ShapeDtypeStruct((FCAP, devs, LANES), BF16),
            pltpu.VMEM((TILE, table.shape[0] // TILE * LANES), BF16),
        ),
        in_specs=[SMEM] + [HBM] * len(ins),
        out_specs=(VMEM, VMEM, VMEM, VMEM, VMEM),
        scratch_shapes=[pltpu.VMEM(a.shape, a.dtype) for a in ins]
        + [pltpu.VMEM((devs, LANES), I32), pltpu.SemaphoreType.DMA((len(ins),))],
        compiler_params=params(),
        name="place",
    )(group, *in_hbm(*ins))


def gather_kernel(got, wide, rows, wanted_out, hot_scr, hi_scr, out_scr, out_sems):
    devs = LANES
    lines = devs // GROUP
    quarter = iota((lines, LANES), 1) // CAP
    wanted = jnp.zeros((lines, LANES), I32)
    for i in range(GROUP):
        wanted = wanted + jnp.where(quarter == i, got[pl.ds(i, lines, stride=GROUP), :], 0)
    wanted_out[...] = wanted
    wanted_t = wanted.T
    lo = wanted_t % TILE
    hi = wanted_t // TILE
    lanes = iota((LANES, TILE), 1)
    for b in range(lines):
        hot_scr[b * LANES : (b + 1) * LANES, :] = onehot(lo[:, b : b + 1] == lanes)
        hi_scr[b * LANES : (b + 1) * LANES, :] = jnp.broadcast_to(hi[:, b : b + 1], (LANES, LANES))
    quarter_rows = out_scr.shape[0] // 4
    chunks = [quarter_rows] * 3 + [quarter_rows // 2] + [quarter_rows // 4] * 2
    outs = []
    for c, chunk in enumerate(chunks):
        at = pl.ds(sum(chunks[:c]), chunk)
        hot = hot_scr[at, :]
        high = hi_scr[at, :]
        out = jnp.zeros((chunk, LANES), F32)
        for q in range(0, wide.shape[1] // LANES, 2):
            both = dot(hot, wide[:, q * LANES : (q + 2) * LANES])
            out = jnp.where(high == q, both[:, :LANES], out)
            out = jnp.where(high == q + 1, both[:, LANES:], out)
        out_scr[at, :] = out.astype(BF16)
        copy = pltpu.make_async_copy(out_scr.at[at, :], rows.at[at, :], out_sems.at[c])
        copy.start()
        outs.append(copy)
    for copy in outs:
        copy.wait()


def gather(got, wide):
    slots = LANES * CAP
    return pl.pallas_call(
        gather_kernel,
        out_shape=(
            pltpu.HBM((slots, LANES), BF16),
            pltpu.HBM((LANES // GROUP, LANES), I32),
        ),
        in_specs=[VMEM, VMEM],
        out_specs=(HBM, VMEM),
        scratch_shapes=[
            pltpu.VMEM((slots, TILE), BF16),
            pltpu.VMEM((slots, LANES), I32),
            pltpu.VMEM((slots, LANES), BF16),
            pltpu.SemaphoreType.DMA((slots // 512,)),
        ],
        compiler_params=params(),
        name="gather_rows",
    )(got, wide)


def paper_kernel(got, paper_in, rows, paper, scr, sem):
    copies = fetch([(paper_in, paper)], sem)
    devs = LANES
    sub = iota((devs, LANES), 0)
    lane = iota((devs, LANES), 1)
    first = ((sub % GROUP + 1) % GROUP) * CAP
    parts = paper.shape[1] // LANES
    span = REL_ROWS + PAPER_ROWS
    for i in range(REL_ROWS):
        scr[pl.ds(i, devs, stride=span), :] = jnp.zeros((devs, LANES), F32)
    copies[0].wait()
    for t in range(FCAP):
        asked = jnp.sum(jnp.where(lane == first + t, got[...], 0), axis=1, keepdims=True)
        hot = onehot(asked == iota((devs, paper.shape[0]), 1))
        found = dot(hot, paper[...])
        for i in range(parts):
            scr[pl.ds(REL_ROWS + t * parts + i, devs, stride=span), :] = found[
                :, i * LANES : (i + 1) * LANES
            ]
    rows[...] = scr[...].astype(BF16).reshape(rows.shape)


def paper_rows(got, paper):
    span = REL_ROWS + PAPER_ROWS
    return pl.pallas_call(
        paper_kernel,
        out_shape=pltpu.HBM((LANES, span, LANES), BF16),
        in_specs=[VMEM, HBM],
        out_specs=VMEM,
        scratch_shapes=[
            pltpu.VMEM(paper.shape, BF16),
            pltpu.VMEM((LANES * span, LANES), F32),
            pltpu.SemaphoreType.DMA((1,)),
        ],
        compiler_params=params(),
        cost_estimate=pl.CostEstimate(
            flops=2 * FCAP * LANES * paper.shape[0] * paper.shape[1],
            bytes_accessed=4 * paper.size,
            transcendentals=0,
        ),
        name="gather_papers",
    )(got, *in_hbm(paper))


def prep_kernel(feats, w_self_in, cot_in, w_in, pre, cot, w_rel, w_self, sems):
    copies = fetch([(w_self_in, w_self), (cot_in, cot), (w_in, w_rel)], sems)
    copies[0].wait()
    pre[...] = dot(feats[...], w_self[...])
    for c in copies[1:]:
        c.wait()


def prep(feats, w_self, cotangent, w_rel):
    return pl.pallas_call(
        prep_kernel,
        out_shape=(
            pltpu.VMEM(cotangent.shape, F32),
            pltpu.VMEM(cotangent.shape, F32),
            pltpu.VMEM(w_rel.shape, BF16),
        ),
        in_specs=[VMEM, HBM, HBM, HBM],
        out_specs=(VMEM, VMEM, VMEM),
        scratch_shapes=[pltpu.VMEM(w_self.shape, BF16), pltpu.SemaphoreType.DMA((3,))],
        compiler_params=params(),
        cost_estimate=pl.CostEstimate(
            flops=2 * feats.size * w_self.shape[1], bytes_accessed=4 << 20, transcendentals=0
        ),
        name="prep",
    )(feats, *in_hbm(w_self, cotangent, w_rel))


def turn_kernel(feats, far, out):
    seeds = feats.shape[0]
    out[:, :seeds] = feats[...].T
    out[:, seeds:] = far[...].T


def turn(feats, far):
    seeds, width = feats.shape
    return pl.pallas_call(
        turn_kernel,
        out_shape=pltpu.HBM((width, 2 * seeds), BF16),
        in_specs=[VMEM, VMEM],
        out_specs=VMEM,
        compiler_params=params(),
        cost_estimate=pl.CostEstimate(flops=0, bytes_accessed=8 * feats.size, transcendentals=0),
        name="turn",
    )(feats, far)


def layer_kernel(
    core,
    fetched,
    seed_of,
    cnt,
    pre_self,
    cot,
    w_rel,
    *rest,
):
    here_out, there_out, grad_out = rest[-3:]
    devs = LANES
    lines = seed_of.shape[0]
    seed1 = iota((devs, LANES), 0) + 1
    agg = jnp.zeros((devs, LANES), F32)
    for b in range(0, lines, 2):
        match = jnp.concatenate(
            [onehot(seed1 == seed_of[b : b + 1, :]), onehot(seed1 == seed_of[b + 1 : b + 2, :])],
            axis=1,
        )
        agg = agg + dot(match, fetched[b * LANES : (b + 2) * LANES, :])
    count = cnt[...]
    agg_b = (agg / count).astype(BF16)
    pre = pre_self[...] + dot(agg_b, w_rel[...])
    sig = jax.nn.sigmoid(pre)
    dpre = (cot[...] * sig * (1.0 + pre * (1.0 - sig))).astype(BF16)
    half = dpre.shape[1] // 2
    first = core[0] == 0
    here_out[:, :half] = jnp.where(first, dpre[:, :half], dpre[:, half:])
    there_out[:, :half] = jnp.where(first, dpre[:, half:], dpre[:, :half])
    here_out[:, half:] = agg_b
    there_out[:, half:] = agg_b
    dagg = dot(dpre, w_rel[...], ((1,), (1,)))
    grad_out[...] = (dagg / count).astype(BF16)


def layer(core, fetched, seed_of, cnt, pre_self, cotangent, w_rel, *ready):
    seeds, hidden = cotangent.shape
    return pl.pallas_call(
        layer_kernel,
        out_shape=(
            jax.ShapeDtypeStruct((seeds, hidden // 2 + LANES), BF16),
            jax.ShapeDtypeStruct((seeds, hidden // 2 + LANES), BF16),
            jax.ShapeDtypeStruct((seeds, LANES), BF16),
        ),
        in_specs=[SMEM] + [VMEM] * 6 + [ANY] * len(ready),
        out_specs=(VMEM, VMEM, VMEM),
        compiler_params=params(),
        name="layer",
    )(core, fetched, seed_of, cnt, pre_self, cotangent, w_rel, *in_hbm(*ready))


def slots_kernel(seed_of, grad, papers_in, feats_in, out, papers, feats, sems):
    copies = fetch([(papers_in, papers), (feats_in, feats)], sems)
    seeds_t = seed_of[...].T
    lane1 = iota((LANES, LANES), 1) + 1
    for b in range(seed_of.shape[0]):
        match = onehot(seeds_t[:, b : b + 1] == lane1)
        out[b * GROUP : (b + 1) * GROUP] = (
            dot(match, grad[...]).astype(BF16).reshape(GROUP, CAP, LANES)
        )
    for c in copies:
        c.wait()


def slot_grads(seed_of, grad, papers, feats_t):
    return pl.pallas_call(
        slots_kernel,
        out_shape=(
            pltpu.VMEM((LANES, CAP, LANES), BF16),
            pltpu.VMEM(papers.shape, BF16),
            pltpu.VMEM(feats_t.shape, BF16),
        ),
        in_specs=[VMEM, VMEM, HBM, HBM],
        out_specs=(VMEM, VMEM, VMEM),
        scratch_shapes=[pltpu.SemaphoreType.DMA((2,))],
        compiler_params=params(),
        cost_estimate=pl.CostEstimate(
            flops=2 * LANES * CAP * LANES * LANES, bytes_accessed=4 << 20, transcendentals=0
        ),
        name="slot_grads",
    )(seed_of, grad, *in_hbm(papers, feats_t))


def weight_kernel(feats_t, here, far, slots, papers, bundle):
    both = jnp.concatenate([here[...], far[...]], axis=0)
    emb = LANES
    right, aggs = both[:, :-emb], both[:, -emb:]
    columns = right.shape[1] // LANES
    blocks = LANES // columns
    span = 2 * REL_ROWS
    where = iota((span * blocks, emb), 0)
    spread_rows = onehot(
        (where // span * REL_ROWS + where % span == iota((span * blocks, emb), 1))
        & (where % span < REL_ROWS)
    )
    aggs_t = dot(spread_rows, aggs, ((1,), (1,))).astype(BF16)
    for cb in range(columns):
        mine = slice(cb % 2 * LANES, (cb % 2 + 1) * LANES)
        if cb % 2 == 0:
            cols = right[:, cb * LANES : (cb + 2) * LANES]
            both_f = dot(feats_t[...], cols).astype(BF16)
            both_a = dot(aggs_t, cols)
        part_f, part_a = both_f[:, mine], both_a[:, mine]
        for i in range(blocks):
            d = cb * blocks + i
            bundle[d, :CAP, :] = slots[d]
            bundle[d, CAP:REL_AT, :] = part_f[i * SELF_ROWS : (i + 1) * SELF_ROWS]
            paper = papers[d].astype(F32)
            rel = part_a[i * span : (i + 1) * span] + paper[:span]
            bundle[d, REL_AT : REL_AT + span, :] = rel.astype(BF16)
            bundle[d, REL_AT + span :, :] = paper[span:].astype(BF16)


def weight_part(feats_t, here, far, slots, papers):
    return pl.pallas_call(
        weight_kernel,
        out_shape=jax.ShapeDtypeStruct((LANES, BUNDLE, LANES), BF16),
        in_specs=[VMEM] * 5,
        out_specs=VMEM,
        compiler_params=params(),
        name="weight_part",
    )(feats_t, here, far, slots, papers)


def sum_kernel(bundle, out, out_scr, sems):
    span = 2 * REL_ROWS
    half = [jnp.zeros((SELF_ROWS + span, LANES), F32) for _ in range(2)]
    for d in range(LANES):
        c = (d // GROUP) % 2
        half[c] = half[c] + bundle[d, CAP : REL_AT + span, :].astype(F32)
    rel = [h[SELF_ROWS : SELF_ROWS + REL_ROWS] for h in half]
    mine = jnp.concatenate([half[0][:SELF_ROWS], half[1][:SELF_ROWS], rel[0], rel[1]], axis=0)
    mine = mine.astype(BF16)
    for i in range(out_scr.shape[0]):
        out_scr[i] = mine
    copy = fetch([(out_scr, out)], sems)[0]
    copy.wait()


def sum_parts(bundle, peers):
    rows = 2 * (SELF_ROWS + REL_ROWS)
    return pl.pallas_call(
        sum_kernel,
        out_shape=pltpu.HBM((peers, rows, LANES), BF16),
        in_specs=[VMEM],
        out_specs=HBM,
        scratch_shapes=[
            pltpu.VMEM((peers, rows, LANES), BF16),
            pltpu.SemaphoreType.DMA((1,)),
        ],
        compiler_params=params(),
        name="sum_parts",
    )(bundle)


def spread_kernel(side, got, *rest):
    grad_self, grad_rel, self_scr, rel_scr, sems = rest[-5:]
    columns, steps = got.shape[:2]
    copies = []
    rows_self = GROUP * SELF_ROWS
    rows_rel = GROUP * REL_ROWS
    for i in range(steps):
        for cb in range(columns):
            rel = [[], []]
            for mp in range(GROUP):
                block = got[cb, i, mp].astype(F32)
                for h in range(2):
                    cols = slice((h * columns + cb) * LANES, (h * columns + cb + 1) * LANES)
                    self_scr[i, mp * SELF_ROWS : (mp + 1) * SELF_ROWS, cols] = block[
                        h * SELF_ROWS : (h + 1) * SELF_ROWS
                    ]
                    at = 2 * SELF_ROWS + h * REL_ROWS
                    rel[h].append(block[at : at + REL_ROWS])
            for h in range(2):
                cols = slice((h * columns + cb) * LANES, (h * columns + cb + 1) * LANES)
                rel_scr[i, :, cols] = jnp.concatenate(rel[h], axis=0)
        block_at = 2 * i + side[0]
        copies += fetch(
            [
                (self_scr.at[i], grad_self.at[pl.ds(block_at * rows_self, rows_self), :]),
                (rel_scr.at[i], grad_rel.at[pl.ds(block_at * rows_rel, rows_rel), :]),
            ],
            sems.at[i],
        )
    for c in copies:
        c.wait()


def spread(side, got, feats, emb, hidden, others=()):
    columns = hidden // LANES // 2
    peers, rows, _ = got.shape
    steps = peers // columns // GROUP
    return pl.pallas_call(
        spread_kernel,
        out_shape=(
            pltpu.HBM((feats, hidden), F32),
            pltpu.HBM((emb, hidden), F32),
        ),
        in_specs=[SMEM, VMEM] + [HBM] * len(others),
        out_specs=(HBM, HBM),
        scratch_shapes=[
            pltpu.VMEM((steps, GROUP * SELF_ROWS, hidden), F32),
            pltpu.VMEM((steps, GROUP * REL_ROWS, hidden), F32),
            pltpu.SemaphoreType.DMA((steps, 2)),
        ],
        input_output_aliases={2 + i: i for i in range(len(others))},
        compiler_params=params(),
        cost_estimate=pl.CostEstimate(
            flops=feats * hidden, bytes_accessed=3 * feats * hidden, transcendentals=0
        ),
        name="weight_out",
    )(side, got.reshape(columns, steps, GROUP, rows, LANES), *others)


def after_kernel(*refs):
    pass


def after(a, *ready):
    return pl.pallas_call(
        after_kernel,
        out_shape=jax.ShapeDtypeStruct(a.shape, a.dtype),
        in_specs=[ANY] * (1 + len(ready)),
        out_specs=ANY,
        input_output_aliases={0: 0},
        compiler_params=params(),
        name="after",
    )(a, *in_hbm(*ready))


def adam_kernel(
    wanted, bundle, table, m1, m2, new_table, new_m1, new_m2, done, arrived, hot_scr, side_scr, sem
):
    step = pl.program_id(0)
    lines = wanted.shape[0]
    done[...] = jnp.zeros_like(done)

    @pl.when(step == 0)
    def _():
        copy = pltpu.make_async_copy(bundle.at[:, pl.ds(0, CAP), :], arrived, sem.at[0])
        copy.start()
        lo = wanted[...] % 256
        hi = (wanted[...] // 256).astype(F32).T
        sub = iota((256, LANES), 0)
        for b in range(lines):
            at = slice(b * LANES, (b + 1) * LANES)
            hot_scr[:, at] = onehot(sub == lo[b : b + 1, :])
            side_scr[at, :] = jnp.broadcast_to(hi[:, b : b + 1], (LANES, LANES)).astype(BF16)
        copy.wait()

    got = arrived[...].reshape(LANES * CAP, LANES)
    parts = table.shape[0] // 256
    for part in range(parts):
        at = slice(part * 256, (part + 1) * 256)
        here = side_scr[...] == (step * parts + part).astype(F32).astype(BF16)
        mark = jnp.where(here, BF16(1.0), BF16(0.0))
        both = dot(hot_scr[...], jnp.concatenate([got * mark, mark], axis=1))
        grad = both[:, :LANES]
        touched = both[:, LANES:] > 0.0
        m = 0.9 * m1[at, :] + 0.1 * grad
        v = 0.999 * m2[at, :] + 0.001 * grad * grad
        update = 0.05 * (m / (1.0 - 0.9**10)) / (jnp.sqrt(v / (1.0 - 0.999**10)) + 1e-08)
        new_table[at, :] = jnp.where(touched, table[at, :] - update, table[at, :])
        new_m1[at, :] = jnp.where(touched, m, m1[at, :])
        new_m2[at, :] = jnp.where(touched, v, m2[at, :])


def adam(wanted, bundle, table, m1, m2):
    rows = 512
    block = pl.BlockSpec((rows, LANES), lambda i: (i, 0))
    slots = LANES * CAP
    return pl.pallas_call(
        adam_kernel,
        grid=(table.shape[0] // rows,),
        out_shape=(jax.ShapeDtypeStruct(table.shape, F32),) * 3
        + (jax.ShapeDtypeStruct((8, LANES), F32),),
        in_specs=[pl.BlockSpec(wanted.shape, lambda i: (0, 0)), ANY, block, block, block],
        out_specs=(block, block, block, pl.BlockSpec((8, LANES), lambda i: (0, 0))),
        scratch_shapes=[
            pltpu.VMEM((LANES, CAP, LANES), BF16),
            pltpu.VMEM((256, slots), BF16),
            pltpu.VMEM((slots, LANES), BF16),
            pltpu.SemaphoreType.DMA((1,)),
        ],
        cost_estimate=pl.CostEstimate(
            flops=2 * 2 * slots * LANES * table.shape[0],
            bytes_accessed=7 << 20,
            transcendentals=0,
        ),
        name="adam",
    )(wanted, bundle, table, m1, m2)


def shards(
    feats,
    edge_owner,
    edge_row,
    counts,
    table,
    moment1,
    moment2,
    w_self,
    w_rel,
    cotangent,
    next_owner,
    next_row,
    paper_table,
):
    every = ("chip", "core", "mp")
    peers = ("chip", "mp")
    devs = lax.axis_size(every)
    seeds, width = feats.shape
    hidden = cotangent.shape[1]
    emb = table.shape[1]
    core = lax.axis_index("core").astype(I32).reshape(1)
    group = lax.axis_index("mp").astype(I32).reshape(1)

    def exchange(a, axes):
        return lax.all_to_all(a, axes, split_axis=0, concat_axis=0, tiled=True)

    def swap(a):
        return lax.ppermute(a, "core", [(0, 1), (1, 0)])

    asked, seed_of, cnt, paper_pick, wide = place(
        group,
        edge_owner.reshape(-1, LANES),
        edge_row.reshape(-1, LANES),
        counts.reshape(1, -1),
        next_owner.reshape(1, -1),
        next_row.reshape(1, -1),
        table,
    )
    got = exchange(asked.reshape(devs, 1, LANES), every).reshape(devs, LANES)
    rows, wanted = gather(got, wide)
    fetched = exchange(rows.reshape(devs, CAP, emb), every).reshape(devs * CAP, emb)

    pre_self, cot, w_rel = prep(feats, w_self, cotangent, w_rel)
    feats_t = turn(feats, swap(feats))
    papers = paper_rows(got, paper_table)
    here, there, grad = layer(
        core, fetched, seed_of, cnt, pre_self, cot, w_rel, feats_t, papers
    )

    far = swap(there)
    slots, papers, feats_t = slot_grads(seed_of, grad, papers, feats_t)
    bundle = weight_part(feats_t, here, far, slots, papers)
    bundle = exchange(bundle, every)
    full = exchange(sum_parts(bundle, lax.axis_size(peers)), peers)
    new_table, new_moment1, new_moment2, done = adam(wanted, bundle, table, moment1, moment2)
    papers = bundle[:, PAPER_AT : PAPER_AT + FCAP * width // LANES, :].reshape(devs, -1)
    next_feats = functools.reduce(
        lambda a, b: a + b,
        [
            lax.dot_general(
                paper_pick[t],
                papers[:, t * width : (t + 1) * width],
                (((0,), (0,)), ((), ())),
                preferred_element_type=F32,
            )
            for t in range(FCAP)
        ],
    ).astype(BF16)
    full = after(full, done, next_feats)
    part = spread(core, full, width, emb, hidden)
    grad_self, grad_rel = spread(1 - core, swap(full), width, emb, hidden, part)
    return (new_table, new_moment1, new_moment2, grad_self, grad_rel, next_feats)


def solution(mesh):
    n_mp = mesh.shape["mp"]
    wide = Mesh(mesh.devices.reshape(-1, 2, n_mp), ("chip", "core", "mp"))
    rows = P(("chip", "core", "mp"), None)
    line = P(("chip", "core", "mp"))
    in_specs = (rows, rows, line, line, rows, rows, rows, P(), P(), rows, rows, line, rows)
    out_specs = (rows, rows, rows, P(), P(), rows)
    return jax.shard_map(shards, mesh=wide, in_specs=in_specs, out_specs=out_specs, check_vma=False)
```
